32 devices in a mesh: fsdp: 8 (over z, x), tp: 4 (over y, core).
Axes of the slice: x: 2, y: 2, z: 4, core: 2. Of those that a mesh axis runs over, the one named last changes fastest.
Arguments:
- dec_query: bfloat16 [8, 2, 4096], P('fsdp'), may hold values from -200 to 200
- new_keys: bfloat16 [8, 2, 512], P('fsdp'), may hold values from -6 to 6
- new_values: bfloat16 [8, 2, 512], P('fsdp'), may hold values from -6 to 6
- cache_keys: bfloat16 [8, 2048, 512], P('fsdp', 'tp'), may hold values from -6 to 6
- cache_values: bfloat16 [8, 2048, 512], P('fsdp', 'tp'), may hold values from -6 to 6
- lengths: int32 [8], P('fsdp'), may hold values from 256 to 2048, as said below
- out_weight: bfloat16 [4096, 4096], P('fsdp', 'tp'), may hold values from -0.09375 to 0.09375
- train_attn: bfloat16 [1024, 4096], P('fsdp', 'tp'), may hold values from -0.5 to 0.5
- grad_out: bfloat16 [1024, 4096], P('fsdp'), may hold values from -6 to 6
Outputs:
- dec_out: bfloat16 [8, 2, 4096], P('fsdp', None, 'tp')
- grad_attn: bfloat16 [1024, 4096], P('fsdp', 'tp')
- grad_weight: float32 [4096, 4096], P('fsdp', 'tp')
The draws below stay inside these ranges and needn't reach their ends.
Inputs may be any that keep to these rules, and one draw needn't show every extreme that they name: `lengths`: the length 2048 occurs.
All inputs are finite; a program needn't handle non-finite values.
Results may differ from the reference program's by a relative error of at most 0.0049.
Values may be sent and summed in bfloat16 or wider, within the bound.
No kernel may reach another device: no remote copies, remote signals or barrier semaphores. Data moves between devices by JAX's collectives and lax.ppermute only.
A program may use at most 64 MiB of HBM per device.

```python
import jax
import jax.numpy as jnp
from jax import lax

DOUT = 4096
QH = 32
KVH = 4
HD = 128
CACHE = 2048
STEPS = 2
GROUP = 8
QW = 4096
KVW = 512
DEC_ROWS = 8
TOKENS = 1024


def decode_pair(key):
    key_draw = jax.random.truncated_normal(jax.random.fold_in(key, 101), -6.0, 6.0, (DEC_ROWS, STEPS, KVH, HD), jnp.float32)
    jitter = jax.random.truncated_normal(jax.random.fold_in(key, 102), -6.0, 6.0, (DEC_ROWS, STEPS, KVH, GROUP, HD), jnp.float32)
    queries = 2.5 * jitter + 0.7 * key_draw[:, :, :, None, :]
    return (key_draw.reshape(DEC_ROWS, STEPS, KVH * HD), queries.reshape(DEC_ROWS, STEPS, QH * HD))


def draw_dec_query(key, part):
    return decode_pair(key)[1].astype(jnp.bfloat16)


def draw_new_keys(key, part):
    return decode_pair(key)[0].astype(jnp.bfloat16)


def draw_lengths(key, part):
    lengths_drawn = jax.random.randint(jax.random.fold_in(key, 201), (DEC_ROWS,), CACHE // 8, CACHE + 1, dtype=jnp.int32)
    shuffled = jax.random.permutation(jax.random.fold_in(key, 202), DEC_ROWS)
    lengths_drawn = lengths_drawn.at[shuffled[0]].set(CACHE)
    lengths_drawn = lengths_drawn.at[shuffled[1]].set(CACHE // 8)
    return lengths_drawn


def spiked(result, stream_key, source, target, shards_of, factor):
    def block_of(position):
        return (jnp.arange(result.shape[position]) // (result.shape[position] // shards_of)).reshape((-1,) + (1,) * (result.ndim - 1 - position))

    one_side = jax.random.permutation(stream_key, shards_of)[block_of(target)]
    far = (block_of(target) + shards_of // 2) % shards_of
    return jnp.where((block_of(source) == one_side) | (block_of(source) == far), factor * result, result)


def steps_of(stream_key, shape, pieces, smallest, top_value):
    def one(position, blocks):
        heights = jax.random.uniform(jax.random.fold_in(jax.random.fold_in(stream_key, 6), position), (blocks,), jnp.float32, smallest / len(pieces), top_value / len(pieces))
        return jnp.repeat(jnp.exp(heights), shape[position] // blocks).reshape((-1,) + (1,) * (len(shape) - position - 1))

    loudness = one(*pieces[0])
    for cut in pieces[1:]:
        loudness = loudness * one(*cut)
    return loudness


def noise(key, shape, deviation, reach, shards=(), kind=jnp.bfloat16):
    result = jax.random.normal(key, shape, jnp.float32) * deviation
    if len(shards) > 0:
        result = steps_of(key, shape, shards, -0.22, 0.18) * result
    return jnp.clip(result, min=-reach, max=reach).astype(kind)


def gaussian_with(key, extent, scale, most, cuts, heavy, kind=jnp.bfloat16):
    values = scale * jax.random.normal(key, extent, jnp.float32)
    if cuts:
        values = values * steps_of(key, extent, cuts, -0.22, 0.18)
    return jnp.clip(spiked(values, jax.random.fold_in(key, 3), *heavy), -most, most).astype(kind)


def setup_inputs(seed: int = 0) -> dict:
    keys = jax.random.split(jax.random.key(seed), 10)
    dec_query = draw_dec_query(jax.random.fold_in(keys[9], 71), 0)
    new_keys = draw_new_keys(jax.random.fold_in(keys[9], 71), 0)
    new_values = noise(keys[2], (DEC_ROWS, STEPS, KVW), 1.0, 6.0, ((0, 8),))
    cache_keys = noise(keys[3], (DEC_ROWS, CACHE, KVW), 1.0, 6.0, ((0, 8), (1, 4)))
    cache_values = noise(keys[4], (DEC_ROWS, CACHE, KVW), 1.0, 6.0, ((0, 8), (1, 4)))
    lengths = draw_lengths(jax.random.fold_in(keys[9], 71), 0)
    out_weight = noise(keys[6], (DOUT, QW), QW ** -0.5, 0.09375, ((0, 8), (1, 4)))
    train_attn = noise(keys[7], (TOKENS, QW), (TOKENS ** -0.5), 0.5, ((0, 8), (1, 4)))
    grad_out = gaussian_with(keys[8], (TOKENS, DOUT), 1.0, 6.0, ((0, 8),), (0, 1, 8, 2.0))
    return {"dec_query": dec_query, "new_keys": new_keys, "new_values": new_values, "cache_keys": cache_keys, "cache_values": cache_values, "lengths": lengths, "out_weight": out_weight, "train_attn": train_attn, "grad_out": grad_out}


def reference(dec_query, new_keys, new_values, cache_keys, cache_values, lengths, out_weight, train_attn, grad_out):
    scaling = 1.0 / (HD ** 0.5)
    step_allowed = jnp.arange(STEPS, dtype=jnp.int32)[None, :] <= jnp.arange(STEPS, dtype=jnp.int32)[:, None]

    def one_row(record):
        queries, key_new, value_new, key_cache, value_cache, length = record
        q_float = queries.astype(jnp.float32).reshape(STEPS, KVH, GROUP, HD)
        all_keys = jnp.concatenate([key_cache, key_new], axis=0).astype(jnp.float32).reshape(CACHE + STEPS, KVH, HD)
        all_values = jnp.concatenate([value_cache, value_new], axis=0).astype(jnp.float32).reshape(CACHE + STEPS, KVH, HD)
        cache_allowed = jnp.arange(CACHE, dtype=jnp.int32) < length
        allowed = jnp.concatenate([jnp.broadcast_to(cache_allowed[None, :], (STEPS, CACHE)), step_allowed], axis=1)
        scores = jnp.einsum("sgqd,pgd->sgqp", q_float, all_keys, precision=lax.Precision.HIGHEST) * scaling
        usable = allowed[:, None, None, :]
        maxima = jnp.max(jnp.where(usable, scores, -jnp.inf), axis=-1, keepdims=True)
        exp_terms = jnp.where(usable, jnp.exp(scores - maxima), jnp.float32(0.0))
        weighted = jnp.einsum("sgqp,pgd->sgqd", exp_terms, all_values, precision=lax.Precision.HIGHEST)
        attended = weighted / jnp.sum(exp_terms, axis=-1)[..., None]
        return attended.reshape(STEPS, QW).astype(jnp.bfloat16)

    dec_attn = lax.map(one_row, (dec_query, new_keys, new_values, cache_keys, cache_values, lengths))
    dec_out = jnp.dot(dec_attn.reshape(DEC_ROWS * STEPS, QW), out_weight.T, preferred_element_type=jnp.float32)
    dec_out = dec_out.reshape(DEC_ROWS, STEPS, DOUT).astype(jnp.bfloat16)
    grad_attn = jnp.dot(grad_out, out_weight, preferred_element_type=jnp.float32).astype(jnp.bfloat16)
    grad_weight = jnp.dot(grad_out.T, train_attn, preferred_element_type=jnp.float32)
    return dec_out, grad_attn, grad_weight
```

```python
import jax
import jax.numpy as jnp
from jax import lax
from jax.sharding import PartitionSpec as P

KVH = 4
HD = 128
NEG_FILL = -1e30
BF16 = jnp.bfloat16
F32 = jnp.float32


def flip(a, axis, bits):
    size = lax.axis_size(axis)
    return lax.ppermute(a, axis, [(i, i ^ bits) for i in range(size)])


def local_attention(query, keys, values, usable):
    steps, width = query.shape
    heads = width // HD
    group = heads // KVH
    rows = query.reshape(steps, heads, HD).transpose(1, 0, 2).reshape(heads * steps, HD)
    own = jnp.arange(heads * steps)[:, None] // (group * steps) == jnp.arange(KVH * HD)[None, :] // HD
    spread = jnp.where(own, jnp.tile(rows, (1, KVH)), jnp.zeros((), query.dtype))
    scores = lax.dot_general(spread, keys, (((1,), (1,)), ((), ())), preferred_element_type=F32)
    scores = scores * (1.0 / HD**0.5)
    maxima = jnp.max(jnp.where(usable, scores, NEG_FILL), axis=-1, keepdims=True)
    terms = jnp.where(usable, jnp.exp(scores - maxima), 0.0)
    totals = jnp.sum(terms, axis=-1, keepdims=True)
    upper = lax.reduce_precision(terms, 8, 7)
    both = jnp.concatenate([upper.astype(BF16), (terms - upper).astype(BF16)], axis=0)
    wide = jnp.dot(both, values, preferred_element_type=F32)
    wide = wide[: heads * steps] + wide[heads * steps :]
    wide = jnp.where(own, wide, 0.0)
    weighted = sum(wide[:, g * HD : (g + 1) * HD] for g in range(KVH))
    return weighted, maxima, totals


def decode(dec_query, new_keys, new_values, cache_keys, cache_values, lengths, out_weight):
    rows, steps, width = dec_query.shape
    tp_size = lax.axis_size("tp")
    tp_index = lax.axis_index("tp")
    fsdp_size = lax.axis_size("fsdp")
    fsdp_index = lax.axis_index("fsdp")
    cache_len = cache_keys.shape[1]
    heads = width // HD
    heads_dev = heads // tp_size
    group = heads // KVH
    positions = tp_index * cache_len + jnp.arange(cache_len, dtype=jnp.int32)
    packed = []
    for r in range(rows):
        usable = (positions < lengths[r])[None, :]
        weighted, maxima, totals = local_attention(dec_query[r], cache_keys[r], cache_values[r], usable)
        packed.append(
            jnp.concatenate(
                [weighted, jnp.broadcast_to(maxima, (heads * steps, HD // 2)), jnp.broadcast_to(totals, (heads * steps, HD // 2))],
                axis=1,
            ).reshape(tp_size, heads_dev, steps, 2 * HD)
        )
    packed = jnp.stack(packed, axis=1)
    parts = [lax.dynamic_index_in_dim(packed, tp_index, 0, False)]
    for k in range(1, tp_size):
        parts.append(flip(lax.dynamic_index_in_dim(packed, tp_index ^ k, 0, False), "tp", k))

    own_query = lax.dynamic_slice_in_dim(dec_query.reshape(rows, steps, heads, HD), tp_index * heads_dev, heads_dev, 2)
    key_own = lax.dynamic_slice_in_dim(
        jnp.repeat(new_keys.reshape(rows, steps, KVH, HD), group, axis=2), tp_index * heads_dev, heads_dev, 2
    )
    value_own = lax.dynamic_slice_in_dim(
        jnp.repeat(new_values.reshape(rows, steps, KVH, HD), group, axis=2), tp_index * heads_dev, heads_dev, 2
    ).astype(F32)
    new_scores = jnp.sum(own_query.astype(F32)[:, :, None] * key_own.astype(F32)[:, None], axis=-1) * (1.0 / HD**0.5)
    new_scores = new_scores.transpose(0, 3, 1, 2)
    allowed = jnp.arange(steps)[None, :] <= jnp.arange(steps)[:, None]
    highest = jnp.max(jnp.where(allowed, new_scores, NEG_FILL), axis=-1)
    for part in parts:
        highest = jnp.maximum(highest, part[..., HD])
    new_terms = jnp.where(allowed, jnp.exp(new_scores - highest[..., None]), 0.0)
    total = jnp.sum(new_terms, axis=-1)
    weighted = sum(new_terms[..., j, None] * value_own[:, j, :, None, :] for j in range(steps))
    for part in parts:
        scale = jnp.exp(part[..., HD] - highest)
        total = total + part[..., HD + HD // 2] * scale
        weighted = weighted + part[..., :HD] * scale[..., None]
    attended = (weighted / total[..., None]).astype(BF16)
    attended = attended.transpose(0, 2, 1, 3).reshape(rows * steps, heads_dev * HD)

    every = attended[None]
    reach = 1
    while reach < fsdp_size:
        other = flip(every, "fsdp", reach)
        low = (fsdp_index // reach) % 2 == 0
        every = jnp.where(low, jnp.concatenate([every, other]), jnp.concatenate([other, every]))
        reach *= 2
    every = every.reshape(fsdp_size * rows * steps, heads_dev * HD)
    partial = lax.dot_general(every, out_weight, (((1,), (1,)), ((), ())), preferred_element_type=F32)
    feats = partial.shape[1]
    share = fsdp_size // tp_size
    partial = partial.reshape(tp_size, share, rows * steps, feats)
    mine = lax.dynamic_index_in_dim(partial, tp_index, 0, False)
    for k in range(1, tp_size):
        mine = mine + flip(lax.dynamic_index_in_dim(partial, tp_index ^ k, 0, False), "tp", k)
    mine = mine.astype(BF16)
    out = jnp.zeros((share, rows * steps, feats), BF16)
    for j in range(share):
        perm = [
            (f * tp_size + q, (q * share + (f % share ^ j)) * tp_size + f // share)
            for f in range(fsdp_size)
            for q in range(tp_size)
        ]
        piece = lax.dynamic_index_in_dim(mine, fsdp_index % share ^ j, 0, False)
        got = lax.ppermute(piece, ("fsdp", "tp"), perm)
        out = lax.dynamic_update_index_in_dim(out, got, fsdp_index % share ^ j, 0)
    return out.transpose(1, 0, 2).reshape(rows, steps, share * feats)


def gradients(out_weight, train_attn, grad_out):
    inner = 2
    fsdp_size = lax.axis_size("fsdp")
    outer = fsdp_size // inner
    fsdp_index = lax.axis_index("fsdp")
    z, x = fsdp_index // inner, fsdp_index % inner
    core = lax.axis_index("tp") % 2
    tokens, dout = grad_out.shape
    feats = out_weight.shape[0]
    plane = feats * inner
    half = tokens // 2
    other_weight = flip(out_weight, "fsdp", 1)
    got = [
        flip(lax.dynamic_slice(grad_out, (core * half, (z ^ k) * plane), (half, plane)), "fsdp", k * inner)
        for k in range(1, outer)
    ]
    attn = [train_attn] + [flip(train_attn, "fsdp", k * inner) for k in range(1, outer)]
    got = jnp.stack(got)
    twin = flip(got, "tp", 1)
    cot = jnp.where(core == 0, jnp.concatenate([got, twin], axis=1), jnp.concatenate([twin, got], axis=1))
    own_cot = lax.dynamic_slice(grad_out, (0, z * plane), (tokens, plane))
    cots = jnp.concatenate([own_cot[None], cot]).reshape(outer * tokens, plane)
    cot_x = lax.dynamic_slice(cots, (0, x * feats), (outer * tokens, feats))
    cot_o = lax.dynamic_slice(cots, (0, (1 - x) * feats), (outer * tokens, feats))
    dot = lambda a, b: jnp.dot(a, b, preferred_element_type=F32)
    partial = (dot(cot_x, out_weight) + dot(cot_o, other_weight)).reshape(outer, tokens, -1)
    grad_attn = partial[0]
    sent = partial[1:].astype(BF16)
    for k in range(1, outer):
        grad_attn = grad_attn + flip(sent[k - 1], "fsdp", k * inner).astype(F32)
    attn = jnp.concatenate(attn)
    span = outer * half
    piece = flip(lax.dynamic_slice(cot_o, (core * span, 0), (span, feats)), "fsdp", 1)
    piece_twin = flip(piece, "tp", 1)
    cot_far = jnp.where(core == 0, jnp.concatenate([piece, piece_twin]), jnp.concatenate([piece_twin, piece]))
    attn_far = flip(attn, "fsdp", 1)
    over_tokens = lambda a, b: lax.dot_general(a, b, (((0,), (0,)), ((), ())), preferred_element_type=F32)
    grad_weight = over_tokens(cot_x, attn) + over_tokens(cot_far, attn_far)
    return grad_attn.astype(BF16), grad_weight


def shards(dec_query, new_keys, new_values, cache_keys, cache_values, lengths, out_weight, train_attn, grad_out):
    grad_attn, grad_weight = gradients(out_weight, train_attn, grad_out)
    dec_out = decode(dec_query, new_keys, new_values, cache_keys, cache_values, lengths, out_weight)
    return dec_out, grad_attn, grad_weight


def solution(mesh):
    return jax.shard_map(
        shards,
        mesh=mesh,
        in_specs=(
            P("fsdp", None, None),
            P("fsdp", None, None),
            P("fsdp", None, None),
            P("fsdp", "tp", None),
            P("fsdp", "tp", None),
            P("fsdp"),
            P("fsdp", "tp"),
            P("fsdp", "tp"),
            P("fsdp", None),
        ),
        out_specs=(P("fsdp", None, "tp"), P("fsdp", "tp"), P("fsdp", "tp")),
        check_vma=False,
    )
```

```python
import functools

import jax
import jax.numpy as jnp
from jax import lax
from jax.experimental import pallas as pl
from jax.experimental.pallas import tpu as pltpu
from jax.sharding import PartitionSpec as P

KVH = 4
HD = 128
NEG_FILL = -1e30
INNER = 2
PAD = 16
BF16 = jnp.bfloat16
F32 = jnp.float32


def flip(a, axis, bits, name):
    size = lax.axis_size(axis)
    with jax.named_scope(name):
        return lax.ppermute(a, axis, [(i, i ^ bits) for i in range(size)])


def dot(a, b):
    return jnp.dot(a, b, preferred_element_type=F32)


def over_features(a, b):
    return lax.dot_general(a, b, (((1,), (1,)), ((), ())), preferred_element_type=F32)


def over_tokens(a, b):
    return lax.dot_general(a, b, (((0,), (0,)), ((), ())), preferred_element_type=F32)


class Mover:
    def __init__(self, sems):
        self.sems, self.count, self.open = sems, 0, []

    def start(self, source, target):
        copy = pltpu.make_async_copy(source, target, self.sems.at[self.count])
        self.count += 1
        self.open.append(copy)
        copy.start()
        return copy

    def wait(self, *copies):
        for copy in copies:
            copy.wait()
            self.open = [other for other in self.open if other is not copy]

    def finish(self):
        self.wait(*list(self.open))


def places():
    fsdp_index, tp_index = lax.axis_index("fsdp"), lax.axis_index("tp")
    return tp_index, tp_index % 2, fsdp_index // INNER, fsdp_index % INNER, tp_index * KVH // lax.axis_size("tp")


def call(kernel, name, operands, out_shapes, scratch, waits=(), scalars=None, room=12):
    copies = 4 * (len(operands) + len(out_shapes))
    scalars = [] if scalars is None else [scalars]

    def body(*refs):
        front, refs = refs[: len(scalars)], refs[len(scalars) :]
        ins, refs = refs[: len(operands)], refs[len(operands) + len(waits) :]
        outs, refs = refs[: len(out_shapes)], refs[len(out_shapes) :]
        mover = Mover(refs[-1])
        kernel(mover, *front, ins, outs, refs[:-1])
        mover.finish()

    results = pl.pallas_call(
        body,
        out_shape=[jax.ShapeDtypeStruct(shape, dtype) for shape, dtype in out_shapes],
        in_specs=[pl.BlockSpec(memory_space=pltpu.SMEM)] * len(scalars)
        + [pl.BlockSpec(memory_space=pltpu.HBM)] * (len(operands) + len(waits)),
        out_specs=[pl.BlockSpec(memory_space=pltpu.HBM)] * len(out_shapes),
        scratch_shapes=[pltpu.VMEM(shape, dtype) for shape, dtype in scratch] + [pltpu.SemaphoreType.DMA((copies,))],
        compiler_params=pltpu.CompilerParams(vmem_limit_bytes=room << 20),
        cost_estimate=pl.CostEstimate(flops=0, bytes_accessed=0, transcendentals=0),
        name=name,
    )(*scalars, *operands, *waits)
    return list(results)


def shaped(*arrays):
    return [(a.shape, a.dtype) for a in arrays]


def attend_kernel(steps, mover, lengths_ref, ins, outs, scratch):
    query_hbm, keys_hbm, values_hbm, new_keys_hbm, new_values_hbm = ins
    query_ref, keys_ref, values_ref, new_keys_ref, new_values_ref, query_rows, out_rows, own_rows, own_ref = scratch
    tp_index, _, _, _, own_group = places()
    length = lengths_ref[0]
    own_out, *part_outs = outs
    tp_size = sum(out.shape[0] for out in part_outs)
    first = mover.start(query_hbm.at[0], query_ref)
    news = [mover.start(new_keys_hbm.at[0], new_keys_ref), mover.start(new_values_hbm.at[0], new_values_ref)]
    groups = [slice(g * HD, (g + 1) * HD) for g in range(KVH)]
    arrive = [
        (mover.start(keys_hbm.at[0, :, group], keys_ref.at[:, group]), mover.start(values_hbm.at[0, :, group], values_ref.at[:, group]))
        for group in groups
    ]
    width = query_ref.shape[1]
    cache_len = keys_ref.shape[0]
    rows = width // HD // KVH * steps
    mover.wait(first)
    for h in range(width // HD):
        query_rows[h * steps : (h + 1) * steps, :] = query_ref[:, h * HD : (h + 1) * HD].astype(F32)
    usable = lax.broadcasted_iota(jnp.int32, (rows, cache_len), 1) + tp_index * cache_len < length
    left = lax.broadcasted_iota(jnp.int32, (rows, HD), 1) < HD // 2
    for g in range(KVH):
        mover.wait(*arrive[g])
        query = query_rows[g * rows : (g + 1) * rows, :].astype(BF16)
        scores = over_features(query, keys_ref[:, g * HD : (g + 1) * HD]) * (1.0 / HD**0.5)
        maxima = jnp.max(jnp.where(usable, scores, NEG_FILL), axis=1, keepdims=True)
        terms = jnp.where(usable, jnp.exp(scores - maxima), 0.0)
        totals = jnp.sum(terms, axis=1, keepdims=True)
        upper = terms.astype(BF16)
        lower = (terms - upper.astype(F32)).astype(BF16)
        both = dot(jnp.concatenate([upper, lower], axis=0), values_ref[:, g * HD : (g + 1) * HD])
        out_rows[g * rows : (g + 1) * rows, :HD] = both[:rows] + both[rows:]
        out_rows[g * rows : (g + 1) * rows, HD:] = jnp.where(left, maxima, totals)
    count = own_rows.shape[1]
    for t in range(KVH * rows // count):
        for k in range(tp_size):

            @pl.when(tp_index ^ k == t)
            def _():
                own_rows[k] = out_rows[t * count : (t + 1) * count, :]

        @pl.when(tp_index == t)
        def _():
            own_ref[:count, :HD] = query_rows[t * count : (t + 1) * count, :]

    first = 0
    for part_out in part_outs:
        mover.start(own_rows.at[first : first + part_out.shape[0]], part_out)
        first += part_out.shape[0]
    mover.wait(*news)
    own_ref[:count, HD:] = jnp.zeros((count, HD), F32)
    for at, ref in ((0, new_keys_ref), (HD, new_values_ref)):
        chosen = ref[:, :HD].astype(F32)
        for g in range(1, KVH):
            chosen = jnp.where(own_group == g, ref[:, groups[g]].astype(F32), chosen)
        own_ref[count : count + steps, at : at + HD] = chosen
    mover.start(own_ref, own_out)


def combine_kernel(steps, own_ref, attn_ref, *refs):
    *part_refs, out_ref, rows_ref = refs
    tokens = attn_ref.shape[0]
    count = part_refs[0].shape[1]
    out_ref[:tokens, :] = attn_ref[...]
    rows_ref[...] = jnp.zeros_like(rows_ref)
    step = lax.broadcasted_iota(jnp.int32, (count, 1), 0) % steps
    query = own_ref[:count, :HD]
    keys, values = own_ref[count:, :HD], own_ref[count:, HD:]
    parts = [part_ref[part_ref.shape[0] - 1] for part_ref in part_refs]
    scores = []
    for j in range(steps):
        score = jnp.sum(query * keys[j : j + 1], axis=-1, keepdims=True) * (1.0 / HD**0.5)
        scores.append(jnp.where(step >= j, score, NEG_FILL))
    maxima = [part[:, HD : HD + 1] for part in parts]
    highest = functools.reduce(jnp.maximum, scores + maxima)
    total = jnp.zeros((count, 1), F32)
    weighted = jnp.zeros((count, HD), F32)
    for part, own in zip(parts, maxima):
        scale = jnp.exp(own - highest)
        total = total + part[:, HD + HD // 2 : HD + HD // 2 + 1] * scale
        weighted = weighted + part[:, :HD] * scale
    for j in range(steps):
        term = jnp.where(step >= j, jnp.exp(scores[j] - highest), 0.0)
        total = total + term
        weighted = weighted + term * values[j : j + 1]
    attended = weighted / total
    for row in range(count):
        h, s = row // steps, row % steps
        rows_ref[s : s + 1, h * HD : (h + 1) * HD] = attended[row : row + 1]
    out_ref[tokens:, :] = rows_ref[...].astype(BF16)


def middle_kernel(outer, mover, ins, outs, scratch):
    grad_hbm, weight_hbm, other_hbm, *cot_hbms = ins
    sent_outs, (total_out, cot_own_out, cot_far_out) = outs[: outer - 1], outs[outer - 1 :]
    cots_ref, weight_ref, other_ref, sent_ref, total_ref, cot_own_ref, cot_far_ref = scratch
    _, core, z, x, _ = places()
    tokens = grad_hbm.shape[0]
    plane = cots_ref.shape[1]
    feats = weight_ref.shape[0]
    half = tokens // 2
    weights = [mover.start(weight_hbm, weight_ref), mover.start(other_hbm, other_ref)]
    blocks = [[mover.start(grad_hbm.at[:, pl.ds(pl.multiple_of(z * plane, plane), plane)], cots_ref.at[:tokens])]]
    for k in range(1, outer):
        blocks.append([])
        for hbms, side in ((cot_hbms[:2], core), (cot_hbms[2:], 1 - core)):
            base = pl.multiple_of(k * tokens + side * half, half)
            for i, hbm in enumerate(hbms):
                size = hbm.shape[0]
                low, high = max((k - 1) * half, i * size), min(k * half, (i + 1) * size)
                if low < high:
                    source = hbm.at[low - i * size : high - i * size]
                    first = pl.multiple_of(base + (low - (k - 1) * half), half // 2)
                    blocks[k].append(mover.start(source, cots_ref.at[pl.ds(first, high - low)]))
    mover.wait(*weights)
    span = outer * half
    for k in reversed(range(outer)):
        mover.wait(*blocks[k])
        here = slice(k * tokens, (k + 1) * tokens)
        block = cots_ref[here, :]
        low, high = block[:, :feats], block[:, feats:]
        own = jnp.where(x == 0, low, high)
        other = jnp.where(x == 0, high, low)
        total = dot(own, weight_ref[...]) + dot(other, other_ref[...])
        if k == 0:
            total_ref[...] = total
            mover.start(total_ref, total_out)
        else:
            sent_ref[k - 1] = total.astype(BF16)
            mover.start(sent_ref.at[k - 1], sent_outs[k - 1])
        cot_own_ref[here, :] = own
        for side in range(2):
            if span * side <= k * tokens < span * (side + 1):

                @pl.when(core == side)
                def _():
                    cot_far_ref[k * tokens - span * side : (k + 1) * tokens - span * side, :] = other

    mover.start(cot_far_ref, cot_far_out)
    mover.start(cot_own_ref, cot_own_out)


def decode_kernel(steps, mover, ins, outs, scratch):
    weight_hbm, other_hbm, *load_hbms = ins
    pack_out, *part_outs = outs
    weight_ref, other_ref, loads_ref, rows_ref, by_row_ref, parts_ref = scratch
    q, _, z, x, _ = places()
    outer = len(load_hbms)
    tokens = load_hbms[0].shape[0] - PAD
    loads = [mover.start(hbm, loads_ref.at[k]) for k, hbm in enumerate(load_hbms)]
    weights = [mover.start(weight_hbm, weight_ref), mover.start(other_hbm, other_ref)]
    mover.wait(*loads)
    for k in range(outer):
        mover.start(loads_ref.at[k, :tokens], pack_out.at[k * tokens : (k + 1) * tokens])
    mover.wait(*weights)
    for k in range(outer):
        rows_ref[k * steps : (k + 1) * steps, :] = loads_ref[k, tokens:, :].astype(F32)[:steps]
    every = rows_ref[...].astype(BF16)
    own, other = over_features(every, weight_ref[...]), over_features(every, other_ref[...])
    wide = jnp.concatenate([jnp.where(x == 0, own, other), jnp.where(x == 0, other, own)], axis=1)
    for k in range(outer):
        by_row_ref[k] = wide[k * steps : (k + 1) * steps]
    share = parts_ref.shape[1]
    for k, out in enumerate(part_outs):
        for i in range(share):
            parts_ref[k, i] = by_row_ref[((q ^ k) * share + i) ^ z]
        mover.start(parts_ref.at[k], out)


def stack_kernel(mover, ins, outs, scratch):
    half, size = ins[0].shape[0], outs[0].shape[0]
    arrive = [mover.start(hbm, scratch[0].at[k * half : (k + 1) * half]) for k, hbm in enumerate(ins)]
    mover.wait(*arrive)
    for i, out in enumerate(outs):
        mover.start(scratch[0].at[i * size : (i + 1) * size], out)


def release_kernel(mover, ins, outs, scratch):
    arrive = [mover.start(hbm, scratch[0].at[k]) for k, hbm in enumerate(ins)]
    for k, copy in enumerate(arrive):
        mover.wait(copy)
        mover.start(scratch[0].at[k], outs[k])


def sum_kernel(mover, ins, outs, scratch):
    total_hbm, *part_hbms = ins
    total_ref, parts_ref, out_ref = scratch
    arrive = [mover.start(total_hbm, total_ref)]
    arrive += [mover.start(hbm, parts_ref.at[i]) for i, hbm in enumerate(part_hbms)]
    mover.wait(*arrive)
    total = total_ref[...]
    for i in range(len(part_hbms)):
        total = total + parts_ref[i].astype(F32)
    out_ref[...] = total.astype(BF16)
    mover.start(out_ref, outs[0])


def product_kernel(mover, ins, outs, scratch):
    cot_hbm, cot_twin_hbm, attn_hbm, total_hbm = ins
    cots_ref, attn_ref, total_ref, out_ref = scratch
    _, core, _, _, _ = places()
    span = cot_hbm.shape[0]
    arrive = [
        mover.start(cot_hbm, cots_ref.at[pl.ds(pl.multiple_of(core * span, span), span)]),
        mover.start(cot_twin_hbm, cots_ref.at[pl.ds(pl.multiple_of((1 - core) * span, span), span)]),
        mover.start(attn_hbm, attn_ref),
    ]
    pieces = 2
    step = out_ref.shape[0] // pieces
    totals = [mover.start(total_hbm.at[i * step : (i + 1) * step], total_ref.at[i * step : (i + 1) * step]) for i in range(pieces)]
    mover.wait(*arrive)
    for i in range(pieces):
        here = slice(i * step, (i + 1) * step)
        product = over_tokens(cots_ref[:, here], attn_ref[...])
        mover.wait(totals[i])
        out_ref[here, :] = total_ref[here, :] + product
        mover.start(out_ref.at[here], outs[0].at[here])


def shards(dec_query, new_keys, new_values, cache_keys, cache_values, lengths, out_weight, train_attn, grad_out):
    rows, steps, width = dec_query.shape
    assert rows == 1
    fsdp_size = lax.axis_size("fsdp")
    tp_size = lax.axis_size("tp")
    outer = fsdp_size // INNER
    share = outer // tp_size
    fsdp_index = lax.axis_index("fsdp")
    tp_index = lax.axis_index("tp")
    z, x = fsdp_index // INNER, fsdp_index % INNER
    tokens = grad_out.shape[0]
    feats, cols = out_weight.shape
    plane = feats * INNER
    slot = tp_index % 4
    heads = width // HD
    count = heads // tp_size * steps
    far = range(1, outer)
    others = range(1, tp_size)

    other_weight = flip(out_weight, "fsdp", 1, "weight_x")

    half = tokens // 2
    got = [
        flip(lax.dynamic_slice(grad_out, (tp_index % 2 * half, (z ^ k) * plane), (half, plane)), "fsdp", k * INNER, f"cot_z{k}")
        for k in far
    ]

    sizes = [1 << b for b in range(tp_size.bit_length() - 1)]
    own, part, *chunks = call(
        functools.partial(attend_kernel, steps),
        "attend",
        [dec_query, cache_keys, cache_values, new_keys, new_values],
        [((count + 8, 2 * HD), F32), ((1, count, 2 * HD), F32)] + [((size, count, 2 * HD), F32) for size in sizes],
        shaped(dec_query[0], cache_keys[0], cache_values[0], new_keys[0], new_values[0])
        + [((heads * steps, HD), F32), ((heads * steps, 2 * HD), F32), ((tp_size, count, 2 * HD), F32), ((count + 8, 2 * HD), F32)],
        scalars=lengths,
        room=63,
    )
    held = []
    for size, chunk in reversed(list(zip(sizes, chunks))):
        leaving = [chunk] + [a if size == 1 else a[size:] for a in held]
        held = [a if size == 1 else a[:size] for a in held]
        came = [flip(a, "tp", size, f"softmax_tp{size}") for a in leaving]
        held = [a[:1] if size == 1 and a.shape[0] > 1 else a for a in held] + came
    parts = [part, *held]
    load = pl.pallas_call(
        functools.partial(combine_kernel, steps),
        out_shape=jax.ShapeDtypeStruct((tokens + PAD, cols), BF16),
        in_specs=[pl.BlockSpec(memory_space=pltpu.VMEM)] * (len(parts) + 2),
        out_specs=pl.BlockSpec(memory_space=pltpu.VMEM),
        scratch_shapes=[pltpu.VMEM((PAD, cols), F32)],
        cost_estimate=pl.CostEstimate(flops=0, bytes_accessed=0, transcendentals=0),
        name="combine",
    )(own, train_attn, *parts)
    loads = [flip(load, "fsdp", k * INNER, f"attn_z{k}") for k in far]

    stacked = call(
        stack_kernel,
        "stack",
        got,
        [((len(far) * half // 2, plane), BF16)] * 2,
        [((len(far) * half, plane), BF16)],
        waits=[load],
    )
    twins = [flip(a, "tp", 1, "cot_core") for a in stacked]

    *sent, total, cot_own, cot_far = call(
        functools.partial(middle_kernel, outer),
        "middle",
        [grad_out, out_weight, other_weight, *stacked, *twins],
        [((tokens, cols), BF16)] * len(far)
        + [((tokens, cols), F32), ((outer * tokens, feats), BF16), ((outer * half, feats), BF16)],
        [
            ((outer * tokens, plane), BF16),
            ((feats, cols), BF16),
            ((feats, cols), BF16),
            ((len(far), tokens, cols), BF16),
            ((tokens, cols), F32),
            ((outer * tokens, feats), BF16),
            ((outer * half, feats), BF16),
        ],
    )
    cot_x = flip(cot_far, "fsdp", 1, "cot_x")
    pack, *dec = call(
        functools.partial(decode_kernel, steps),
        "decode",
        [out_weight, other_weight, load, *loads],
        [((outer * tokens, cols), BF16)] + [((share, steps, plane), F32)] * tp_size,
        [
            ((feats, cols), BF16),
            ((feats, cols), BF16),
            ((outer, tokens + PAD, cols), BF16),
            ((outer * steps, cols), F32),
            ((outer, steps, plane), F32),
            ((tp_size, share, steps, plane), F32),
        ],
        waits=[cot_x],
    )
    sums = [flip(sent[k - 1], "fsdp", k * INNER, f"sum_z{k}") for k in far]
    pack_x = flip(pack, "fsdp", 1, "attn_x")
    cot_x_twin = flip(cot_x, "tp", 1, "cot_x_core")

    dec = call(
        release_kernel, "release", dec, [((share, steps, plane), F32)] * tp_size, [((tp_size, share, steps, plane), F32)], waits=[cot_x_twin]
    )
    dec = (dec[0] + sum(flip(dec[k], "tp", k, f"dec_tp{k}") for k in others)).astype(BF16)
    pieces = []
    for j in range(share):
        perm = [
            ((a * INNER + b) * tp_size + q, ((q * share + (a % share ^ j)) * INNER + b) * tp_size + a // share)
            for a in range(outer)
            for b in range(INNER)
            for q in range(tp_size)
        ]
        with jax.named_scope("dec_place"):
            pieces.append(lax.ppermute(lax.dynamic_index_in_dim(dec, z % share ^ j, 0, False), ("fsdp", "tp"), perm))
    pieces = jnp.stack(pieces)
    dec_out = jnp.concatenate(
        [lax.dynamic_index_in_dim(pieces, (z % share) ^ s, 0, False) for s in range(share)], axis=1
    ).reshape(rows, steps, share * plane)

    (grad_attn,) = call(
        sum_kernel,
        "sum",
        [total, *sums],
        [((tokens, cols), BF16)],
        [((tokens, cols), F32), ((len(far), tokens, cols), BF16), ((tokens, cols), BF16)],
    )

    own_total = over_tokens(cot_own, pack)
    (grad_weight,) = call(
        product_kernel,
        "product",
        [cot_x, cot_x_twin, pack_x, own_total],
        [((feats, cols), F32)],
        [((outer * tokens, feats), BF16), ((outer * tokens, cols), BF16), ((feats, cols), F32), ((feats, cols), F32)],
        waits=[grad_attn],
    )
    return dec_out, grad_attn, grad_weight


def solution(mesh):
    return jax.shard_map(
        shards,
        mesh=mesh,
        in_specs=(
            P("fsdp", None, None),
            P("fsdp", None, None),
            P("fsdp", None, None),
            P("fsdp", "tp", None),
            P("fsdp", "tp", None),
            P("fsdp"),
            P("fsdp", "tp"),
            P("fsdp", "tp"),
            P("fsdp", None),
        ),
        out_specs=(P("fsdp", None, "tp"), P("fsdp", "tp"), P("fsdp", "tp")),
        check_vma=False,
    )
```

```python
import functools

import jax
import jax.numpy as jnp
from jax import lax
from jax.experimental import pallas as pl
from jax.experimental.pallas import tpu as pltpu
from jax.sharding import PartitionSpec as P

KVH = 4
HD = 128
NEG_FILL = -1e30
INNER = 2
PAD = 16
BF16 = jnp.bfloat16
F32 = jnp.float32


def flip(a, axis, bits, name):
    size = lax.axis_size(axis)
    with jax.named_scope(name):
        return lax.ppermute(a, axis, [(i, i ^ bits) for i in range(size)])


def turn(a, steps, name):
    outer = lax.axis_size("fsdp") // INNER
    with jax.named_scope(name):
        return lax.ppermute(
            a, "fsdp", [(z * INNER + x, (z + steps) % outer * INNER + x) for z in range(outer) for x in range(INNER)]
        )


def dot(a, b):
    return jnp.dot(a, b, preferred_element_type=F32)


def over_features(a, b):
    return lax.dot_general(a, b, (((1,), (1,)), ((), ())), preferred_element_type=F32)


def over_tokens(a, b):
    return lax.dot_general(a, b, (((0,), (0,)), ((), ())), preferred_element_type=F32)


class Mover:
    def __init__(self, sems):
        self.sems, self.count, self.open = sems, 0, []

    def start(self, source, target):
        copy = pltpu.make_async_copy(source, target, self.sems.at[self.count])
        self.count += 1
        self.open.append(copy)
        copy.start()
        return copy

    def wait(self, *copies):
        for copy in copies:
            copy.wait()
            self.open = [other for other in self.open if other is not copy]

    def finish(self):
        self.wait(*list(self.open))


def places():
    fsdp_index, tp_index = lax.axis_index("fsdp"), lax.axis_index("tp")
    return tp_index, tp_index % 2, fsdp_index // INNER, fsdp_index % INNER, tp_index * KVH // lax.axis_size("tp")


def call(kernel, name, operands, out_shapes, scratch, waits=(), scalars=None, room=12, fast=()):
    copies = 4 * (len(operands) + len(out_shapes))
    scalars = [] if scalars is None else [scalars]

    def body(*refs):
        front, refs = refs[: len(scalars)], refs[len(scalars) :]
        ins, refs = refs[: len(operands)], refs[len(operands) + len(waits) :]
        outs, refs = refs[: len(out_shapes)], refs[len(out_shapes) :]
        mover = Mover(refs[-1])
        kernel(mover, *front, ins, outs, refs[:-1])
        mover.finish()

    results = pl.pallas_call(
        body,
        out_shape=[jax.ShapeDtypeStruct(shape, dtype) for shape, dtype in out_shapes],
        in_specs=[pl.BlockSpec(memory_space=pltpu.SMEM)] * len(scalars)
        + [pl.BlockSpec(memory_space=pltpu.HBM)] * (len(operands) + len(waits)),
        out_specs=[
            pl.BlockSpec(memory_space=pltpu.VMEM if i in fast else pltpu.HBM) for i in range(len(out_shapes))
        ],
        scratch_shapes=[pltpu.VMEM(shape, dtype) for shape, dtype in scratch] + [pltpu.SemaphoreType.DMA((copies,))],
        compiler_params=pltpu.CompilerParams(vmem_limit_bytes=room << 20),
        cost_estimate=pl.CostEstimate(flops=0, bytes_accessed=0, transcendentals=0),
        name=name,
    )(*scalars, *operands, *waits)
    return list(results)


def shaped(*arrays):
    return [(a.shape, a.dtype) for a in arrays]


def attend_kernel(steps, mover, lengths_ref, ins, outs, scratch):
    query_hbm, keys_hbm, values_hbm, new_keys_hbm, new_values_hbm, attn_hbm = ins
    query_ref, keys_ref, values_ref, new_keys_ref, new_values_ref, query_rows, out_rows, attn_ref = scratch
    tp_index, _, _, _, own_group = places()
    length = lengths_ref[0]
    load_out, own_ref, *part_refs = outs
    tp_size = sum(ref.shape[0] for ref in part_refs)
    first = mover.start(query_hbm.at[0], query_ref)
    news = [mover.start(new_keys_hbm.at[0], new_keys_ref), mover.start(new_values_hbm.at[0], new_values_ref)]
    groups = [slice(g * HD, (g + 1) * HD) for g in range(KVH)]
    arrive = [
        (mover.start(keys_hbm.at[0, :, group], keys_ref.at[:, group]), mover.start(values_hbm.at[0, :, group], values_ref.at[:, group]))
        for group in groups
    ]
    attn = mover.start(attn_hbm, attn_ref)
    width = query_ref.shape[1]
    cache_len = keys_ref.shape[0]
    rows = width // HD // KVH * steps
    mover.wait(first)
    for h in range(width // HD):
        query_rows[h * steps : (h + 1) * steps, :] = query_ref[:, h * HD : (h + 1) * HD].astype(F32)
    usable = lax.broadcasted_iota(jnp.int32, (rows, cache_len), 1) + tp_index * cache_len < length
    left = lax.broadcasted_iota(jnp.int32, (rows, HD), 1) < HD // 2
    for g in range(KVH):
        if g == KVH - 1:
            mover.wait(attn)
            mover.start(attn_ref, load_out.at[: attn_ref.shape[0]])
        mover.wait(*arrive[g])
        query = query_rows[g * rows : (g + 1) * rows, :].astype(BF16)
        scores = over_features(query, keys_ref[:, g * HD : (g + 1) * HD]) * (1.0 / HD**0.5)
        maxima = jnp.max(jnp.where(usable, scores, NEG_FILL), axis=1, keepdims=True)
        terms = jnp.where(usable, jnp.exp(scores - maxima), 0.0)
        totals = jnp.sum(terms, axis=1, keepdims=True)
        upper = terms.astype(BF16)
        lower = (terms - upper.astype(F32)).astype(BF16)
        both = dot(jnp.concatenate([upper, lower], axis=0), values_ref[:, g * HD : (g + 1) * HD])
        out_rows[g * rows : (g + 1) * rows, :HD] = both[:rows] + both[rows:]
        out_rows[g * rows : (g + 1) * rows, HD:] = jnp.where(left, maxima, totals)
    count = part_refs[0].shape[1]
    for t in range(KVH * rows // count):
        for i, part_ref in enumerate(part_refs):
            for k in range(part_ref.shape[0]):

                @pl.when(tp_index ^ ((i and part_ref.shape[0]) + k) == t)
                def _():
                    part_ref[k] = out_rows[t * count : (t + 1) * count, :]

        @pl.when(tp_index == t)
        def _():
            own_ref[:count, :HD] = query_rows[t * count : (t + 1) * count, :]

    mover.wait(*news)
    own_ref[:count, HD:] = jnp.zeros((count, HD), F32)
    for at, ref in ((0, new_keys_ref), (HD, new_values_ref)):
        chosen = ref[:, :HD].astype(F32)
        for g in range(1, KVH):
            chosen = jnp.where(own_group == g, ref[:, groups[g]].astype(F32), chosen)
        own_ref[count : count + steps, at : at + HD] = chosen


def combine_kernel(steps, indices, load_ref, own_ref, *refs):
    *part_refs, out_ref, rows_ref, low_ref, sem = refs
    count = part_refs[0].shape[1]
    rows_ref[...] = jnp.zeros_like(rows_ref)
    step = lax.broadcasted_iota(jnp.int32, (count, 1), 0) % steps
    query = own_ref[:count, :HD]
    keys, values = own_ref[count:, :HD], own_ref[count:, HD:]
    parts = [part_ref[i] for i, part_ref in zip(indices, part_refs)]
    scores = []
    for j in range(steps):
        score = jnp.sum(query * keys[j : j + 1], axis=-1, keepdims=True) * (1.0 / HD**0.5)
        scores.append(jnp.where(step >= j, score, NEG_FILL))
    maxima = [part[:, HD : HD + 1] for part in parts]
    highest = functools.reduce(jnp.maximum, scores + maxima)
    total = jnp.zeros((count, 1), F32)
    weighted = jnp.zeros((count, HD), F32)
    for part, own in zip(parts, maxima):
        scale = jnp.exp(own - highest)
        total = total + part[:, HD + HD // 2 : HD + HD // 2 + 1] * scale
        weighted = weighted + part[:, :HD] * scale
    for j in range(steps):
        term = jnp.where(step >= j, jnp.exp(scores[j] - highest), 0.0)
        total = total + term
        weighted = weighted + term * values[j : j + 1]
    attended = weighted / total
    for row in range(count):
        h, s = row // steps, row % steps
        rows_ref[s : s + 1, h * HD : (h + 1) * HD] = attended[row : row + 1]
    low_ref[...] = rows_ref[...].astype(BF16)
    copy = pltpu.make_async_copy(low_ref, out_ref.at[out_ref.shape[0] - PAD :], sem)
    copy.start()
    copy.wait()


def middle_kernel(outer, mover, ins, outs, scratch):
    grad_hbm, weight_hbm, other_hbm, *cot_hbms = ins
    sent_outs, (total_out, cot_own_out, *cot_far_outs) = outs[: outer - 1], outs[outer - 1 :]
    cots_ref, weight_ref, other_ref, sent_ref, total_ref, cot_own_ref, cot_far_ref = scratch
    _, core, z, x, _ = places()
    tokens = grad_hbm.shape[0]
    plane = cots_ref.shape[1]
    feats = weight_ref.shape[0]
    half = tokens // 2
    weights = [mover.start(weight_hbm, weight_ref), mover.start(other_hbm, other_ref)]
    blocks = [[mover.start(grad_hbm.at[:, pl.ds(pl.multiple_of(z * plane, plane), plane)], cots_ref.at[:tokens])]]
    for k in range(1, outer):
        blocks.append([])
        for hbms, side in ((cot_hbms[:2], core), (cot_hbms[2:], 1 - core)):
            base = pl.multiple_of(k * tokens + side * half, half)
            for i, hbm in enumerate(hbms):
                size = hbm.shape[0]
                low, high = max((k - 1) * half, i * size), min(k * half, (i + 1) * size)
                if low < high:
                    source = hbm.at[low - i * size : high - i * size]
                    first = pl.multiple_of(base + (low - (k - 1) * half), half // 2)
                    blocks[k].append(mover.start(source, cots_ref.at[pl.ds(first, high - low)]))
    mover.wait(*weights)
    span = outer * half
    for k in reversed(range(outer)):
        mover.wait(*blocks[k])
        here = slice(k * tokens, (k + 1) * tokens)
        block = cots_ref[here, :]
        low, high = block[:, :feats], block[:, feats:]
        own = jnp.where(x == 0, low, high)
        other = jnp.where(x == 0, high, low)
        total = dot(own, weight_ref[...]) + dot(other, other_ref[...])
        if k == 0:
            total_ref[...] = total
            mover.start(total_ref, total_out)
        else:
            sent_ref[k - 1] = total.astype(BF16)
            mover.start(sent_ref.at[k - 1], sent_outs[k - 1])
        cot_own_ref[here, :] = own
        cot_far_ref[here, :] = other

    for i, out in enumerate(cot_far_outs):
        mover.start(cot_far_ref.at[i * span : (i + 1) * span], out)
    mover.start(cot_own_ref, cot_own_out)


def decode_kernel(steps, mover, ins, outs, scratch):
    weight_hbm, other_hbm, *load_hbms = ins
    weight_ref, other_ref, dec_ref, rows_ref, by_row_ref, parts_ref = scratch
    _, _, z, x, _ = places()
    tokens = load_hbms[0].shape[0] - PAD
    outer, share = len(load_hbms), outs[0].shape[1]
    arrive = [mover.start(hbm.at[tokens:], dec_ref.at[k]) for k, hbm in enumerate(load_hbms)]
    mover.wait(*arrive, mover.start(weight_hbm, weight_ref), mover.start(other_hbm, other_ref))
    for k in range(outer):
        rows_ref[k * steps : (k + 1) * steps, :] = dec_ref[k].astype(F32)[:steps]
    every = rows_ref[...].astype(BF16)
    own, other = over_features(every, weight_ref[...]), over_features(every, other_ref[...])
    wide = jnp.concatenate([jnp.where(x == 0, own, other), jnp.where(x == 0, other, own)], axis=1)
    for k in range(outer):
        by_row_ref[k] = wide[k * steps : (k + 1) * steps]
    for q in range(parts_ref.shape[0]):
        for i in range(share):
            parts_ref[q, i] = by_row_ref[(z - (q * share + i)) % outer]
    mover.start(parts_ref, outs[0])


def own_kernel(mover, ins, outs, scratch):
    cots_ref, attn_ref, out_ref = scratch
    mover.wait(mover.start(ins[0], cots_ref), mover.start(ins[1], attn_ref))
    pieces = 2
    step = out_ref.shape[0] // pieces
    for i in range(pieces):
        here = slice(i * step, (i + 1) * step)
        out_ref[here, :] = over_tokens(cots_ref[:, here], attn_ref[...])
        mover.start(out_ref.at[here], outs[0].at[here])


def last_kernel(outer, share, mover, ins, outs, scratch):
    total_hbm, own_hbm, attn_hbm, *rest = ins
    cot_hbms, part_hbms, piece_hbms = rest[:2], rest[2 : outer + 1], rest[outer + 1 :]
    total_ref, parts_ref, sum_ref, pieces_ref, cots_ref, attn_ref, own_ref, out_ref = scratch
    _, _, z, _, _ = places()
    plane = pieces_ref.shape[2]
    span = cot_hbms[0].shape[0]
    attn = mover.start(attn_hbm, attn_ref)
    cots = [mover.start(hbm, cots_ref.at[i * span : (i + 1) * span]) for i, hbm in enumerate(cot_hbms)]
    pieces = 2
    step = out_ref.shape[0] // pieces
    heres = [slice(i * step, (i + 1) * step) for i in range(pieces)]
    owns = [mover.start(own_hbm.at[here], own_ref.at[here]) for here in heres]
    arrive = [mover.start(total_hbm, total_ref)]
    arrive += [mover.start(hbm, parts_ref.at[i]) for i, hbm in enumerate(part_hbms)]
    places_in = [mover.start(hbm, pieces_ref.at[j]) for j, hbm in enumerate(piece_hbms)]
    mover.wait(attn, *cots)
    for here, own in zip(heres, owns):
        product = over_tokens(cots_ref[:, here], attn_ref[...])
        mover.wait(own)
        out_ref[here, :] = own_ref[here, :] + product
        mover.start(out_ref.at[here], outs[2].at[here])
    mover.wait(*arrive)
    total = total_ref[...]
    for i in range(outer - 1):
        total = total + parts_ref[i].astype(F32)
    sum_ref[...] = total.astype(BF16)
    mover.start(sum_ref, outs[1])
    mover.wait(*places_in)
    for j in range(share):
        mover.start(pieces_ref.at[j], outs[0].at[0, :, pl.ds(pl.multiple_of((z % share ^ j) * plane, plane), plane)])


def stack_kernel(mover, ins, outs, scratch):
    half, size = ins[0].shape[0], outs[0].shape[0]
    arrive = [mover.start(hbm, scratch[0].at[k * half : (k + 1) * half]) for k, hbm in enumerate(ins)]
    mover.wait(*arrive)
    for i, out in enumerate(outs):
        mover.start(scratch[0].at[i * size : (i + 1) * size], out)


def gate_kernel(count, wait_count, *refs):
    refs, (pack_out, pack_ref, in_sems, out_sems) = refs[count : -4 - count], refs[-4:]
    refs = refs[:len(refs) - wait_count]
    tokens = pack_out.shape[0] // len(refs)
    parts = [slice(k * tokens, (k + 1) * tokens) for k in range(len(refs))]
    arrive = [pltpu.make_async_copy(ref.at[:tokens], pack_ref.at[part], in_sems.at[k]) for k, (ref, part) in enumerate(zip(refs, parts))]
    leave = [pltpu.make_async_copy(pack_ref.at[part], pack_out.at[part], out_sems.at[k]) for k, part in enumerate(parts)]
    for copy in arrive:
        copy.start()
    for copy, follow in zip(arrive, leave):
        copy.wait()
        follow.start()
    for copy in leave:
        copy.wait()


def shards(dec_query, new_keys, new_values, cache_keys, cache_values, lengths, out_weight, train_attn, grad_out):
    rows, steps, width = dec_query.shape
    assert rows == 1
    fsdp_size = lax.axis_size("fsdp")
    tp_size = lax.axis_size("tp")
    outer = fsdp_size // INNER
    share = outer // tp_size
    fsdp_index = lax.axis_index("fsdp")
    tp_index = lax.axis_index("tp")
    z, x = fsdp_index // INNER, fsdp_index % INNER
    tokens = grad_out.shape[0]
    feats, cols = out_weight.shape
    plane = feats * INNER
    slot = tp_index % 4
    heads = width // HD
    count = heads // tp_size * steps
    far = range(1, outer)
    others = range(1, tp_size)

    other_weight = flip(out_weight, "fsdp", 1, "weight_x")

    half = tokens // 2

    first = tp_index % 2 * half
    got = [
        turn(lax.dynamic_slice(grad_out, (first, (z + k) % outer * plane), (half, plane)), k, f"cot_z{k}") for k in far
    ]

    sizes = [1 << b for b in range(tp_size.bit_length() - 1)]
    load, own, part, *chunks = call(
        functools.partial(attend_kernel, steps),
        "attend",
        [dec_query, cache_keys, cache_values, new_keys, new_values, train_attn],
        [((tokens + PAD, cols), BF16), ((count + 8, 2 * HD), F32), ((1, count, 2 * HD), F32)]
        + [((size, count, 2 * HD), F32) for size in sizes],
        shaped(dec_query[0], cache_keys[0], cache_values[0], new_keys[0], new_values[0])
        + [((heads * steps, HD), F32), ((heads * steps, 2 * HD), F32), ((tokens, cols), BF16)],
        scalars=lengths,
        room=63,
        fast=range(1, 3 + len(sizes)),
    )
    parts, indices, held = [part], [0], []
    for size, chunk in reversed(list(zip(sizes, chunks))):
        if size > 1:
            came = [flip(a, "tp", size, f"softmax_tp{size}") for a in [chunk] + [a[size:] for a in held]]
            held = [a[:size] for a in held] + came
        else:
            parts += held + [flip(a, "tp", size, f"softmax_tp{size}") for a in [chunk] + held]
            indices += [0] * len(held) + [0] + [1] * len(held)
    load = pl.pallas_call(
        functools.partial(combine_kernel, steps, indices),
        out_shape=jax.ShapeDtypeStruct((tokens + PAD, cols), BF16),
        in_specs=[pl.BlockSpec(memory_space=pltpu.HBM)] + [pl.BlockSpec(memory_space=pltpu.VMEM)] * (len(parts) + 1),
        out_specs=pl.BlockSpec(memory_space=pltpu.HBM),
        scratch_shapes=[pltpu.VMEM((PAD, cols), F32), pltpu.VMEM((PAD, cols), BF16), pltpu.SemaphoreType.DMA],
        input_output_aliases={0: 0},
        cost_estimate=pl.CostEstimate(flops=0, bytes_accessed=0, transcendentals=0),
        name="combine",
    )(load, own, *parts)
    loads = [turn(load, k, f"attn_z{k}") for k in far]

    stacked = call(
        stack_kernel,
        "stack",
        got,
        [((len(far) * half // 2, plane), BF16)] * 2,
        [((len(far) * half, plane), BF16)],
        waits=[load],
    )
    twins = [flip(a, "tp", 1, "cot_core") for a in stacked]

    *sent, total, cot_own, cot_low, cot_high = call(
        functools.partial(middle_kernel, outer),
        "middle",
        [grad_out, out_weight, other_weight, *stacked, *twins],
        [((tokens, cols), BF16)] * len(far)
        + [((tokens, cols), F32), ((outer * tokens, feats), BF16)] + [((outer * half, feats), BF16)] * 2,
        [
            ((outer * tokens, plane), BF16),
            ((feats, cols), BF16),
            ((feats, cols), BF16),
            ((len(far), tokens, cols), BF16),
            ((tokens, cols), F32),
            ((outer * tokens, feats), BF16),
            ((outer * tokens, feats), BF16),
        ],
        room=63,
    )
    cots_x = [flip(a, "fsdp", 1, "cot_x") for a in (cot_low, cot_high)]

    waits = cots_x
    results = pl.pallas_call(
        functools.partial(gate_kernel, len(sent), len(waits)),
        out_shape=[jax.ShapeDtypeStruct(a.shape, a.dtype) for a in sent]
        + [jax.ShapeDtypeStruct((outer * tokens, cols), BF16)],
        in_specs=[pl.BlockSpec(memory_space=pltpu.HBM)] * (len(sent) + outer + len(waits)),
        out_specs=[pl.BlockSpec(memory_space=pltpu.HBM)] * (len(sent) + 1),
        scratch_shapes=[
            pltpu.VMEM((outer * tokens, cols), BF16),
            pltpu.SemaphoreType.DMA((outer,)),
            pltpu.SemaphoreType.DMA((outer,)),
        ],
        input_output_aliases={i: i for i in range(len(sent))},
        compiler_params=pltpu.CompilerParams(vmem_limit_bytes=63 << 20),
        cost_estimate=pl.CostEstimate(flops=0, bytes_accessed=0, transcendentals=0),
        name="gate",
    )(*sent, load, *loads, *waits)
    sent, pack = results[:-1], results[-1]
    sums = [turn(sent[k - 1], outer - k, f"sum_z{k}") for k in far]
    pack_x = flip(pack, "fsdp", 1, "attn_x")
    (dec,) = call(
        functools.partial(decode_kernel, steps),
        "decode",
        [out_weight, other_weight, load, *loads],
        [((tp_size, share, steps, plane), F32)],
        [
            ((feats, cols), BF16),
            ((feats, cols), BF16),
            ((outer, PAD, cols), BF16),
            ((outer * steps, cols), F32),
            ((outer, steps, plane), F32),
            ((tp_size, share, steps, plane), F32),
        ],
        waits=[pack],
        room=63,
    )
    with jax.named_scope("dec_tp"):
        dec = lax.all_to_all(dec, "tp", 0, 0, tiled=True).sum(axis=0).astype(BF16)
    pieces = []
    for j in range(share):
        perm = [
            ((a * INNER + b) * tp_size + q, ((q * share + (a % share ^ j)) * INNER + b) * tp_size + a // share)
            for a in range(outer)
            for b in range(INNER)
            for q in range(tp_size)
        ]
        with jax.named_scope("dec_place"):
            pieces.append(lax.ppermute(lax.dynamic_index_in_dim(dec, z % share ^ j, 0, False), ("fsdp", "tp"), perm))
    (own_total,) = call(
        own_kernel,
        "own",
        [cot_own, pack],
        [((feats, cols), F32)],
        [((outer * tokens, feats), BF16), ((outer * tokens, cols), BF16), ((feats, cols), F32)],
        room=63,
    )
    dec_out, grad_attn, grad_weight = call(
        functools.partial(last_kernel, outer, share),
        "last",
        [total, own_total, pack_x, *cots_x, *sums, *pieces],
        [((rows, steps, share * plane), BF16), ((tokens, cols), BF16), ((feats, cols), F32)],
        [
            ((tokens, cols), F32),
            ((len(far), tokens, cols), BF16),
            ((tokens, cols), BF16),
            ((share, steps, plane), BF16),
            ((outer * tokens, feats), BF16),
            ((outer * tokens, cols), BF16),
            ((feats, cols), F32),
            ((feats, cols), F32),
        ],
        room=63,
    )
    return dec_out, grad_attn, grad_weight


def solution(mesh):
    return jax.shard_map(
        shards,
        mesh=mesh,
        in_specs=(
            P("fsdp", None, None),
            P("fsdp", None, None),
            P("fsdp", None, None),
            P("fsdp", "tp", None),
            P("fsdp", "tp", None),
            P("fsdp"),
            P("fsdp", "tp"),
            P("fsdp", "tp"),
            P("fsdp", None),
        ),
        out_specs=(P("fsdp", None, "tp"), P("fsdp", "tp"), P("fsdp", "tp")),
        check_vma=False,
    )
```

```python
import functools

import jax
import jax.numpy as jnp
from jax import lax
from jax.experimental import pallas as pl
from jax.experimental.pallas import tpu as pltpu
from jax.sharding import PartitionSpec as P

KVH = 4
HD = 128
NEG_FILL = -1e30
INNER = 2
PAD = 16
BF16 = jnp.bfloat16
F32 = jnp.float32


def flip(a, axis, bits, name):
    size = lax.axis_size(axis)
    with jax.named_scope(name):
        return lax.ppermute(a, axis, [(i, i ^ bits) for i in range(size)])


def turn(a, steps, name):
    outer = lax.axis_size("fsdp") // INNER
    with jax.named_scope(name):
        return lax.ppermute(
            a, "fsdp", [(z * INNER + x, (z + steps) % outer * INNER + x) for z in range(outer) for x in range(INNER)]
        )


def dot(a, b):
    return jnp.dot(a, b, preferred_element_type=F32)


def over_features(a, b):
    return lax.dot_general(a, b, (((1,), (1,)), ((), ())), preferred_element_type=F32)


def over_tokens(a, b):
    return lax.dot_general(a, b, (((0,), (0,)), ((), ())), preferred_element_type=F32)


class Mover:
    def __init__(self, sems):
        self.sems, self.count, self.open = sems, 0, []

    def start(self, source, target):
        copy = pltpu.make_async_copy(source, target, self.sems.at[self.count])
        self.count += 1
        self.open.append(copy)
        copy.start()
        return copy

    def wait(self, *copies):
        for copy in copies:
            copy.wait()
            self.open = [other for other in self.open if other is not copy]

    def finish(self):
        self.wait(*list(self.open))


def places():
    fsdp_index, tp_index = lax.axis_index("fsdp"), lax.axis_index("tp")
    return tp_index, tp_index % 2, fsdp_index // INNER, fsdp_index % INNER, tp_index * KVH // lax.axis_size("tp")


def call(kernel, name, operands, out_shapes, scratch, waits=(), scalars=None, room=12, fast=(), near=()):
    copies = 4 * (len(operands) + len(out_shapes))
    scalars = [] if scalars is None else [scalars]

    def body(*refs):
        front, refs = refs[: len(scalars)], refs[len(scalars) :]
        ins, refs = refs[: len(operands)], refs[len(operands) + len(waits) :]
        outs, refs = refs[: len(out_shapes)], refs[len(out_shapes) :]
        mover = Mover(refs[-1])
        kernel(mover, *front, ins, outs, refs[:-1])
        mover.finish()

    results = pl.pallas_call(
        body,
        out_shape=[jax.ShapeDtypeStruct(shape, dtype) for shape, dtype in out_shapes],
        in_specs=[pl.BlockSpec(memory_space=pltpu.SMEM)] * len(scalars)
        + [pl.BlockSpec(memory_space=pltpu.VMEM if i in near else pltpu.HBM) for i in range(len(operands))]
        + [pl.BlockSpec(memory_space=pltpu.HBM)] * len(waits),
        out_specs=[
            pl.BlockSpec(memory_space=pltpu.VMEM if i in fast else pltpu.HBM) for i in range(len(out_shapes))
        ],
        scratch_shapes=[pltpu.VMEM(shape, dtype) for shape, dtype in scratch] + [pltpu.SemaphoreType.DMA((copies,))],
        compiler_params=pltpu.CompilerParams(vmem_limit_bytes=room << 20),
        cost_estimate=pl.CostEstimate(flops=0, bytes_accessed=0, transcendentals=0),
        name=name,
    )(*scalars, *operands, *waits)
    return list(results)


def kept(arrays, waits, name):
    count = len(arrays)
    results = pl.pallas_call(
        lambda *refs: None,
        out_shape=[jax.ShapeDtypeStruct(a.shape, a.dtype) for a in arrays],
        in_specs=[pl.BlockSpec(memory_space=pltpu.HBM)] * (count + len(waits)),
        out_specs=[pl.BlockSpec(memory_space=pltpu.HBM)] * count,
        input_output_aliases={i: i for i in range(count)},
        compiler_params=pltpu.CompilerParams(vmem_limit_bytes=12 << 20),
        cost_estimate=pl.CostEstimate(flops=0, bytes_accessed=0, transcendentals=0),
        name=name,
    )(*arrays, *waits)
    return list(results)


def shaped(*arrays):
    return [(a.shape, a.dtype) for a in arrays]


def attend_kernel(steps, mover, lengths_ref, ins, outs, scratch):
    query_hbm, keys_hbm, values_hbm, new_keys_hbm, new_values_hbm = ins
    query_ref, keys_ref, values_ref, new_keys_ref, new_values_ref, query_rows, out_rows = scratch
    tp_index, _, _, _, own_group = places()
    length = lengths_ref[0]
    own_ref, *chunk_refs = outs
    first = mover.start(query_hbm.at[0], query_ref)
    news = [mover.start(new_keys_hbm.at[0], new_keys_ref), mover.start(new_values_hbm.at[0], new_values_ref)]
    groups = [slice(g * HD, (g + 1) * HD) for g in range(KVH)]
    arrive = [
        (mover.start(keys_hbm.at[0, :, group], keys_ref.at[:, group]), mover.start(values_hbm.at[0, :, group], values_ref.at[:, group]))
        for group in groups
    ]
    width = query_ref.shape[1]
    cache_len = keys_ref.shape[0]
    rows = width // HD // KVH * steps
    mover.wait(first)
    for h in range(width // HD):
        query_rows[h * steps : (h + 1) * steps, :] = query_ref[:, h * HD : (h + 1) * HD].astype(F32)
    usable = lax.broadcasted_iota(jnp.int32, (rows, cache_len), 1) + tp_index * cache_len < length
    left = lax.broadcasted_iota(jnp.int32, (rows, HD), 1) < HD // 2
    for g in range(KVH):
        mover.wait(*arrive[g])
        query = query_rows[g * rows : (g + 1) * rows, :].astype(BF16)
        scores = over_features(query, keys_ref[:, g * HD : (g + 1) * HD]) * (1.0 / HD**0.5)
        maxima = jnp.max(jnp.where(usable, scores, NEG_FILL), axis=1, keepdims=True)
        terms = jnp.where(usable, jnp.exp(scores - maxima), 0.0)
        totals = jnp.sum(terms, axis=1, keepdims=True)
        upper = terms.astype(BF16)
        lower = (terms - upper.astype(F32)).astype(BF16)
        both = dot(jnp.concatenate([upper, lower], axis=0), values_ref[:, g * HD : (g + 1) * HD])
        out_rows[g * rows : (g + 1) * rows, :HD] = both[:rows] + both[rows:]
        out_rows[g * rows : (g + 1) * rows, HD:] = jnp.where(left, maxima, totals)
    count = chunk_refs[0].shape[1]
    for t in range(KVH * rows // count):
        for chunk_ref in chunk_refs:
            for k in range(chunk_ref.shape[0]):

                @pl.when(tp_index ^ (chunk_ref.shape[0] + k) == t)
                def _():
                    chunk_ref[k] = out_rows[t * count : (t + 1) * count, :]

        @pl.when(tp_index == t)
        def _():
            own_ref[:count, :] = out_rows[t * count : (t + 1) * count, :]
            own_ref[count : 2 * count, :HD] = query_rows[t * count : (t + 1) * count, :]

    mover.wait(*news)
    own_ref[count : 2 * count, HD:] = jnp.zeros((count, HD), F32)
    for at, ref in ((0, new_keys_ref), (HD, new_values_ref)):
        chosen = ref[:, :HD].astype(F32)
        for g in range(1, KVH):
            chosen = jnp.where(own_group == g, ref[:, groups[g]].astype(F32), chosen)
        own_ref[2 * count : 2 * count + steps, at : at + HD] = chosen


def combine_kernel(steps, sent, indices, attn_hbm, own_ref, *refs):
    *part_refs, out_hbm, rows_ref, load_ref, sems = refs
    rest = attn_hbm.shape[0] - sent
    arrive = pltpu.make_async_copy(attn_hbm.at[sent:], load_ref.at[:rest], sems.at[0])
    arrive.start()
    count = part_refs[0].shape[1]
    own = own_ref[...]
    rows_ref[...] = jnp.zeros_like(rows_ref)
    step = lax.broadcasted_iota(jnp.int32, (count, 1), 0) % steps
    query = own[count : 2 * count, :HD]
    keys, values = own[2 * count :, :HD], own[2 * count :, HD:]
    parts = [own[:count]] + [part_ref[i] for i, part_ref in zip(indices, part_refs)]
    scores = []
    for j in range(steps):
        score = jnp.sum(query * keys[j : j + 1], axis=-1, keepdims=True) * (1.0 / HD**0.5)
        scores.append(jnp.where(step >= j, score, NEG_FILL))
    maxima = [part[:, HD : HD + 1] for part in parts]
    highest = functools.reduce(jnp.maximum, scores + maxima)
    total = jnp.zeros((count, 1), F32)
    weighted = jnp.zeros((count, HD), F32)
    for part, own in zip(parts, maxima):
        scale = jnp.exp(own - highest)
        total = total + part[:, HD + HD // 2 : HD + HD // 2 + 1] * scale
        weighted = weighted + part[:, :HD] * scale
    for j in range(steps):
        term = jnp.where(step >= j, jnp.exp(scores[j] - highest), 0.0)
        total = total + term
        weighted = weighted + term * values[j : j + 1]
    attended = weighted / total
    for row in range(count):
        h, s = row // steps, row % steps
        rows_ref[s : s + 1, h * HD : (h + 1) * HD] = attended[row : row + 1]
    load_ref[rest:, :] = rows_ref[...].astype(BF16)
    arrive.wait()
    leave = pltpu.make_async_copy(load_ref, out_hbm, sems.at[1])
    leave.start()
    leave.wait()


def cut_kernel(outer, half, early, mover, ins, outs, scratch):
    grad_hbm, attn_hbm = ins
    plane = outs[0].shape[1]
    _, core, z, _, _ = places()
    rows = pl.ds(pl.multiple_of(core * half, half), half)
    for k in range(1, outer):
        columns = pl.ds(pl.multiple_of((z + k) % outer * plane, plane), plane)
        mover.start(grad_hbm.at[rows, columns], scratch[0].at[k - 1, :half])
        mover.start(attn_hbm.at[:early], scratch[0].at[k - 1, half:])
    arrive = list(mover.open)
    for k in range(1, outer):
        mover.wait(*arrive[2 * k - 2 : 2 * k])
        mover.start(scratch[0].at[k - 1], outs[k - 1])


def middle_kernel(outer, mover, ins, outs, scratch):
    grad_hbm, weight_hbm, other_hbm, *cot_hbms = ins
    sent_outs, (total_out, cot_own_out, *cot_far_outs) = outs[: outer - 1], outs[outer - 1 :]
    cots_ref, weight_ref, other_ref, sent_ref, total_ref, cot_own_ref, cot_far_ref = scratch
    _, core, z, x, _ = places()
    tokens = grad_hbm.shape[0]
    plane = cots_ref.shape[1]
    feats = weight_ref.shape[0]
    half = tokens // 2
    weights = [mover.start(weight_hbm, weight_ref), mover.start(other_hbm, other_ref)]
    blocks = [[mover.start(grad_hbm.at[:, pl.ds(pl.multiple_of(z * plane, plane), plane)], cots_ref.at[:tokens])]]
    for k in range(1, outer):
        blocks.append([])
        for hbm, side in ((cot_hbms[k - 1], core), (cot_hbms[outer + k - 2], 1 - core)):
            first = pl.multiple_of(k * tokens + side * half, half)
            blocks[k].append(mover.start(hbm.at[:half], cots_ref.at[pl.ds(first, half)]))
    mover.wait(*weights)
    span = outer * half
    for k in reversed(range(outer)):
        mover.wait(*blocks[k])
        here = slice(k * tokens, (k + 1) * tokens)
        block = cots_ref[here, :]
        low, high = block[:, :feats], block[:, feats:]
        own = jnp.where(x == 0, low, high)
        other = jnp.where(x == 0, high, low)
        total = dot(own, weight_ref[...]) + dot(other, other_ref[...])
        if k == 0:
            total_ref[...] = total
            mover.start(total_ref, total_out)
        else:
            sent_ref[k - 1] = total.astype(BF16)
            mover.start(sent_ref.at[k - 1], sent_outs[k - 1])
        cot_own_ref[here, :] = own
        cot_far_ref[here, :] = other

    size = cot_far_outs[0].shape[0]
    for i, out in enumerate(cot_far_outs):
        first = pl.multiple_of(core * span + i * size, size)
        mover.start(cot_far_ref.at[pl.ds(first, size)], out)
    mover.start(cot_own_ref, cot_own_out)


def decode_kernel(steps, mover, ins, outs, scratch):
    weight_hbm, other_hbm, *load_hbms = ins
    weight_ref, other_ref, dec_ref, rows_ref, by_row_ref, parts_ref = scratch
    _, _, z, x, _ = places()
    tokens = load_hbms[0].shape[0] - PAD
    outer, share = len(load_hbms), outs[0].shape[1]
    arrive = [mover.start(hbm.at[tokens:], dec_ref.at[k]) for k, hbm in enumerate(load_hbms)]
    mover.wait(*arrive, mover.start(weight_hbm, weight_ref), mover.start(other_hbm, other_ref))
    for k in range(outer):
        rows_ref[k * steps : (k + 1) * steps, :] = dec_ref[k].astype(F32)[:steps]
    every = rows_ref[...].astype(BF16)
    own, other = over_features(every, weight_ref[...]), over_features(every, other_ref[...])
    wide = jnp.concatenate([jnp.where(x == 0, own, other), jnp.where(x == 0, other, own)], axis=1)
    for k in range(outer):
        by_row_ref[k] = wide[k * steps : (k + 1) * steps]
    for q in range(parts_ref.shape[0]):
        for i in range(share):
            parts_ref[q, i] = by_row_ref[(z - (q * share + i)) % outer]
    mover.start(parts_ref, outs[0])


def own_kernel(mover, ins, outs, scratch):
    cots_ref, attn_ref = scratch
    mover.wait(mover.start(ins[0], cots_ref), mover.start(ins[1], attn_ref))
    outs[0][...] = over_tokens(cots_ref[...], attn_ref[...])


def last_kernel(outer, share, mover, ins, outs, scratch):
    total_ref, own_ref, attn_ref, *rest = ins
    cot_refs, part_refs, piece_refs = rest[:2], rest[2 : outer + 1], rest[outer + 1 :]
    sum_ref, cots_ref, out_ref = scratch
    _, core, z, _, _ = places()
    plane = piece_refs[0].shape[1]
    size = cot_refs[0].shape[0]
    for j in range(share):
        mover.start(piece_refs[j], outs[0].at[0, :, pl.ds(pl.multiple_of((z % share ^ j) * plane, plane), plane)])
    for i, ref in enumerate(cot_refs):
        first = pl.multiple_of((core ^ i) * size, size)
        cots_ref[pl.ds(first, size), :] = ref[...]
    pieces = 2
    step = out_ref.shape[0] // pieces
    for i in range(pieces):
        here = slice(i * step, (i + 1) * step)
        out_ref[here, :] = own_ref[here, :] + over_tokens(cots_ref[:, here], attn_ref[...])
        mover.start(out_ref.at[here], outs[2].at[here])
    total = total_ref[...]
    for part_ref in part_refs:
        total = total + part_ref[...].astype(F32)
    sum_ref[...] = total.astype(BF16)
    mover.start(sum_ref, outs[1])


def pack_kernel(early, skip, mover, ins, outs, scratch):
    low_hbm, high_hbm, own_hbm, *first_hbms = ins
    cots_ref, attn_ref = scratch
    tokens, size = own_hbm.shape[0], low_hbm.shape[0]
    parts = [(low_hbm, cots_ref, outs[0], 0, size), (high_hbm, cots_ref, outs[0], size, size), (own_hbm, attn_ref, outs[1], 0, tokens)]
    parts += [(hbm.at[skip:], attn_ref, outs[1], (k + 1) * tokens, early) for k, hbm in enumerate(first_hbms)]
    arrive = [mover.start(source, ref.at[at : at + rows]) for source, ref, _, at, rows in parts]
    for copy, (_, ref, out, at, rows) in zip(arrive, parts):
        mover.wait(copy)
        mover.start(ref.at[at : at + rows], out.at[at : at + rows])


def gate_kernel(count, early, *refs):
    refs, pack_out, (last_ref, in_sems, out_sems) = refs[count + 2 : -4 - count], refs[-4], refs[-3:]
    rest = refs[0].shape[0] - PAD
    tokens = rest + early
    arrive, leave = [], []
    for k, ref in enumerate(refs):
        arrive.append(pltpu.make_async_copy(ref.at[:rest], last_ref.at[k], in_sems.at[k]))
        target = pack_out.at[(k + 1) * tokens + early : (k + 2) * tokens]
        leave.append(pltpu.make_async_copy(last_ref.at[k], target, out_sems.at[k]))
    for copy in arrive:
        copy.start()
    for copy, follow in zip(arrive, leave):
        copy.wait()
        follow.start()
    for copy in leave:
        copy.wait()


def shards(dec_query, new_keys, new_values, cache_keys, cache_values, lengths, out_weight, train_attn, grad_out):
    rows, steps, width = dec_query.shape
    assert rows == 1
    fsdp_size = lax.axis_size("fsdp")
    tp_size = lax.axis_size("tp")
    outer = fsdp_size // INNER
    share = outer // tp_size
    fsdp_index = lax.axis_index("fsdp")
    tp_index = lax.axis_index("tp")
    z, x = fsdp_index // INNER, fsdp_index % INNER
    tokens = grad_out.shape[0]
    feats, cols = out_weight.shape
    plane = feats * INNER
    slot = tp_index % 4
    heads = width // HD
    count = heads // tp_size * steps
    far = range(1, outer)
    others = range(1, tp_size)

    other_weight = flip(out_weight, "fsdp", 1, "weight_x")

    half = tokens // 2

    early = tokens // 4
    cot_rows = half * plane // cols
    if plane == cols:
        cuts = call(
            functools.partial(cut_kernel, outer, half, early),
            "cut",
            [grad_out, train_attn],
            [((half + early, cols), BF16)] * len(far),
            [((len(far), half + early, cols), BF16)],
            room=63,
        )
    else:
        first = tp_index % 2 * half
        cuts = [
            jnp.concatenate(
                [
                    lax.dynamic_slice(grad_out, (first, (z + k) % outer * plane), (half, plane)).reshape(cot_rows, cols),
                    train_attn[:early],
                ]
            )
            for k in far
        ]
    firsts = [turn(cuts[k - 1], k, f"first_z{k}") for k in far]
    got = firsts if plane == cols else [a[:cot_rows].reshape(half, plane) for a in firsts]

    sizes = [1 << b for b in range(tp_size.bit_length() - 1)]
    own, *chunks = call(
        functools.partial(attend_kernel, steps),
        "attend",
        [dec_query, cache_keys, cache_values, new_keys, new_values],
        [((2 * count + 8, 2 * HD), F32)]
        + [((size, count, 2 * HD), F32) for size in sizes],
        shaped(dec_query[0], cache_keys[0], cache_values[0], new_keys[0], new_values[0])
        + [((heads * steps, HD), F32), ((heads * steps, 2 * HD), F32)],
        scalars=lengths,
        room=63,
        fast=range(1 + len(sizes)),
    )
    own = pl.pallas_call(
        lambda in_ref, out_ref: out_ref.__setitem__(..., in_ref[...]),
        out_shape=jax.ShapeDtypeStruct(own.shape, own.dtype),
        in_specs=[pl.BlockSpec(memory_space=pltpu.VMEM)],
        out_specs=pl.BlockSpec(memory_space=pltpu.VMEM),
        compiler_params=pltpu.CompilerParams(vmem_limit_bytes=12 << 20),
        cost_estimate=pl.CostEstimate(flops=0, bytes_accessed=0, transcendentals=0),
        name="hold",
    )(own)
    parts, indices, held = [], [], []
    for size, chunk in reversed(list(zip(sizes, chunks))):
        if size > 1:
            came = [flip(a, "tp", size, f"softmax_tp{size}") for a in [chunk] + [a[size:] for a in held]]
            held = [a[:size] for a in held] + came
        else:
            parts += held + [flip(a, "tp", size, f"softmax_tp{size}") for a in [chunk] + held]
            indices += [0] * len(held) + [0] + [1] * len(held)
    last = pl.pallas_call(
        functools.partial(combine_kernel, steps, early, indices),
        out_shape=jax.ShapeDtypeStruct((tokens - early + PAD, cols), BF16),
        in_specs=[pl.BlockSpec(memory_space=pltpu.HBM)] + [pl.BlockSpec(memory_space=pltpu.VMEM)] * (len(parts) + 1),
        out_specs=pl.BlockSpec(memory_space=pltpu.HBM),
        scratch_shapes=[
            pltpu.VMEM((PAD, cols), F32),
            pltpu.VMEM((tokens - early + PAD, cols), BF16),
            pltpu.SemaphoreType.DMA((2,)),
        ],
        compiler_params=pltpu.CompilerParams(vmem_limit_bytes=12 << 20),
        cost_estimate=pl.CostEstimate(flops=0, bytes_accessed=0, transcendentals=0),
        name="combine",
    )(train_attn, own, *parts)

    lasts = [last] + [turn(last, k, f"last_z{k}") for k in far]

    got = kept(got, [last], "kept")
    twins = [flip(a, "tp", 1, "cot_core") for a in got]

    *sent, total, cot_own, cot_low, cot_high = call(
        functools.partial(middle_kernel, outer),
        "middle",
        [grad_out, out_weight, other_weight, *got, *twins],
        [((tokens, cols), BF16)] * len(far)
        + [((tokens, cols), F32), ((outer * tokens, feats), BF16)] + [((outer * half // 2, feats), BF16)] * 2,
        [
            ((outer * tokens, plane), BF16),
            ((feats, cols), BF16),
            ((feats, cols), BF16),
            ((len(far), tokens, cols), BF16),
            ((tokens, cols), F32),
            ((outer * tokens, feats), BF16),
            ((outer * tokens, feats), BF16),
        ],
        room=63,
    )
    cots_x = [flip(a, "fsdp", 1, "cot_x") for a in (cot_low, cot_high)]

    cots_x, pack = call(
        functools.partial(pack_kernel, early, cot_rows),
        "pack",
        [*cots_x, train_attn, *(got if plane == cols else firsts)],
        [((outer * half, feats), BF16), ((outer * tokens, cols), BF16)],
        [((outer * half, feats), BF16), ((outer * tokens, cols), BF16)],
        room=63,
    )

    results = pl.pallas_call(
        functools.partial(gate_kernel, len(sent), early),
        out_shape=[jax.ShapeDtypeStruct(a.shape, a.dtype) for a in [*sent, pack]],
        in_specs=[pl.BlockSpec(memory_space=pltpu.HBM)] * (len(sent) + 2 + len(far)),
        out_specs=[pl.BlockSpec(memory_space=pltpu.HBM)] * (len(sent) + 1),
        scratch_shapes=[
            pltpu.VMEM((len(far), tokens - early, cols), BF16),
            pltpu.SemaphoreType.DMA((len(far),)),
            pltpu.SemaphoreType.DMA((len(far),)),
        ],
        input_output_aliases={i: i for i in range(len(sent) + 1)},
        compiler_params=pltpu.CompilerParams(vmem_limit_bytes=63 << 20),
        cost_estimate=pl.CostEstimate(flops=0, bytes_accessed=0, transcendentals=0),
        name="gate",
    )(*sent, pack, cots_x, *lasts[1:])
    sent, pack = results[:-1], results[-1]
    sums = [turn(sent[k - 1], outer - k, f"sum_z{k}") for k in far]
    pack_x = flip(pack, "fsdp", 1, "attn_x")
    twin_x = flip(cots_x, "tp", 1, "cot_x_core")

    (dec,) = call(
        functools.partial(decode_kernel, steps),
        "decode",
        [out_weight, other_weight, *lasts],
        [((tp_size, share, steps, plane), F32)],
        [
            ((feats, cols), BF16),
            ((feats, cols), BF16),
            ((outer, PAD, cols), BF16),
            ((outer * steps, cols), F32),
            ((outer, steps, plane), F32),
            ((tp_size, share, steps, plane), F32),
        ],
        waits=[pack],
        room=63,
    )
    with jax.named_scope("dec_tp"):
        dec = lax.all_to_all(dec, "tp", 0, 0, tiled=True).sum(axis=0).astype(BF16)
    pieces = []
    for j in range(share):
        perm = [
            ((a * INNER + b) * tp_size + q, ((q * share + (a % share ^ j)) * INNER + b) * tp_size + a // share)
            for a in range(outer)
            for b in range(INNER)
            for q in range(tp_size)
        ]
        with jax.named_scope("dec_place"):
            pieces.append(lax.ppermute(lax.dynamic_index_in_dim(dec, z % share ^ j, 0, False), ("fsdp", "tp"), perm))
    (own_total,) = call(
        own_kernel,
        "own",
        [cot_own, pack],
        [((feats, cols), F32)],
        [((outer * tokens, feats), BF16), ((outer * tokens, cols), BF16)],
        waits=[twin_x],
        fast=[0],
    )
    operands = [total, own_total, pack_x, cots_x, twin_x, *sums, *pieces]
    dec_out, grad_attn, grad_weight = call(
        functools.partial(last_kernel, outer, share),
        "last",
        operands,
        [((rows, steps, share * plane), BF16), ((tokens, cols), BF16), ((feats, cols), F32)],
        [((tokens, cols), BF16), ((outer * tokens, feats), BF16), ((feats, cols), F32)],
        near=range(len(operands)),
    )
    return dec_out, grad_attn, grad_weight


def solution(mesh):
    return jax.shard_map(
        shards,
        mesh=mesh,
        in_specs=(
            P("fsdp", None, None),
            P("fsdp", None, None),
            P("fsdp", None, None),
            P("fsdp", "tp", None),
            P("fsdp", "tp", None),
            P("fsdp"),
            P("fsdp", "tp"),
            P("fsdp", "tp"),
            P("fsdp", None),
        ),
        out_specs=(P("fsdp", None, "tp"), P("fsdp", "tp"), P("fsdp", "tp")),
        check_vma=False,
    )
```

```python
import functools

import jax
import jax.numpy as jnp
from jax import lax
from jax.experimental import pallas as pl
from jax.experimental.pallas import tpu as pltpu
from jax.sharding import PartitionSpec as P

KVH = 4
HD = 128
NEG_FILL = -1e30
INNER = 2
PAD = 8
BF16 = jnp.bfloat16
F32 = jnp.float32


def flip(a, axis, bits, name):
    size = lax.axis_size(axis)
    with jax.named_scope(name):
        return lax.ppermute(a, axis, [(i, i ^ bits) for i in range(size)])


def turn(a, steps, name):
    outer = lax.axis_size("fsdp") // INNER
    with jax.named_scope(name):
        return lax.ppermute(
            a, "fsdp", [(z * INNER + x, (z + steps) % outer * INNER + x) for z in range(outer) for x in range(INNER)]
        )


def dot(a, b):
    return jnp.dot(a, b, preferred_element_type=F32)


def over_features(a, b):
    return lax.dot_general(a, b, (((1,), (1,)), ((), ())), preferred_element_type=F32)


def over_tokens(a, b):
    return lax.dot_general(a, b, (((0,), (0,)), ((), ())), preferred_element_type=F32)


class Mover:
    def __init__(self, sems):
        self.sems, self.count, self.open = sems, 0, []

    def start(self, source, target):
        copy = pltpu.make_async_copy(source, target, self.sems.at[self.count])
        self.count += 1
        self.open.append(copy)
        copy.start()
        return copy

    def wait(self, *copies):
        for copy in copies:
            copy.wait()
            self.open = [other for other in self.open if other is not copy]

    def finish(self):
        self.wait(*list(self.open))


def places():
    fsdp_index, tp_index = lax.axis_index("fsdp"), lax.axis_index("tp")
    return tp_index, tp_index % 2, fsdp_index // INNER, fsdp_index % INNER, tp_index * KVH // lax.axis_size("tp")


def call(kernel, name, operands, out_shapes, scratch, waits=(), scalars=None, room=12, fast=(), near=()):
    copies = 4 * (len(operands) + len(out_shapes))
    scalars = [] if scalars is None else [scalars]

    def body(*refs):
        front, refs = refs[: len(scalars)], refs[len(scalars) :]
        ins, refs = refs[: len(operands)], refs[len(operands) + len(waits) :]
        outs, refs = refs[: len(out_shapes)], refs[len(out_shapes) :]
        mover = Mover(refs[-1])
        kernel(mover, *front, ins, outs, refs[:-1])
        mover.finish()

    results = pl.pallas_call(
        body,
        out_shape=[jax.ShapeDtypeStruct(shape, dtype) for shape, dtype in out_shapes],
        in_specs=[pl.BlockSpec(memory_space=pltpu.SMEM)] * len(scalars)
        + [pl.BlockSpec(memory_space=pltpu.VMEM if i in near else pltpu.HBM) for i in range(len(operands))]
        + [pl.BlockSpec(memory_space=pltpu.HBM)] * len(waits),
        out_specs=[
            pl.BlockSpec(memory_space=pltpu.VMEM if i in fast else pltpu.HBM) for i in range(len(out_shapes))
        ],
        scratch_shapes=[pltpu.VMEM(shape, dtype) for shape, dtype in scratch] + [pltpu.SemaphoreType.DMA((copies,))],
        compiler_params=pltpu.CompilerParams(vmem_limit_bytes=room << 20),
        cost_estimate=pl.CostEstimate(flops=0, bytes_accessed=0, transcendentals=0),
        name=name,
    )(*scalars, *operands, *waits)
    return list(results)


def kept(arrays, waits, name):
    count = len(arrays)
    results = pl.pallas_call(
        lambda *refs: None,
        out_shape=[jax.ShapeDtypeStruct(a.shape, a.dtype) for a in arrays],
        in_specs=[pl.BlockSpec(memory_space=pltpu.HBM)] * (count + len(waits)),
        out_specs=[pl.BlockSpec(memory_space=pltpu.HBM)] * count,
        input_output_aliases={i: i for i in range(count)},
        compiler_params=pltpu.CompilerParams(vmem_limit_bytes=12 << 20),
        cost_estimate=pl.CostEstimate(flops=0, bytes_accessed=0, transcendentals=0),
        name=name,
    )(*arrays, *waits)
    return list(results)


def shaped(*arrays):
    return [(a.shape, a.dtype) for a in arrays]


def attend_kernel(steps, mover, lengths_ref, ins, outs, scratch):
    query_hbm, keys_hbm, values_hbm, new_keys_hbm, new_values_hbm = ins
    query_ref, keys_ref, values_ref, new_keys_ref, new_values_ref, query_rows, out_rows = scratch
    tp_index, _, _, _, own_group = places()
    length = lengths_ref[0]
    own_ref, *chunk_refs = outs
    first = mover.start(query_hbm.at[0], query_ref)
    news = [mover.start(new_keys_hbm.at[0], new_keys_ref), mover.start(new_values_hbm.at[0], new_values_ref)]
    groups = [slice(g * HD, (g + 1) * HD) for g in range(KVH)]
    arrive = [
        (mover.start(keys_hbm.at[0, :, group], keys_ref.at[:, group]), mover.start(values_hbm.at[0, :, group], values_ref.at[:, group]))
        for group in groups
    ]
    width = query_ref.shape[1]
    cache_len = keys_ref.shape[0]
    rows = width // HD // KVH * steps
    mover.wait(first)
    for h in range(width // HD):
        query_rows[h * steps : (h + 1) * steps, :] = query_ref[:, h * HD : (h + 1) * HD].astype(F32)
    usable = lax.broadcasted_iota(jnp.int32, (rows, cache_len), 1) + tp_index * cache_len < length
    left = lax.broadcasted_iota(jnp.int32, (rows, HD), 1) < HD // 2
    for g in range(KVH):
        mover.wait(*arrive[g])
        query = query_rows[g * rows : (g + 1) * rows, :].astype(BF16)
        scores = over_features(query, keys_ref[:, g * HD : (g + 1) * HD]) * (1.0 / HD**0.5)
        maxima = jnp.max(jnp.where(usable, scores, NEG_FILL), axis=1, keepdims=True)
        terms = jnp.where(usable, jnp.exp(scores - maxima), 0.0)
        totals = jnp.sum(terms, axis=1, keepdims=True)
        upper = terms.astype(BF16)
        lower = (terms - upper.astype(F32)).astype(BF16)
        both = dot(jnp.concatenate([upper, lower], axis=0), values_ref[:, g * HD : (g + 1) * HD])
        out_rows[g * rows : (g + 1) * rows, :HD] = both[:rows] + both[rows:]
        out_rows[g * rows : (g + 1) * rows, HD:] = jnp.where(left, maxima, totals)
    count = chunk_refs[0].shape[1]
    for t in range(KVH * rows // count):
        for chunk_ref in chunk_refs:
            for k in range(chunk_ref.shape[0]):

                @pl.when(tp_index ^ (chunk_ref.shape[0] + k) == t)
                def _():
                    chunk_ref[k] = out_rows[t * count : (t + 1) * count, :]

        @pl.when(tp_index == t)
        def _():
            own_ref[:count, :] = out_rows[t * count : (t + 1) * count, :]
            own_ref[count : 2 * count, :HD] = query_rows[t * count : (t + 1) * count, :]

    mover.wait(*news)
    own_ref[count : 2 * count, HD:] = jnp.zeros((count, HD), F32)
    for at, ref in ((0, new_keys_ref), (HD, new_values_ref)):
        chosen = ref[:, :HD].astype(F32)
        for g in range(1, KVH):
            chosen = jnp.where(own_group == g, ref[:, groups[g]].astype(F32), chosen)
        own_ref[2 * count : 2 * count + steps, at : at + HD] = chosen


def combine_kernel(steps, sent, indices, attn_hbm, own_ref, *refs):
    *part_refs, out_hbm, rows_ref, load_ref, sems = refs
    rest = attn_hbm.shape[0] - sent
    arrive = pltpu.make_async_copy(attn_hbm.at[sent:], load_ref.at[:rest], sems.at[0])
    arrive.start()
    count = part_refs[0].shape[1]
    own = own_ref[...]
    rows_ref[...] = jnp.zeros_like(rows_ref)
    step = lax.broadcasted_iota(jnp.int32, (count, 1), 0) % steps
    query = own[count : 2 * count, :HD]
    keys, values = own[2 * count :, :HD], own[2 * count :, HD:]
    parts = [own[:count]] + [part_ref[i] for i, part_ref in zip(indices, part_refs)]
    scores = []
    for j in range(steps):
        score = jnp.sum(query * keys[j : j + 1], axis=-1, keepdims=True) * (1.0 / HD**0.5)
        scores.append(jnp.where(step >= j, score, NEG_FILL))
    maxima = [part[:, HD : HD + 1] for part in parts]
    highest = functools.reduce(jnp.maximum, scores + maxima)
    total = jnp.zeros((count, 1), F32)
    weighted = jnp.zeros((count, HD), F32)
    for part, own in zip(parts, maxima):
        scale = jnp.exp(own - highest)
        total = total + part[:, HD + HD // 2 : HD + HD // 2 + 1] * scale
        weighted = weighted + part[:, :HD] * scale
    for j in range(steps):
        term = jnp.where(step >= j, jnp.exp(scores[j] - highest), 0.0)
        total = total + term
        weighted = weighted + term * values[j : j + 1]
    attended = weighted / total
    for row in range(count):
        h, s = row // steps, row % steps
        rows_ref[s : s + 1, h * HD : (h + 1) * HD] = attended[row : row + 1]
    load_ref[rest:, :] = rows_ref[...].astype(BF16)
    arrive.wait()
    leave = pltpu.make_async_copy(load_ref, out_hbm, sems.at[1])
    leave.start()
    leave.wait()


def cut_kernel(outer, half, early, mover, ins, outs, scratch):
    grad_hbm, attn_hbm = ins
    plane = outs[0].shape[1]
    _, core, z, _, _ = places()
    rows = pl.ds(pl.multiple_of(core * half, half), half)
    for k in range(1, outer):
        columns = pl.ds(pl.multiple_of((z + k) % outer * plane, plane), plane)
        mover.start(grad_hbm.at[rows, columns], scratch[0].at[k - 1, :half])
        mover.start(attn_hbm.at[:early], scratch[0].at[k - 1, half:])
    arrive = list(mover.open)
    for k in range(1, outer):
        mover.wait(*arrive[2 * k - 2 : 2 * k])
        mover.start(scratch[0].at[k - 1], outs[k - 1])


def middle_kernel(outer, mover, ins, outs, scratch):
    grad_hbm, weight_hbm, other_hbm, *cot_hbms = ins
    sent_outs, (total_out, cot_own_out, *cot_far_outs) = outs[: outer - 1], outs[outer - 1 :]
    cots_ref, weight_ref, other_ref, sent_ref, total_ref, cot_own_ref, cot_far_ref = scratch
    _, core, z, x, _ = places()
    tokens = grad_hbm.shape[0]
    plane = cots_ref.shape[1]
    feats = weight_ref.shape[0]
    half = tokens // 2
    weights = [mover.start(weight_hbm, weight_ref), mover.start(other_hbm, other_ref)]
    blocks = [[mover.start(grad_hbm.at[:, pl.ds(pl.multiple_of(z * plane, plane), plane)], cots_ref.at[:tokens])]]
    for k in range(1, outer):
        blocks.append([])
        for hbm, side in ((cot_hbms[k - 1], core), (cot_hbms[outer + k - 2], 1 - core)):
            first = pl.multiple_of(k * tokens + side * half, half)
            blocks[k].append(mover.start(hbm.at[:half], cots_ref.at[pl.ds(first, half)]))
    mover.wait(*weights)
    span = outer * half
    for k in reversed(range(outer)):
        mover.wait(*blocks[k])
        here = slice(k * tokens, (k + 1) * tokens)
        block = cots_ref[here, :]
        low, high = block[:, :feats], block[:, feats:]
        own = jnp.where(x == 0, low, high)
        other = jnp.where(x == 0, high, low)
        total = dot(own, weight_ref[...]) + dot(other, other_ref[...])
        if k == 0:
            total_ref[...] = total
            mover.start(total_ref, total_out)
        else:
            sent_ref[k - 1] = total.astype(BF16)
            mover.start(sent_ref.at[k - 1], sent_outs[k - 1])
        cot_own_ref[here, :] = own
        cot_far_ref[here, :] = other

    size = cot_far_outs[0].shape[0]
    for i, out in enumerate(cot_far_outs):
        first = pl.multiple_of(core * span + i * size, size)
        mover.start(cot_far_ref.at[pl.ds(first, size)], out)
    mover.start(cot_own_ref, cot_own_out)


def decode_kernel(steps, mover, ins, outs, scratch):
    weight_hbm, other_hbm, *load_hbms = ins
    weight_ref, other_ref, dec_ref, rows_ref, by_row_ref, parts_ref = scratch
    _, _, z, x, _ = places()
    tokens = load_hbms[0].shape[0] - PAD
    outer, share = len(load_hbms), outs[0].shape[1]
    arrive = [mover.start(hbm, dec_ref.at[k]) for k, hbm in enumerate(load_hbms)]
    mover.wait(*arrive, mover.start(weight_hbm, weight_ref), mover.start(other_hbm, other_ref))
    for k in range(outer):
        rows_ref[k * steps : (k + 1) * steps, :] = dec_ref[k, tokens:, :].astype(F32)[:steps]
    every = rows_ref[...].astype(BF16)
    own, other = over_features(every, weight_ref[...]), over_features(every, other_ref[...])
    wide = jnp.concatenate([jnp.where(x == 0, own, other), jnp.where(x == 0, other, own)], axis=1)
    for k in range(outer):
        by_row_ref[k] = wide[k * steps : (k + 1) * steps]
    for q in range(parts_ref.shape[0]):
        for i in range(share):
            parts_ref[q, i] = by_row_ref[(z - (q * share + i)) % outer]
    mover.start(parts_ref, outs[0])


def own_kernel(mover, ins, outs, scratch):
    cots_ref, attn_ref = scratch
    mover.wait(mover.start(ins[0], cots_ref), mover.start(ins[1], attn_ref))
    outs[0][...] = over_tokens(cots_ref[...], attn_ref[...])


def product_kernel(mover, ins, outs, scratch):
    own_ref, attn_ref, *cot_refs = ins
    cots_ref, out_ref = scratch
    _, core, _, _, _ = places()
    size = cot_refs[0].shape[0]
    for i, ref in enumerate(cot_refs):
        first = pl.multiple_of((core ^ i) * size, size)
        cots_ref[pl.ds(first, size), :] = ref[...]
    pieces = 2
    step = out_ref.shape[0] // pieces
    for i in range(pieces):
        here = slice(i * step, (i + 1) * step)
        out_ref[here, :] = own_ref[here, :] + over_tokens(cots_ref[:, here], attn_ref[...])
        mover.start(out_ref.at[here], outs[0].at[here])
    outs[1][...] = jnp.zeros(outs[1].shape, F32)


def sum_kernel(outer, share, mover, ins, outs, scratch):
    total_ref, *rest = ins
    part_hbms, piece_refs = rest[: outer - 1], rest[outer - 1 :]
    parts_ref, sum_ref = scratch
    _, _, z, _, _ = places()
    plane = piece_refs[0].shape[1]
    arrive = [mover.start(hbm, parts_ref.at[i]) for i, hbm in enumerate(part_hbms)]
    for j in range(share):
        mover.start(piece_refs[j], outs[0].at[0, :, pl.ds(pl.multiple_of((z % share ^ j) * plane, plane), plane)])
    mover.wait(*arrive)
    total = total_ref[...]
    for i in range(outer - 1):
        total = total + parts_ref[i].astype(F32)
    sum_ref[...] = total.astype(BF16)
    mover.start(sum_ref, outs[1])


def pack_kernel(early, skip, mover, ins, outs, scratch):
    low_hbm, high_hbm, own_hbm, *first_hbms = ins
    cots_ref, attn_ref = scratch
    tokens, size = own_hbm.shape[0], low_hbm.shape[0]
    parts = [(low_hbm, cots_ref, outs[0], 0, size), (high_hbm, cots_ref, outs[0], size, size), (own_hbm, attn_ref, outs[1], 0, tokens)]
    parts += [(hbm.at[skip:], attn_ref, outs[1], (k + 1) * tokens, early) for k, hbm in enumerate(first_hbms)]
    arrive = [mover.start(source, ref.at[at : at + rows]) for source, ref, _, at, rows in parts]
    for copy, (_, ref, out, at, rows) in zip(arrive, parts):
        mover.wait(copy)
        mover.start(ref.at[at : at + rows], out.at[at : at + rows])


def gate_kernel(count, early, *refs):
    refs, pack_out, (last_ref, in_sems, out_sems) = refs[count + 2 : -4 - count], refs[-4], refs[-3:]
    rest = refs[0].shape[0] - PAD
    tokens = rest + early
    arrive, leave = [], []
    for k, ref in enumerate(refs):
        arrive.append(pltpu.make_async_copy(ref.at[:rest], last_ref.at[k], in_sems.at[k]))
        target = pack_out.at[(k + 1) * tokens + early : (k + 2) * tokens]
        leave.append(pltpu.make_async_copy(last_ref.at[k], target, out_sems.at[k]))
    for copy in arrive:
        copy.start()
    for copy, follow in zip(arrive, leave):
        copy.wait()
        follow.start()
    for copy in leave:
        copy.wait()


def shards(dec_query, new_keys, new_values, cache_keys, cache_values, lengths, out_weight, train_attn, grad_out):
    rows, steps, width = dec_query.shape
    assert rows == 1
    fsdp_size = lax.axis_size("fsdp")
    tp_size = lax.axis_size("tp")
    outer = fsdp_size // INNER
    share = outer // tp_size
    fsdp_index = lax.axis_index("fsdp")
    tp_index = lax.axis_index("tp")
    z, x = fsdp_index // INNER, fsdp_index % INNER
    tokens = grad_out.shape[0]
    feats, cols = out_weight.shape
    plane = feats * INNER
    slot = tp_index % 4
    heads = width // HD
    count = heads // tp_size * steps
    far = range(1, outer)
    others = range(1, tp_size)

    other_weight = flip(out_weight, "fsdp", 1, "weight_x")

    half = tokens // 2

    early = tokens // 8
    cot_rows = half * plane // cols
    if plane == cols:
        cuts = call(
            functools.partial(cut_kernel, outer, half, early),
            "cut",
            [grad_out, train_attn],
            [((half + early, cols), BF16)] * len(far),
            [((len(far), half + early, cols), BF16)],
            room=63,
        )
    else:
        first = tp_index % 2 * half
        cuts = [
            jnp.concatenate(
                [
                    lax.dynamic_slice(grad_out, (first, (z + k) % outer * plane), (half, plane)).reshape(cot_rows, cols),
                    train_attn[:early],
                ]
            )
            for k in far
        ]
    firsts = [turn(cuts[k - 1], k, f"first_z{k}") for k in far]
    got = firsts if plane == cols else [a[:cot_rows].reshape(half, plane) for a in firsts]

    sizes = [1 << b for b in range(tp_size.bit_length() - 1)]
    own, *chunks = call(
        functools.partial(attend_kernel, steps),
        "attend",
        [dec_query, cache_keys, cache_values, new_keys, new_values],
        [((2 * count + 8, 2 * HD), F32)]
        + [((size, count, 2 * HD), F32) for size in sizes],
        shaped(dec_query[0], cache_keys[0], cache_values[0], new_keys[0], new_values[0])
        + [((heads * steps, HD), F32), ((heads * steps, 2 * HD), F32)],
        scalars=lengths,
        room=63,
        fast=range(1 + len(sizes)),
    )
    own = pl.pallas_call(
        lambda in_ref, out_ref: out_ref.__setitem__(..., in_ref[...]),
        out_shape=jax.ShapeDtypeStruct(own.shape, own.dtype),
        in_specs=[pl.BlockSpec(memory_space=pltpu.VMEM)],
        out_specs=pl.BlockSpec(memory_space=pltpu.VMEM),
        compiler_params=pltpu.CompilerParams(vmem_limit_bytes=12 << 20),
        cost_estimate=pl.CostEstimate(flops=0, bytes_accessed=0, transcendentals=0),
        name="hold",
    )(own)
    parts, indices, held = [], [], []
    for size, chunk in reversed(list(zip(sizes, chunks))):
        if size > 1:
            came = [flip(a, "tp", size, f"softmax_tp{size}") for a in [chunk] + [a[size:] for a in held]]
            held = [a[:size] for a in held] + came
        else:
            parts += held + [flip(a, "tp", size, f"softmax_tp{size}") for a in [chunk] + held]
            indices += [0] * len(held) + [0] + [1] * len(held)
    last = pl.pallas_call(
        functools.partial(combine_kernel, steps, early, indices),
        out_shape=jax.ShapeDtypeStruct((tokens - early + PAD, cols), BF16),
        in_specs=[pl.BlockSpec(memory_space=pltpu.HBM)] + [pl.BlockSpec(memory_space=pltpu.VMEM)] * (len(parts) + 1),
        out_specs=pl.BlockSpec(memory_space=pltpu.HBM),
        scratch_shapes=[
            pltpu.VMEM((PAD, cols), F32),
            pltpu.VMEM((tokens - early + PAD, cols), BF16),
            pltpu.SemaphoreType.DMA((2,)),
        ],
        compiler_params=pltpu.CompilerParams(vmem_limit_bytes=12 << 20),
        cost_estimate=pl.CostEstimate(flops=0, bytes_accessed=0, transcendentals=0),
        name="combine",
    )(train_attn, own, *parts)

    lasts = [last] + [turn(last, k, f"last_z{k}") for k in far]

    got = kept(got, [last], "kept")
    twins = [flip(a, "tp", 1, "cot_core") for a in got]

    *sent, total, cot_own, cot_low, cot_high = call(
        functools.partial(middle_kernel, outer),
        "middle",
        [grad_out, out_weight, other_weight, *got, *twins],
        [((tokens, cols), BF16)] * len(far)
        + [((tokens, cols), F32), ((outer * tokens, feats), BF16)] + [((outer * half // 2, feats), BF16)] * 2,
        [
            ((outer * tokens, plane), BF16),
            ((feats, cols), BF16),
            ((feats, cols), BF16),
            ((len(far), tokens, cols), BF16),
            ((tokens, cols), F32),
            ((outer * tokens, feats), BF16),
            ((outer * tokens, feats), BF16),
        ],
        room=63,
    )
    cots_x = [flip(a, "fsdp", 1, "cot_x") for a in (cot_low, cot_high)]

    cots_x, pack = call(
        functools.partial(pack_kernel, early, cot_rows),
        "pack",
        [*cots_x, train_attn, *(got if plane == cols else firsts)],
        [((outer * half, feats), BF16), ((outer * tokens, cols), BF16)],
        [((outer * half, feats), BF16), ((outer * tokens, cols), BF16)],
        room=63,
    )

    results = pl.pallas_call(
        functools.partial(gate_kernel, len(sent), early),
        out_shape=[jax.ShapeDtypeStruct(a.shape, a.dtype) for a in [*sent, pack]],
        in_specs=[pl.BlockSpec(memory_space=pltpu.HBM)] * (len(sent) + 2 + len(far)),
        out_specs=[pl.BlockSpec(memory_space=pltpu.HBM)] * (len(sent) + 1),
        scratch_shapes=[
            pltpu.VMEM((len(far), tokens - early, cols), BF16),
            pltpu.SemaphoreType.DMA((len(far),)),
            pltpu.SemaphoreType.DMA((len(far),)),
        ],
        input_output_aliases={i: i for i in range(len(sent) + 1)},
        compiler_params=pltpu.CompilerParams(vmem_limit_bytes=63 << 20),
        cost_estimate=pl.CostEstimate(flops=0, bytes_accessed=0, transcendentals=0),
        name="gate",
    )(*sent, pack, cots_x, *lasts[1:])
    sent, pack = results[:-1], results[-1]
    sums = [turn(sent[k - 1], outer - k, f"sum_z{k}") for k in far]
    pack_x = flip(pack, "fsdp", 1, "attn_x")
    twin_x = flip(cots_x, "tp", 1, "cot_x_core")

    (dec,) = call(
        functools.partial(decode_kernel, steps),
        "decode",
        [out_weight, other_weight, *lasts],
        [((tp_size, share, steps, plane), F32)],
        [
            ((feats, cols), BF16),
            ((feats, cols), BF16),
            ((outer, tokens - early + PAD, cols), BF16),
            ((outer * steps, cols), F32),
            ((outer, steps, plane), F32),
            ((tp_size, share, steps, plane), F32),
        ],
        waits=[pack],
        room=63,
    )
    with jax.named_scope("dec_tp"):
        dec = lax.all_to_all(dec, "tp", 0, 0, tiled=True).sum(axis=0).astype(BF16)
    pieces = []
    for j in range(share):
        perm = [
            ((a * INNER + b) * tp_size + q, ((q * share + (a % share ^ j)) * INNER + b) * tp_size + a // share)
            for a in range(outer)
            for b in range(INNER)
            for q in range(tp_size)
        ]
        with jax.named_scope("dec_place"):
            pieces.append(lax.ppermute(lax.dynamic_index_in_dim(dec, z % share ^ j, 0, False), ("fsdp", "tp"), perm))
    (own_total,) = call(
        own_kernel,
        "own",
        [cot_own, pack],
        [((feats, cols), F32)],
        [((outer * tokens, feats), BF16), ((outer * tokens, cols), BF16)],
        waits=[twin_x],
        fast=[0],
    )
    grad_weight, mark = call(
        product_kernel,
        "product",
        [own_total, pack_x, cots_x, twin_x],
        [((feats, cols), F32), ((8, HD), F32)],
        [((outer * tokens, feats), BF16), ((feats, cols), F32)],
        near=range(4),
        fast=[1],
    )
    operands = [total, *sums, *pieces]
    dec_out, grad_attn = call(
        functools.partial(sum_kernel, outer, share),
        "sum",
        operands,
        [((rows, steps, share * plane), BF16), ((tokens, cols), BF16)],
        [((len(far), tokens, cols), BF16), ((tokens, cols), BF16)],
        waits=[mark],
        near=[0, *range(outer, len(operands))],
    )
    return dec_out, grad_attn, grad_weight


def solution(mesh):
    return jax.shard_map(
        shards,
        mesh=mesh,
        in_specs=(
            P("fsdp", None, None),
            P("fsdp", None, None),
            P("fsdp", None, None),
            P("fsdp", "tp", None),
            P("fsdp", "tp", None),
            P("fsdp"),
            P("fsdp", "tp"),
            P("fsdp", "tp"),
            P("fsdp", None),
        ),
        out_specs=(P("fsdp", None, "tp"), P("fsdp", "tp"), P("fsdp", "tp")),
        check_vma=False,
    )
```

```python
import functools

import jax
import jax.numpy as jnp
from jax import lax
from jax.experimental import pallas as pl
from jax.experimental.pallas import tpu as pltpu
from jax.sharding import PartitionSpec as P

KVH = 4
HD = 128
NEG_FILL = -1e30
INNER = 2
PAD = 8
BF16 = jnp.bfloat16
F32 = jnp.float32


def flip(a, axis, bits, name):
    size = lax.axis_size(axis)
    with jax.named_scope(name):
        return lax.ppermute(a, axis, [(i, i ^ bits) for i in range(size)])


def turn(a, steps, name):
    outer = lax.axis_size("fsdp") // INNER
    with jax.named_scope(name):
        return lax.ppermute(
            a, "fsdp", [(z * INNER + x, (z + steps) % outer * INNER + x) for z in range(outer) for x in range(INNER)]
        )


def dot(a, b):
    return jnp.dot(a, b, preferred_element_type=F32)


def over_features(a, b):
    return lax.dot_general(a, b, (((1,), (1,)), ((), ())), preferred_element_type=F32)


def over_tokens(a, b):
    return lax.dot_general(a, b, (((0,), (0,)), ((), ())), preferred_element_type=F32)


class Mover:
    def __init__(self, sems):
        self.sems, self.count, self.open = sems, 0, []

    def start(self, source, target):
        copy = pltpu.make_async_copy(source, target, self.sems.at[self.count])
        self.count += 1
        self.open.append(copy)
        copy.start()
        return copy

    def wait(self, *copies):
        for copy in copies:
            copy.wait()
            self.open = [other for other in self.open if other is not copy]

    def finish(self):
        self.wait(*list(self.open))


def places():
    fsdp_index, tp_index = lax.axis_index("fsdp"), lax.axis_index("tp")
    return tp_index, tp_index % 2, fsdp_index // INNER, fsdp_index % INNER, tp_index * KVH // lax.axis_size("tp")


def call(kernel, name, operands, out_shapes, scratch, waits=(), scalars=None, room=12, fast=(), near=()):
    copies = 4 * (len(operands) + len(out_shapes))
    scalars = [] if scalars is None else [scalars]

    def body(*refs):
        front, refs = refs[: len(scalars)], refs[len(scalars) :]
        ins, refs = refs[: len(operands)], refs[len(operands) + len(waits) :]
        outs, refs = refs[: len(out_shapes)], refs[len(out_shapes) :]
        mover = Mover(refs[-1])
        kernel(mover, *front, ins, outs, refs[:-1])
        mover.finish()

    results = pl.pallas_call(
        body,
        out_shape=[jax.ShapeDtypeStruct(shape, dtype) for shape, dtype in out_shapes],
        in_specs=[pl.BlockSpec(memory_space=pltpu.SMEM)] * len(scalars)
        + [pl.BlockSpec(memory_space=pltpu.VMEM if i in near else pltpu.HBM) for i in range(len(operands))]
        + [pl.BlockSpec(memory_space=pltpu.HBM)] * len(waits),
        out_specs=[
            pl.BlockSpec(memory_space=pltpu.VMEM if i in fast else pltpu.HBM) for i in range(len(out_shapes))
        ],
        scratch_shapes=[pltpu.VMEM(shape, dtype) for shape, dtype in scratch] + [pltpu.SemaphoreType.DMA((copies,))],
        compiler_params=pltpu.CompilerParams(vmem_limit_bytes=room << 20),
        cost_estimate=pl.CostEstimate(flops=0, bytes_accessed=0, transcendentals=0),
        name=name,
    )(*scalars, *operands, *waits)
    return list(results)


def kept(arrays, waits, name):
    count = len(arrays)
    results = pl.pallas_call(
        lambda *refs: None,
        out_shape=[jax.ShapeDtypeStruct(a.shape, a.dtype) for a in arrays],
        in_specs=[pl.BlockSpec(memory_space=pltpu.HBM)] * (count + len(waits)),
        out_specs=[pl.BlockSpec(memory_space=pltpu.HBM)] * count,
        input_output_aliases={i: i for i in range(count)},
        compiler_params=pltpu.CompilerParams(vmem_limit_bytes=12 << 20),
        cost_estimate=pl.CostEstimate(flops=0, bytes_accessed=0, transcendentals=0),
        name=name,
    )(*arrays, *waits)
    return list(results)


def shaped(*arrays):
    return [(a.shape, a.dtype) for a in arrays]


def attend_kernel(steps, mover, lengths_ref, ins, outs, scratch):
    query_hbm, keys_hbm, values_hbm, new_keys_hbm, new_values_hbm = ins
    query_ref, keys_ref, values_ref, new_keys_ref, new_values_ref, query_rows, out_rows = scratch
    tp_index, _, _, _, own_group = places()
    length = lengths_ref[0]
    own_ref, *chunk_refs = outs
    first = mover.start(query_hbm.at[0], query_ref)
    news = [mover.start(new_keys_hbm.at[0], new_keys_ref), mover.start(new_values_hbm.at[0], new_values_ref)]
    groups = [slice(g * HD, (g + 1) * HD) for g in range(KVH)]
    arrive = [
        (mover.start(keys_hbm.at[0, :, group], keys_ref.at[:, group]), mover.start(values_hbm.at[0, :, group], values_ref.at[:, group]))
        for group in groups
    ]
    width = query_ref.shape[1]
    cache_len = keys_ref.shape[0]
    rows = width // HD // KVH * steps
    mover.wait(first)
    for h in range(width // HD):
        query_rows[h * steps : (h + 1) * steps, :] = query_ref[:, h * HD : (h + 1) * HD].astype(F32)
    usable = lax.broadcasted_iota(jnp.int32, (rows, cache_len), 1) + tp_index * cache_len < length
    left = lax.broadcasted_iota(jnp.int32, (rows, HD), 1) < HD // 2
    for g in range(KVH):
        mover.wait(*arrive[g])
        query = query_rows[g * rows : (g + 1) * rows, :].astype(BF16)
        scores = over_features(query, keys_ref[:, g * HD : (g + 1) * HD]) * (1.0 / HD**0.5)
        maxima = jnp.max(jnp.where(usable, scores, NEG_FILL), axis=1, keepdims=True)
        terms = jnp.where(usable, jnp.exp(scores - maxima), 0.0)
        totals = jnp.sum(terms, axis=1, keepdims=True)
        upper = terms.astype(BF16)
        lower = (terms - upper.astype(F32)).astype(BF16)
        both = dot(jnp.concatenate([upper, lower], axis=0), values_ref[:, g * HD : (g + 1) * HD])
        out_rows[g * rows : (g + 1) * rows, :HD] = both[:rows] + both[rows:]
        out_rows[g * rows : (g + 1) * rows, HD:] = jnp.where(left, maxima, totals)
    count = chunk_refs[0].shape[1]
    for t in range(KVH * rows // count):
        for chunk_ref in chunk_refs:
            for k in range(chunk_ref.shape[0]):

                @pl.when(tp_index ^ (chunk_ref.shape[0] + k) == t)
                def _():
                    chunk_ref[k] = out_rows[t * count : (t + 1) * count, :]

        @pl.when(tp_index == t)
        def _():
            own_ref[:count, :] = out_rows[t * count : (t + 1) * count, :]
            own_ref[count : 2 * count, :HD] = query_rows[t * count : (t + 1) * count, :]

    mover.wait(*news)
    own_ref[count : 2 * count, HD:] = jnp.zeros((count, HD), F32)
    for at, ref in ((0, new_keys_ref), (HD, new_values_ref)):
        chosen = ref[:, :HD].astype(F32)
        for g in range(1, KVH):
            chosen = jnp.where(own_group == g, ref[:, groups[g]].astype(F32), chosen)
        own_ref[2 * count : 2 * count + steps, at : at + HD] = chosen


def combine_kernel(steps, sent, indices, attn_hbm, own_ref, *refs):
    *part_refs, out_hbm, rows_ref, load_ref, sems = refs
    rest = attn_hbm.shape[0] - sent
    arrive = pltpu.make_async_copy(attn_hbm.at[sent:], load_ref.at[:rest], sems.at[0])
    arrive.start()
    count = part_refs[0].shape[1]
    own = own_ref[...]
    rows_ref[...] = jnp.zeros_like(rows_ref)
    step = lax.broadcasted_iota(jnp.int32, (count, 1), 0) % steps
    query = own[count : 2 * count, :HD]
    keys, values = own[2 * count :, :HD], own[2 * count :, HD:]
    parts = [own[:count]] + [part_ref[i] for i, part_ref in zip(indices, part_refs)]
    scores = []
    for j in range(steps):
        score = jnp.sum(query * keys[j : j + 1], axis=-1, keepdims=True) * (1.0 / HD**0.5)
        scores.append(jnp.where(step >= j, score, NEG_FILL))
    maxima = [part[:, HD : HD + 1] for part in parts]
    highest = functools.reduce(jnp.maximum, scores + maxima)
    total = jnp.zeros((count, 1), F32)
    weighted = jnp.zeros((count, HD), F32)
    for part, own in zip(parts, maxima):
        scale = jnp.exp(own - highest)
        total = total + part[:, HD + HD // 2 : HD + HD // 2 + 1] * scale
        weighted = weighted + part[:, :HD] * scale
    for j in range(steps):
        term = jnp.where(step >= j, jnp.exp(scores[j] - highest), 0.0)
        total = total + term
        weighted = weighted + term * values[j : j + 1]
    attended = weighted / total
    for row in range(count):
        h, s = row // steps, row % steps
        rows_ref[s : s + 1, h * HD : (h + 1) * HD] = attended[row : row + 1]
    load_ref[rest:, :] = rows_ref[...].astype(BF16)
    arrive.wait()
    leave = pltpu.make_async_copy(load_ref, out_hbm, sems.at[1])
    leave.start()
    leave.wait()


def cut_kernel(outer, half, early, mover, ins, outs, scratch):
    grad_hbm, attn_hbm = ins
    plane = outs[0].shape[1]
    _, core, z, _, _ = places()
    rows = pl.ds(pl.multiple_of(core * half, half), half)
    for k in range(1, outer):
        columns = pl.ds(pl.multiple_of((z + k) % outer * plane, plane), plane)
        mover.start(grad_hbm.at[rows, columns], scratch[0].at[k - 1, :half])
        mover.start(attn_hbm.at[:early], scratch[0].at[k - 1, half:])
    arrive = list(mover.open)
    for k in range(1, outer):
        mover.wait(*arrive[2 * k - 2 : 2 * k])
        mover.start(scratch[0].at[k - 1], outs[k - 1])


def middle_kernel(outer, mover, ins, outs, scratch):
    grad_hbm, weight_hbm, other_hbm, *cot_hbms = ins
    sent_outs, (total_out, cot_own_out, *cot_far_outs) = outs[: outer - 1], outs[outer - 1 :]
    cots_ref, weight_ref, other_ref, sent_ref, total_ref, cot_own_ref, cot_far_ref = scratch
    _, core, z, x, _ = places()
    tokens = grad_hbm.shape[0]
    plane = cots_ref.shape[1]
    feats = weight_ref.shape[0]
    half = tokens // 2
    weights = [mover.start(weight_hbm, weight_ref), mover.start(other_hbm, other_ref)]
    blocks = [[mover.start(grad_hbm.at[:, pl.ds(pl.multiple_of(z * plane, plane), plane)], cots_ref.at[:tokens])]]
    for k in range(1, outer):
        blocks.append([])
        for hbm, side in ((cot_hbms[k - 1], core), (cot_hbms[outer + k - 2], 1 - core)):
            first = pl.multiple_of(k * tokens + side * half, half)
            blocks[k].append(mover.start(hbm.at[:half], cots_ref.at[pl.ds(first, half)]))
    mover.wait(*weights)
    span = outer * half
    for k in reversed(range(outer)):
        mover.wait(*blocks[k])
        here = slice(k * tokens, (k + 1) * tokens)
        block = cots_ref[here, :]
        low, high = block[:, :feats], block[:, feats:]
        own = jnp.where(x == 0, low, high)
        other = jnp.where(x == 0, high, low)
        total = dot(own, weight_ref[...]) + dot(other, other_ref[...])
        if k == 0:
            total_ref[...] = total
            mover.start(total_ref, total_out)
        else:
            sent_ref[k - 1] = total.astype(BF16)
            mover.start(sent_ref.at[k - 1], sent_outs[k - 1])
        cot_own_ref[here, :] = own
        cot_far_ref[here, :] = other

    size = cot_far_outs[0].shape[0]
    for i, out in enumerate(cot_far_outs):
        first = pl.multiple_of(core * span + i * size, size)
        mover.start(cot_far_ref.at[pl.ds(first, size)], out)
    mover.start(cot_own_ref, cot_own_out)


def decode_kernel(steps, mover, ins, outs, scratch):
    weight_hbm, other_hbm, *load_hbms = ins
    weight_ref, other_ref, dec_ref, rows_ref, by_row_ref, parts_ref = scratch
    _, _, z, x, _ = places()
    tokens = load_hbms[0].shape[0] - PAD
    outer, share = len(load_hbms), outs[0].shape[1]
    arrive = [mover.start(hbm, dec_ref.at[k]) for k, hbm in enumerate(load_hbms)]
    mover.wait(*arrive, mover.start(weight_hbm, weight_ref), mover.start(other_hbm, other_ref))
    for k in range(outer):
        rows_ref[k * steps : (k + 1) * steps, :] = dec_ref[k, tokens:, :].astype(F32)[:steps]
    every = rows_ref[...].astype(BF16)
    own, other = over_features(every, weight_ref[...]), over_features(every, other_ref[...])
    wide = jnp.concatenate([jnp.where(x == 0, own, other), jnp.where(x == 0, other, own)], axis=1)
    for k in range(outer):
        by_row_ref[k] = wide[k * steps : (k + 1) * steps]
    for q in range(parts_ref.shape[0]):
        for i in range(share):
            parts_ref[q, i] = by_row_ref[(z - (q * share + i)) % outer]
    mover.start(parts_ref, outs[0])


def own_kernel(mover, ins, outs, scratch):
    cots_ref, attn_ref = scratch
    mover.wait(mover.start(ins[0], cots_ref), mover.start(ins[1], attn_ref))
    outs[0][...] = over_tokens(cots_ref[...], attn_ref[...])


def product_kernel(mover, ins, outs, scratch):
    own_ref, attn_ref, *cot_refs = ins
    cots_ref, out_ref = scratch
    _, core, _, _, _ = places()
    size = cot_refs[0].shape[0]
    for i, ref in enumerate(cot_refs):
        first = pl.multiple_of((core ^ i) * size, size)
        cots_ref[pl.ds(first, size), :] = ref[...]
    pieces = 2
    step = out_ref.shape[0] // pieces
    for i in range(pieces):
        here = slice(i * step, (i + 1) * step)
        out_ref[here, :] = own_ref[here, :] + over_tokens(cots_ref[:, here], attn_ref[...])
        mover.start(out_ref.at[here], outs[0].at[here])
    outs[1][...] = jnp.zeros(outs[1].shape, F32)


def sum_kernel(outer, share, mover, ins, outs, scratch):
    total_ref, *rest = ins
    part_hbms, piece_refs = rest[: outer - 1], rest[outer - 1 :]
    parts_ref, sum_ref = scratch
    _, _, z, _, _ = places()
    plane = piece_refs[0].shape[1]
    arrive = [mover.start(hbm, parts_ref.at[i]) for i, hbm in enumerate(part_hbms)]
    for j in range(share):
        mover.start(piece_refs[j], outs[0].at[0, :, pl.ds(pl.multiple_of((z % share ^ j) * plane, plane), plane)])
    mover.wait(*arrive)
    total = total_ref[...]
    for i in range(outer - 1):
        total = total + parts_ref[i].astype(F32)
    sum_ref[...] = total.astype(BF16)
    mover.start(sum_ref, outs[1])


def pack_kernel(early, skip, mover, ins, outs, scratch):
    low_hbm, high_hbm, own_hbm, *first_hbms = ins
    cots_ref, attn_ref = scratch
    tokens, size = own_hbm.shape[0], low_hbm.shape[0]
    parts = [(low_hbm, cots_ref, outs[0], 0, size), (high_hbm, cots_ref, outs[0], size, size), (own_hbm, attn_ref, outs[1], 0, tokens)]
    parts += [(hbm.at[skip:], attn_ref, outs[1], (k + 1) * tokens, early) for k, hbm in enumerate(first_hbms)]
    arrive = [mover.start(source, ref.at[at : at + rows]) for source, ref, _, at, rows in parts]
    for copy, (_, ref, out, at, rows) in zip(arrive, parts):
        mover.wait(copy)
        mover.start(ref.at[at : at + rows], out.at[at : at + rows])


def gate_kernel(count, early, *refs):
    refs, pack_out, (last_ref, in_sems, out_sems) = refs[count + 2 : -4 - count], refs[-4], refs[-3:]
    rest = refs[0].shape[0] - PAD
    tokens = rest + early
    arrive, leave = [], []
    for k, ref in enumerate(refs[::-1]):
        arrive.append(pltpu.make_async_copy(ref.at[:rest], last_ref.at[k], in_sems.at[k]))
        target = pack_out.at[(k + 1) * tokens + early : (k + 2) * tokens]
        leave.append(pltpu.make_async_copy(last_ref.at[k], target, out_sems.at[k]))
    for copy in arrive:
        copy.start()
    for copy, follow in zip(arrive, leave):
        copy.wait()
        follow.start()
    for copy in leave:
        copy.wait()


def shards(dec_query, new_keys, new_values, cache_keys, cache_values, lengths, out_weight, train_attn, grad_out):
    rows, steps, width = dec_query.shape
    assert rows == 1
    fsdp_size = lax.axis_size("fsdp")
    tp_size = lax.axis_size("tp")
    outer = fsdp_size // INNER
    share = outer // tp_size
    fsdp_index = lax.axis_index("fsdp")
    tp_index = lax.axis_index("tp")
    z, x = fsdp_index // INNER, fsdp_index % INNER
    tokens = grad_out.shape[0]
    feats, cols = out_weight.shape
    plane = feats * INNER
    slot = tp_index % 4
    heads = width // HD
    count = heads // tp_size * steps
    far = range(1, outer)
    others = range(1, tp_size)

    other_weight = flip(out_weight, "fsdp", 1, "weight_x")

    half = tokens // 2

    early = tokens // 8
    cot_rows = half * plane // cols
    if plane == cols:
        cuts = call(
            functools.partial(cut_kernel, outer, half, early),
            "cut",
            [grad_out, train_attn],
            [((half + early, cols), BF16)] * len(far),
            [((len(far), half + early, cols), BF16)],
            room=63,
        )
    else:
        first = tp_index % 2 * half
        cuts = [
            jnp.concatenate(
                [
                    lax.dynamic_slice(grad_out, (first, (z + k) % outer * plane), (half, plane)).reshape(cot_rows, cols),
                    train_attn[:early],
                ]
            )
            for k in far
        ]
    firsts = [turn(cuts[k - 1], k, f"first_z{k}") for k in far]
    got = firsts if plane == cols else [a[:cot_rows].reshape(half, plane) for a in firsts]

    sizes = [1 << b for b in range(tp_size.bit_length() - 1)]
    own, *chunks = call(
        functools.partial(attend_kernel, steps),
        "attend",
        [dec_query, cache_keys, cache_values, new_keys, new_values],
        [((2 * count + 8, 2 * HD), F32)]
        + [((size, count, 2 * HD), F32) for size in sizes],
        shaped(dec_query[0], cache_keys[0], cache_values[0], new_keys[0], new_values[0])
        + [((heads * steps, HD), F32), ((heads * steps, 2 * HD), F32)],
        scalars=lengths,
        room=63,
        fast=range(1 + len(sizes)),
    )
    own = pl.pallas_call(
        lambda in_ref, out_ref: out_ref.__setitem__(..., in_ref[...]),
        out_shape=jax.ShapeDtypeStruct(own.shape, own.dtype),
        in_specs=[pl.BlockSpec(memory_space=pltpu.VMEM)],
        out_specs=pl.BlockSpec(memory_space=pltpu.VMEM),
        compiler_params=pltpu.CompilerParams(vmem_limit_bytes=12 << 20),
        cost_estimate=pl.CostEstimate(flops=0, bytes_accessed=0, transcendentals=0),
        name="hold",
    )(own)
    parts, indices, held = [], [], []
    for size, chunk in reversed(list(zip(sizes, chunks))):
        if size > 1:
            came = [flip(a, "tp", size, f"softmax_tp{size}") for a in [chunk] + [a[size:] for a in held]]
            held = [a[:size] for a in held] + came
        else:
            parts += held + [flip(a, "tp", size, f"softmax_tp{size}") for a in [chunk] + held]
            indices += [0] * len(held) + [0] + [1] * len(held)
    last = pl.pallas_call(
        functools.partial(combine_kernel, steps, early, indices),
        out_shape=jax.ShapeDtypeStruct((tokens - early + PAD, cols), BF16),
        in_specs=[pl.BlockSpec(memory_space=pltpu.HBM)] + [pl.BlockSpec(memory_space=pltpu.VMEM)] * (len(parts) + 1),
        out_specs=pl.BlockSpec(memory_space=pltpu.HBM),
        scratch_shapes=[
            pltpu.VMEM((PAD, cols), F32),
            pltpu.VMEM((tokens - early + PAD, cols), BF16),
            pltpu.SemaphoreType.DMA((2,)),
        ],
        compiler_params=pltpu.CompilerParams(vmem_limit_bytes=12 << 20),
        cost_estimate=pl.CostEstimate(flops=0, bytes_accessed=0, transcendentals=0),
        name="combine",
    )(train_attn, own, *parts)

    lasts = [last] + [turn(last, k, f"last_z{k}") for k in far]

    got = kept(got, [last], "kept")
    twins = [flip(a, "tp", 1, "cot_core") for a in got]

    *sent, total, cot_own, cot_low, cot_high = call(
        functools.partial(middle_kernel, outer),
        "middle",
        [grad_out, out_weight, other_weight, *got, *twins],
        [((tokens, cols), BF16)] * len(far)
        + [((tokens, cols), F32), ((outer * tokens, feats), BF16)] + [((outer * half // 2, feats), BF16)] * 2,
        [
            ((outer * tokens, plane), BF16),
            ((feats, cols), BF16),
            ((feats, cols), BF16),
            ((len(far), tokens, cols), BF16),
            ((tokens, cols), F32),
            ((outer * tokens, feats), BF16),
            ((outer * tokens, feats), BF16),
        ],
        room=63,
    )
    cots_x = [flip(a, "fsdp", 1, "cot_x") for a in (cot_low, cot_high)]

    cots_x, pack = call(
        functools.partial(pack_kernel, early, cot_rows),
        "pack",
        [*cots_x, train_attn, *(got if plane == cols else firsts)],
        [((outer * half, feats), BF16), ((outer * tokens, cols), BF16)],
        [((outer * half, feats), BF16), ((outer * tokens, cols), BF16)],
        room=63,
    )

    results = pl.pallas_call(
        functools.partial(gate_kernel, len(sent), early),
        out_shape=[jax.ShapeDtypeStruct(a.shape, a.dtype) for a in [*sent, pack]],
        in_specs=[pl.BlockSpec(memory_space=pltpu.HBM)] * (len(sent) + 2 + len(far)),
        out_specs=[pl.BlockSpec(memory_space=pltpu.HBM)] * (len(sent) + 1),
        scratch_shapes=[
            pltpu.VMEM((len(far), tokens - early, cols), BF16),
            pltpu.SemaphoreType.DMA((len(far),)),
            pltpu.SemaphoreType.DMA((len(far),)),
        ],
        input_output_aliases={i: i for i in range(len(sent) + 1)},
        compiler_params=pltpu.CompilerParams(vmem_limit_bytes=63 << 20),
        cost_estimate=pl.CostEstimate(flops=0, bytes_accessed=0, transcendentals=0),
        name="gate",
    )(*sent, pack, cots_x, *lasts[:0:-1])
    sent, pack = results[:-1], results[-1]
    sums = [turn(sent[k - 1], outer - k, f"sum_z{k}") for k in far]
    pack_x = flip(pack, "fsdp", 1, "attn_x")
    twin_x = flip(cots_x, "tp", 1, "cot_x_core")

    (dec,) = call(
        functools.partial(decode_kernel, steps),
        "decode",
        [out_weight, other_weight, *lasts],
        [((tp_size, share, steps, plane), F32)],
        [
            ((feats, cols), BF16),
            ((feats, cols), BF16),
            ((outer, tokens - early + PAD, cols), BF16),
            ((outer * steps, cols), F32),
            ((outer, steps, plane), F32),
            ((tp_size, share, steps, plane), F32),
        ],
        waits=[pack],
        room=12,
    )
    with jax.named_scope("dec_tp"):
        dec = lax.all_to_all(dec, "tp", 0, 0, tiled=True).sum(axis=0).astype(BF16)
    pieces = []
    for j in range(share):
        perm = [
            ((a * INNER + b) * tp_size + q, ((q * share + (a % share ^ j)) * INNER + b) * tp_size + a // share)
            for a in range(outer)
            for b in range(INNER)
            for q in range(tp_size)
        ]
        with jax.named_scope("dec_place"):
            pieces.append(lax.ppermute(lax.dynamic_index_in_dim(dec, z % share ^ j, 0, False), ("fsdp", "tp"), perm))
    (own_total,) = call(
        own_kernel,
        "own",
        [cot_own, pack],
        [((feats, cols), F32)],
        [((outer * tokens, feats), BF16), ((outer * tokens, cols), BF16)],
        waits=[twin_x],
        fast=[0],
    )
    grad_weight, mark = call(
        product_kernel,
        "product",
        [own_total, pack_x, cots_x, twin_x],
        [((feats, cols), F32), ((8, HD), F32)],
        [((outer * tokens, feats), BF16), ((feats, cols), F32)],
        near=range(4),
        fast=[1],
    )
    operands = [total, *sums[::-1], *pieces]
    dec_out, grad_attn = call(
        functools.partial(sum_kernel, outer, share),
        "sum",
        operands,
        [((rows, steps, share * plane), BF16), ((tokens, cols), BF16)],
        [((len(far), tokens, cols), BF16), ((tokens, cols), BF16)],
        waits=[mark],
        near=[0, *range(outer, len(operands))],
    )
    return dec_out, grad_attn, grad_weight


def solution(mesh):
    return jax.shard_map(
        shards,
        mesh=mesh,
        in_specs=(
            P("fsdp", None, None),
            P("fsdp", None, None),
            P("fsdp", None, None),
            P("fsdp", "tp", None),
            P("fsdp", "tp", None),
            P("fsdp"),
            P("fsdp", "tp"),
            P("fsdp", "tp"),
            P("fsdp", None),
        ),
        out_specs=(P("fsdp", None, "tp"), P("fsdp", "tp"), P("fsdp", "tp")),
        check_vma=False,
    )
```

```python
import functools

import jax
import jax.numpy as jnp
from jax import lax
from jax.experimental import pallas as pl
from jax.experimental.pallas import tpu as pltpu
from jax.sharding import PartitionSpec as P

KVH = 4
HD = 128
NEG_FILL = -1e30
INNER = 2
PAD = 8
BF16 = jnp.bfloat16
F32 = jnp.float32


def flip(a, axis, bits, name):
    size = lax.axis_size(axis)
    with jax.named_scope(name):
        return lax.ppermute(a, axis, [(i, i ^ bits) for i in range(size)])


def turn(a, steps, name):
    outer = lax.axis_size("fsdp") // INNER
    with jax.named_scope(name):
        return lax.ppermute(
            a, "fsdp", [(z * INNER + x, (z + steps) % outer * INNER + x) for z in range(outer) for x in range(INNER)]
        )


def dot(a, b):
    return jnp.dot(a, b, preferred_element_type=F32)


def over_features(a, b):
    return lax.dot_general(a, b, (((1,), (1,)), ((), ())), preferred_element_type=F32)


def over_tokens(a, b):
    return lax.dot_general(a, b, (((0,), (0,)), ((), ())), preferred_element_type=F32)


class Mover:
    def __init__(self, sems):
        self.sems, self.count, self.open = sems, 0, []

    def start(self, source, target):
        copy = pltpu.make_async_copy(source, target, self.sems.at[self.count])
        self.count += 1
        self.open.append(copy)
        copy.start()
        return copy

    def wait(self, *copies):
        for copy in copies:
            copy.wait()
            self.open = [other for other in self.open if other is not copy]

    def finish(self):
        self.wait(*list(self.open))


def places():
    fsdp_index, tp_index = lax.axis_index("fsdp"), lax.axis_index("tp")
    return tp_index, tp_index % 2, fsdp_index // INNER, fsdp_index % INNER, tp_index * KVH // lax.axis_size("tp")


def call(kernel, name, operands, out_shapes, scratch, waits=(), scalars=None, room=12, fast=(), near=()):
    copies = 4 * (len(operands) + len(out_shapes))
    scalars = [] if scalars is None else [scalars]

    def body(*refs):
        front, refs = refs[: len(scalars)], refs[len(scalars) :]
        ins, refs = refs[: len(operands)], refs[len(operands) + len(waits) :]
        outs, refs = refs[: len(out_shapes)], refs[len(out_shapes) :]
        mover = Mover(refs[-1])
        kernel(mover, *front, ins, outs, refs[:-1])
        mover.finish()

    results = pl.pallas_call(
        body,
        out_shape=[jax.ShapeDtypeStruct(shape, dtype) for shape, dtype in out_shapes],
        in_specs=[pl.BlockSpec(memory_space=pltpu.SMEM)] * len(scalars)
        + [pl.BlockSpec(memory_space=pltpu.VMEM if i in near else pltpu.HBM) for i in range(len(operands))]
        + [pl.BlockSpec(memory_space=pltpu.HBM)] * len(waits),
        out_specs=[
            pl.BlockSpec(memory_space=pltpu.VMEM if i in fast else pltpu.HBM) for i in range(len(out_shapes))
        ],
        scratch_shapes=[pltpu.VMEM(shape, dtype) for shape, dtype in scratch] + [pltpu.SemaphoreType.DMA((copies,))],
        compiler_params=pltpu.CompilerParams(vmem_limit_bytes=room << 20),
        cost_estimate=pl.CostEstimate(flops=0, bytes_accessed=0, transcendentals=0),
        name=name,
    )(*scalars, *operands, *waits)
    return list(results)


def kept(arrays, waits, name):
    count = len(arrays)
    results = pl.pallas_call(
        lambda *refs: None,
        out_shape=[jax.ShapeDtypeStruct(a.shape, a.dtype) for a in arrays],
        in_specs=[pl.BlockSpec(memory_space=pltpu.HBM)] * (count + len(waits)),
        out_specs=[pl.BlockSpec(memory_space=pltpu.HBM)] * count,
        input_output_aliases={i: i for i in range(count)},
        compiler_params=pltpu.CompilerParams(vmem_limit_bytes=12 << 20),
        cost_estimate=pl.CostEstimate(flops=0, bytes_accessed=0, transcendentals=0),
        name=name,
    )(*arrays, *waits)
    return list(results)


def shaped(*arrays):
    return [(a.shape, a.dtype) for a in arrays]


def attend_kernel(steps, mover, lengths_ref, ins, outs, scratch):
    query_hbm, keys_hbm, values_hbm, new_keys_hbm, new_values_hbm = ins
    query_ref, keys_ref, values_ref, new_keys_ref, new_values_ref, query_rows, out_rows = scratch
    tp_index, _, _, _, own_group = places()
    length = lengths_ref[0]
    own_ref, *chunk_refs = outs
    first = mover.start(query_hbm.at[0], query_ref)
    news = [mover.start(new_keys_hbm.at[0], new_keys_ref), mover.start(new_values_hbm.at[0], new_values_ref)]
    groups = [slice(g * HD, (g + 1) * HD) for g in range(KVH)]
    arrive = [
        (mover.start(keys_hbm.at[0, :, group], keys_ref.at[:, group]), mover.start(values_hbm.at[0, :, group], values_ref.at[:, group]))
        for group in groups
    ]
    width = query_ref.shape[1]
    cache_len = keys_ref.shape[0]
    rows = width // HD // KVH * steps
    mover.wait(first)
    for h in range(width // HD):
        query_rows[h * steps : (h + 1) * steps, :] = query_ref[:, h * HD : (h + 1) * HD].astype(F32)
    usable = lax.broadcasted_iota(jnp.int32, (rows, cache_len), 1) + tp_index * cache_len < length
    left = lax.broadcasted_iota(jnp.int32, (rows, HD), 1) < HD // 2
    for g in range(KVH):
        mover.wait(*arrive[g])
        query = query_rows[g * rows : (g + 1) * rows, :].astype(BF16)
        scores = over_features(query, keys_ref[:, g * HD : (g + 1) * HD]) * (1.0 / HD**0.5)
        maxima = jnp.max(jnp.where(usable, scores, NEG_FILL), axis=1, keepdims=True)
        terms = jnp.where(usable, jnp.exp(scores - maxima), 0.0)
        totals = jnp.sum(terms, axis=1, keepdims=True)
        upper = terms.astype(BF16)
        lower = (terms - upper.astype(F32)).astype(BF16)
        both = dot(jnp.concatenate([upper, lower], axis=0), values_ref[:, g * HD : (g + 1) * HD])
        out_rows[g * rows : (g + 1) * rows, :HD] = both[:rows] + both[rows:]
        out_rows[g * rows : (g + 1) * rows, HD:] = jnp.where(left, maxima, totals)
    count = chunk_refs[0].shape[1]
    for t in range(KVH * rows // count):
        for chunk_ref in chunk_refs:
            for k in range(chunk_ref.shape[0]):

                @pl.when(tp_index ^ (chunk_ref.shape[0] + k) == t)
                def _():
                    chunk_ref[k] = out_rows[t * count : (t + 1) * count, :]

        @pl.when(tp_index == t)
        def _():
            own_ref[:count, :] = out_rows[t * count : (t + 1) * count, :]
            own_ref[count : 2 * count, :HD] = query_rows[t * count : (t + 1) * count, :]

    mover.wait(*news)
    own_ref[count : 2 * count, HD:] = jnp.zeros((count, HD), F32)
    for at, ref in ((0, new_keys_ref), (HD, new_values_ref)):
        chosen = ref[:, :HD].astype(F32)
        for g in range(1, KVH):
            chosen = jnp.where(own_group == g, ref[:, groups[g]].astype(F32), chosen)
        own_ref[2 * count : 2 * count + steps, at : at + HD] = chosen


def combine_kernel(steps, sent, indices, attn_hbm, own_ref, *refs):
    *part_refs, out_hbm, rows_ref, load_ref, sems = refs
    rest = attn_hbm.shape[0] - sent
    arrive = pltpu.make_async_copy(attn_hbm.at[sent:], load_ref.at[:rest], sems.at[0])
    arrive.start()
    count = part_refs[0].shape[1]
    own = own_ref[...]
    rows_ref[...] = jnp.zeros_like(rows_ref)
    step = lax.broadcasted_iota(jnp.int32, (count, 1), 0) % steps
    query = own[count : 2 * count, :HD]
    keys, values = own[2 * count :, :HD], own[2 * count :, HD:]
    parts = [own[:count]] + [part_ref[i] for i, part_ref in zip(indices, part_refs)]
    scores = []
    for j in range(steps):
        score = jnp.sum(query * keys[j : j + 1], axis=-1, keepdims=True) * (1.0 / HD**0.5)
        scores.append(jnp.where(step >= j, score, NEG_FILL))
    maxima = [part[:, HD : HD + 1] for part in parts]
    highest = functools.reduce(jnp.maximum, scores + maxima)
    total = jnp.zeros((count, 1), F32)
    weighted = jnp.zeros((count, HD), F32)
    for part, own in zip(parts, maxima):
        scale = jnp.exp(own - highest)
        total = total + part[:, HD + HD // 2 : HD + HD // 2 + 1] * scale
        weighted = weighted + part[:, :HD] * scale
    for j in range(steps):
        term = jnp.where(step >= j, jnp.exp(scores[j] - highest), 0.0)
        total = total + term
        weighted = weighted + term * values[j : j + 1]
    attended = weighted / total
    for row in range(count):
        h, s = row // steps, row % steps
        rows_ref[s : s + 1, h * HD : (h + 1) * HD] = attended[row : row + 1]
    load_ref[rest:, :] = rows_ref[...].astype(BF16)
    arrive.wait()
    leave = pltpu.make_async_copy(load_ref, out_hbm, sems.at[1])
    leave.start()
    leave.wait()


def cut_kernel(outer, half, early, mover, ins, outs, scratch):
    grad_hbm, attn_hbm = ins
    plane = outs[0].shape[1]
    _, core, z, _, _ = places()
    rows = pl.ds(pl.multiple_of(core * half, half), half)
    for k in range(1, outer):
        columns = pl.ds(pl.multiple_of((z + k) % outer * plane, plane), plane)
        mover.start(grad_hbm.at[rows, columns], scratch[0].at[k - 1, :half])
        mover.start(attn_hbm.at[:early], scratch[0].at[k - 1, half:])
    arrive = list(mover.open)
    for k in range(1, outer):
        mover.wait(*arrive[2 * k - 2 : 2 * k])
        mover.start(scratch[0].at[k - 1], outs[k - 1])


def middle_kernel(outer, mover, ins, outs, scratch):
    grad_hbm, weight_hbm, other_hbm, *cot_hbms = ins
    sent_outs, (total_out, cot_own_out, *cot_far_outs) = outs[: outer - 1], outs[outer - 1 :]
    cots_ref, weight_ref, other_ref, sent_ref, total_ref, cot_own_ref, cot_far_ref = scratch
    _, core, z, x, _ = places()
    tokens = grad_hbm.shape[0]
    plane = cots_ref.shape[1]
    feats = weight_ref.shape[0]
    half = tokens // 2
    weights = [mover.start(weight_hbm, weight_ref), mover.start(other_hbm, other_ref)]
    blocks = [[mover.start(grad_hbm.at[:, pl.ds(pl.multiple_of(z * plane, plane), plane)], cots_ref.at[:tokens])]]
    for k in range(1, outer):
        blocks.append([])
        for hbm, side in ((cot_hbms[k - 1], core), (cot_hbms[outer + k - 2], 1 - core)):
            first = pl.multiple_of(k * tokens + side * half, half)
            blocks[k].append(mover.start(hbm.at[:half], cots_ref.at[pl.ds(first, half)]))
    mover.wait(*weights)
    span = outer * half
    for k in reversed(range(outer)):
        mover.wait(*blocks[k])
        here = slice(k * tokens, (k + 1) * tokens)
        block = cots_ref[here, :]
        low, high = block[:, :feats], block[:, feats:]
        own = jnp.where(x == 0, low, high)
        other = jnp.where(x == 0, high, low)
        total = dot(own, weight_ref[...]) + dot(other, other_ref[...])
        if k == 0:
            total_ref[...] = total
            mover.start(total_ref, total_out)
        else:
            sent_ref[k - 1] = total.astype(BF16)
            mover.start(sent_ref.at[k - 1], sent_outs[k - 1])
        cot_own_ref[here, :] = own
        cot_far_ref[here, :] = other

    size = cot_far_outs[0].shape[0]
    for i, out in enumerate(cot_far_outs):
        first = pl.multiple_of(core * span + i * size, size)
        mover.start(cot_far_ref.at[pl.ds(first, size)], out)
    mover.start(cot_own_ref, cot_own_out)


def decode_kernel(steps, mover, ins, outs, scratch):
    weight_hbm, other_hbm, *load_hbms = ins
    weight_ref, other_ref, dec_ref, rows_ref, by_row_ref, parts_ref = scratch
    _, _, z, x, _ = places()
    tokens = load_hbms[0].shape[0] - PAD
    outer, share = len(load_hbms), outs[0].shape[1]
    arrive = [mover.start(hbm, dec_ref.at[k]) for k, hbm in enumerate(load_hbms)]
    mover.wait(*arrive, mover.start(weight_hbm, weight_ref), mover.start(other_hbm, other_ref))
    for k in range(outer):
        rows_ref[k * steps : (k + 1) * steps, :] = dec_ref[k, tokens:, :].astype(F32)[:steps]
    every = rows_ref[...].astype(BF16)
    own, other = over_features(every, weight_ref[...]), over_features(every, other_ref[...])
    wide = jnp.concatenate([jnp.where(x == 0, own, other), jnp.where(x == 0, other, own)], axis=1)
    for k in range(outer):
        by_row_ref[k] = wide[k * steps : (k + 1) * steps]
    for q in range(parts_ref.shape[0]):
        for i in range(share):
            parts_ref[q, i] = by_row_ref[(z - (q * share + i)) % outer]
    mover.start(parts_ref, outs[0])


def own_kernel(mover, ins, outs, scratch):
    cot_hbm, attn_hbm, half_hbm, twin_hbm = ins
    cots_ref, attn_ref, others_ref = scratch
    _, core, _, _, _ = places()
    size = half_hbm.shape[0]
    arrive = [mover.start(cot_hbm, cots_ref), mover.start(attn_hbm, attn_ref)]
    halves = [
        mover.start(hbm, others_ref.at[pl.ds(pl.multiple_of((core ^ i) * size, size), size)])
        for i, hbm in enumerate((half_hbm, twin_hbm))
    ]
    mover.wait(*arrive)
    outs[0][...] = over_tokens(cots_ref[...], attn_ref[...])
    mover.wait(*halves)
    outs[1][...] = others_ref[...].T


def product_kernel(mover, ins, outs, scratch):
    own_ref, attn_ref, turned_ref = ins
    (out_ref,) = scratch
    pieces = 2
    step = out_ref.shape[0] // pieces
    for i in range(pieces):
        here = slice(i * step, (i + 1) * step)
        out_ref[here, :] = own_ref[here, :] + dot(turned_ref[here, :], attn_ref[...])
        mover.start(out_ref.at[here], outs[0].at[here])
    outs[1][...] = jnp.zeros(outs[1].shape, F32)


def sum_kernel(outer, share, mover, ins, outs, scratch):
    total_ref, *rest = ins
    part_hbms, piece_refs = rest[: outer - 1], rest[outer - 1 :]
    parts_ref, sum_ref = scratch
    _, _, z, _, _ = places()
    plane = piece_refs[0].shape[1]
    arrive = [mover.start(hbm, parts_ref.at[i]) for i, hbm in enumerate(part_hbms)]
    for j in range(share):
        mover.start(piece_refs[j], outs[0].at[0, :, pl.ds(pl.multiple_of((z % share ^ j) * plane, plane), plane)])
    mover.wait(*arrive)
    total = total_ref[...]
    for i in range(outer - 1):
        total = total + parts_ref[i].astype(F32)
    sum_ref[...] = total.astype(BF16)
    mover.start(sum_ref, outs[1])


def pack_kernel(early, skip, mover, ins, outs, scratch):
    low_hbm, high_hbm, own_hbm, *first_hbms = ins
    cots_ref, attn_out = outs
    (attn_ref,) = scratch
    tokens, size = own_hbm.shape[0], low_hbm.shape[0]
    mover.start(low_hbm, cots_ref.at[:size])
    mover.start(high_hbm, cots_ref.at[size:])
    parts = [(own_hbm, 0, tokens)] + [(hbm.at[skip:], (k + 1) * tokens, early) for k, hbm in enumerate(first_hbms)]
    arrive = [mover.start(source, attn_ref.at[at : at + rows]) for source, at, rows in parts]
    for copy, (_, at, rows) in zip(arrive, parts):
        mover.wait(copy)
        mover.start(attn_ref.at[at : at + rows], attn_out.at[at : at + rows])


def gate_kernel(count, early, *refs):
    refs, pack_out, (last_ref, in_sems, out_sems) = refs[count + 2 : -4 - count], refs[-4], refs[-3:]
    rest = refs[0].shape[0] - PAD
    tokens = rest + early
    arrive, leave = [], []
    for k, ref in enumerate(refs[::-1]):
        arrive.append(pltpu.make_async_copy(ref.at[:rest], last_ref.at[k], in_sems.at[k]))
        target = pack_out.at[(k + 1) * tokens + early : (k + 2) * tokens]
        leave.append(pltpu.make_async_copy(last_ref.at[k], target, out_sems.at[k]))
    for copy in arrive:
        copy.start()
    for copy, follow in zip(arrive, leave):
        copy.wait()
        follow.start()
    for copy in leave:
        copy.wait()


def shards(dec_query, new_keys, new_values, cache_keys, cache_values, lengths, out_weight, train_attn, grad_out):
    rows, steps, width = dec_query.shape
    assert rows == 1
    fsdp_size = lax.axis_size("fsdp")
    tp_size = lax.axis_size("tp")
    outer = fsdp_size // INNER
    share = outer // tp_size
    fsdp_index = lax.axis_index("fsdp")
    tp_index = lax.axis_index("tp")
    z, x = fsdp_index // INNER, fsdp_index % INNER
    tokens = grad_out.shape[0]
    feats, cols = out_weight.shape
    plane = feats * INNER
    slot = tp_index % 4
    heads = width // HD
    count = heads // tp_size * steps
    far = range(1, outer)
    others = range(1, tp_size)

    other_weight = flip(out_weight, "fsdp", 1, "weight_x")

    half = tokens // 2

    early = tokens // 8
    cot_rows = half * plane // cols
    if plane == cols:
        cuts = call(
            functools.partial(cut_kernel, outer, half, early),
            "cut",
            [grad_out, train_attn],
            [((half + early, cols), BF16)] * len(far),
            [((len(far), half + early, cols), BF16)],
            room=63,
        )
    else:
        first = tp_index % 2 * half
        cuts = [
            jnp.concatenate(
                [
                    lax.dynamic_slice(grad_out, (first, (z + k) % outer * plane), (half, plane)).reshape(cot_rows, cols),
                    train_attn[:early],
                ]
            )
            for k in far
        ]
    firsts = [turn(cuts[k - 1], k, f"first_z{k}") for k in far]
    got = firsts if plane == cols else [a[:cot_rows].reshape(half, plane) for a in firsts]

    sizes = [1 << b for b in range(tp_size.bit_length() - 1)]
    own, *chunks = call(
        functools.partial(attend_kernel, steps),
        "attend",
        [dec_query, cache_keys, cache_values, new_keys, new_values],
        [((2 * count + 8, 2 * HD), F32)]
        + [((size, count, 2 * HD), F32) for size in sizes],
        shaped(dec_query[0], cache_keys[0], cache_values[0], new_keys[0], new_values[0])
        + [((heads * steps, HD), F32), ((heads * steps, 2 * HD), F32)],
        scalars=lengths,
        room=63,
        fast=range(1 + len(sizes)),
    )
    own = pl.pallas_call(
        lambda in_ref, out_ref: out_ref.__setitem__(..., in_ref[...]),
        out_shape=jax.ShapeDtypeStruct(own.shape, own.dtype),
        in_specs=[pl.BlockSpec(memory_space=pltpu.VMEM)],
        out_specs=pl.BlockSpec(memory_space=pltpu.VMEM),
        compiler_params=pltpu.CompilerParams(vmem_limit_bytes=12 << 20),
        cost_estimate=pl.CostEstimate(flops=0, bytes_accessed=0, transcendentals=0),
        name="hold",
    )(own)
    parts, indices, held = [], [], []
    for size, chunk in reversed(list(zip(sizes, chunks))):
        if size > 1:
            came = [flip(a, "tp", size, f"softmax_tp{size}") for a in [chunk] + [a[size:] for a in held]]
            held = [a[:size] for a in held] + came
        else:
            parts += held + [flip(a, "tp", size, f"softmax_tp{size}") for a in [chunk] + held]
            indices += [0] * len(held) + [0] + [1] * len(held)
    last = pl.pallas_call(
        functools.partial(combine_kernel, steps, early, indices),
        out_shape=jax.ShapeDtypeStruct((tokens - early + PAD, cols), BF16),
        in_specs=[pl.BlockSpec(memory_space=pltpu.HBM)] + [pl.BlockSpec(memory_space=pltpu.VMEM)] * (len(parts) + 1),
        out_specs=pl.BlockSpec(memory_space=pltpu.HBM),
        scratch_shapes=[
            pltpu.VMEM((PAD, cols), F32),
            pltpu.VMEM((tokens - early + PAD, cols), BF16),
            pltpu.SemaphoreType.DMA((2,)),
        ],
        compiler_params=pltpu.CompilerParams(vmem_limit_bytes=12 << 20),
        cost_estimate=pl.CostEstimate(flops=0, bytes_accessed=0, transcendentals=0),
        name="combine",
    )(train_attn, own, *parts)

    lasts = [last] + [turn(last, k, f"last_z{k}") for k in far]

    got = kept(got, [last], "kept")
    twins = [flip(a, "tp", 1, "cot_core") for a in got]

    *sent, total, cot_own, cot_low, cot_high = call(
        functools.partial(middle_kernel, outer),
        "middle",
        [grad_out, out_weight, other_weight, *got, *twins],
        [((tokens, cols), BF16)] * len(far)
        + [((tokens, cols), F32), ((outer * tokens, feats), BF16)] + [((outer * half // 2, feats), BF16)] * 2,
        [
            ((outer * tokens, plane), BF16),
            ((feats, cols), BF16),
            ((feats, cols), BF16),
            ((len(far), tokens, cols), BF16),
            ((tokens, cols), F32),
            ((outer * tokens, feats), BF16),
            ((outer * tokens, feats), BF16),
        ],
        room=12,
    )
    cots_x = [flip(a, "fsdp", 1, "cot_x") for a in (cot_low, cot_high)]

    cots_x, pack = call(
        functools.partial(pack_kernel, early, cot_rows),
        "pack",
        [*cots_x, train_attn, *(got if plane == cols else firsts)],
        [((outer * half, feats), BF16), ((outer * tokens, cols), BF16)],
        [((outer * tokens, cols), BF16)],
        fast=[0],
    )

    results = pl.pallas_call(
        functools.partial(gate_kernel, len(sent), early),
        out_shape=[jax.ShapeDtypeStruct(a.shape, a.dtype) for a in [*sent, pack]],
        in_specs=[pl.BlockSpec(memory_space=pltpu.HBM)] * (len(sent) + 2 + len(far)),
        out_specs=[pl.BlockSpec(memory_space=pltpu.HBM)] * (len(sent) + 1),
        scratch_shapes=[
            pltpu.VMEM((len(far), tokens - early, cols), BF16),
            pltpu.SemaphoreType.DMA((len(far),)),
            pltpu.SemaphoreType.DMA((len(far),)),
        ],
        input_output_aliases={i: i for i in range(len(sent) + 1)},
        compiler_params=pltpu.CompilerParams(vmem_limit_bytes=12 << 20),
        cost_estimate=pl.CostEstimate(flops=0, bytes_accessed=0, transcendentals=0),
        name="gate",
    )(*sent, pack, cots_x, *lasts[:0:-1])
    sent, pack = results[:-1], results[-1]
    sums = [turn(sent[k - 1], outer - k, f"sum_z{k}") for k in far]
    pack_x = flip(pack, "fsdp", 1, "attn_x")
    twin_x = flip(cots_x, "tp", 1, "cot_x_core")

    (dec,) = call(
        functools.partial(decode_kernel, steps),
        "decode",
        [out_weight, other_weight, *lasts],
        [((tp_size, share, steps, plane), F32)],
        [
            ((feats, cols), BF16),
            ((feats, cols), BF16),
            ((outer, tokens - early + PAD, cols), BF16),
            ((outer * steps, cols), F32),
            ((outer, steps, plane), F32),
            ((tp_size, share, steps, plane), F32),
        ],
        waits=[pack],
        room=12,
    )
    with jax.named_scope("dec_tp"):
        dec = lax.all_to_all(dec, "tp", 0, 0, tiled=True).sum(axis=0).astype(BF16)
    pieces = []
    for j in range(share):
        perm = [
            ((a * INNER + b) * tp_size + q, ((q * share + (a % share ^ j)) * INNER + b) * tp_size + a // share)
            for a in range(outer)
            for b in range(INNER)
            for q in range(tp_size)
        ]
        with jax.named_scope("dec_place"):
            pieces.append(lax.ppermute(lax.dynamic_index_in_dim(dec, z % share ^ j, 0, False), ("fsdp", "tp"), perm))
    own_total, turned = call(
        own_kernel,
        "own",
        [cot_own, pack, cots_x, twin_x],
        [((feats, cols), F32), ((feats, outer * tokens), BF16)],
        [((outer * tokens, feats), BF16), ((outer * tokens, cols), BF16), ((outer * tokens, feats), BF16)],
        fast=[0, 1],
    )
    grad_weight, mark = call(
        product_kernel,
        "product",
        [own_total, pack_x, turned],
        [((feats, cols), F32), ((8, HD), F32)],
        [((feats, cols), F32)],
        near=range(3),
        fast=[1],
    )
    operands = [total, *sums[::-1], *pieces]
    dec_out, grad_attn = call(
        functools.partial(sum_kernel, outer, share),
        "sum",
        operands,
        [((rows, steps, share * plane), BF16), ((tokens, cols), BF16)],
        [((len(far), tokens, cols), BF16), ((tokens, cols), BF16)],
        waits=[mark],
        near=[0, *range(outer, len(operands))],
    )
    return dec_out, grad_attn, grad_weight


def solution(mesh):
    return jax.shard_map(
        shards,
        mesh=mesh,
        in_specs=(
            P("fsdp", None, None),
            P("fsdp", None, None),
            P("fsdp", None, None),
            P("fsdp", "tp", None),
            P("fsdp", "tp", None),
            P("fsdp"),
            P("fsdp", "tp"),
            P("fsdp", "tp"),
            P("fsdp", None),
        ),
        out_specs=(P("fsdp", None, "tp"), P("fsdp", "tp"), P("fsdp", "tp")),
        check_vma=False,
    )
```

```python
import functools

import jax
import jax.numpy as jnp
from jax import lax
from jax.experimental import pallas as pl
from jax.experimental.pallas import tpu as pltpu
from jax.sharding import PartitionSpec as P

KVH = 4
HD = 128
NEG_FILL = -1e30
INNER = 2
PAD = 8
BF16 = jnp.bfloat16
F32 = jnp.float32


def flip(a, axis, bits, name):
    size = lax.axis_size(axis)
    with jax.named_scope(name):
        return lax.ppermute(a, axis, [(i, i ^ bits) for i in range(size)])


def turn(a, steps, name):
    outer = lax.axis_size("fsdp") // INNER
    with jax.named_scope(name):
        return lax.ppermute(
            a, "fsdp", [(z * INNER + x, (z + steps) % outer * INNER + x) for z in range(outer) for x in range(INNER)]
        )


def dot(a, b):
    return jnp.dot(a, b, preferred_element_type=F32)


def over_features(a, b):
    return lax.dot_general(a, b, (((1,), (1,)), ((), ())), preferred_element_type=F32)


def over_tokens(a, b):
    return lax.dot_general(a, b, (((0,), (0,)), ((), ())), preferred_element_type=F32)


class Mover:
    def __init__(self, sems):
        self.sems, self.count, self.open = sems, 0, []

    def start(self, source, target):
        copy = pltpu.make_async_copy(source, target, self.sems.at[self.count])
        self.count += 1
        self.open.append(copy)
        copy.start()
        return copy

    def wait(self, *copies):
        for copy in copies:
            copy.wait()
            self.open = [other for other in self.open if other is not copy]

    def finish(self):
        self.wait(*list(self.open))


def places():
    fsdp_index, tp_index = lax.axis_index("fsdp"), lax.axis_index("tp")
    return tp_index, tp_index % 2, fsdp_index // INNER, fsdp_index % INNER, tp_index * KVH // lax.axis_size("tp")


def call(kernel, name, operands, out_shapes, scratch, waits=(), scalars=None, room=12, fast=(), near=()):
    copies = 4 * (len(operands) + len(out_shapes))
    scalars = [] if scalars is None else [scalars]

    def body(*refs):
        front, refs = refs[: len(scalars)], refs[len(scalars) :]
        ins, refs = refs[: len(operands)], refs[len(operands) + len(waits) :]
        outs, refs = refs[: len(out_shapes)], refs[len(out_shapes) :]
        mover = Mover(refs[-1])
        kernel(mover, *front, ins, outs, refs[:-1])
        mover.finish()

    results = pl.pallas_call(
        body,
        out_shape=[jax.ShapeDtypeStruct(shape, dtype) for shape, dtype in out_shapes],
        in_specs=[pl.BlockSpec(memory_space=pltpu.SMEM)] * len(scalars)
        + [pl.BlockSpec(memory_space=pltpu.VMEM if i in near else pltpu.HBM) for i in range(len(operands))]
        + [pl.BlockSpec(memory_space=pltpu.HBM)] * len(waits),
        out_specs=[
            pl.BlockSpec(memory_space=pltpu.VMEM if i in fast else pltpu.HBM) for i in range(len(out_shapes))
        ],
        scratch_shapes=[pltpu.VMEM(shape, dtype) for shape, dtype in scratch] + [pltpu.SemaphoreType.DMA((copies,))],
        compiler_params=pltpu.CompilerParams(vmem_limit_bytes=room << 20),
        cost_estimate=pl.CostEstimate(flops=0, bytes_accessed=0, transcendentals=0),
        name=name,
    )(*scalars, *operands, *waits)
    return list(results)


def kept(arrays, waits, name):
    count = len(arrays)
    results = pl.pallas_call(
        lambda *refs: None,
        out_shape=[jax.ShapeDtypeStruct(a.shape, a.dtype) for a in arrays],
        in_specs=[pl.BlockSpec(memory_space=pltpu.HBM)] * (count + len(waits)),
        out_specs=[pl.BlockSpec(memory_space=pltpu.HBM)] * count,
        input_output_aliases={i: i for i in range(count)},
        compiler_params=pltpu.CompilerParams(vmem_limit_bytes=12 << 20),
        cost_estimate=pl.CostEstimate(flops=0, bytes_accessed=0, transcendentals=0),
        name=name,
    )(*arrays, *waits)
    return list(results)


def shaped(*arrays):
    return [(a.shape, a.dtype) for a in arrays]


def attend_kernel(steps, mover, lengths_ref, ins, outs, scratch):
    query_hbm, keys_hbm, values_hbm, new_keys_hbm, new_values_hbm = ins
    query_ref, keys_ref, values_ref, new_keys_ref, new_values_ref, query_rows, out_rows = scratch
    tp_index, _, _, _, own_group = places()
    length = lengths_ref[0]
    own_ref, *chunk_refs = outs
    first = mover.start(query_hbm.at[0], query_ref)
    news = [mover.start(new_keys_hbm.at[0], new_keys_ref), mover.start(new_values_hbm.at[0], new_values_ref)]
    groups = [slice(g * HD, (g + 1) * HD) for g in range(KVH)]
    arrive = [
        (mover.start(keys_hbm.at[0, :, group], keys_ref.at[:, group]), mover.start(values_hbm.at[0, :, group], values_ref.at[:, group]))
        for group in groups
    ]
    width = query_ref.shape[1]
    cache_len = keys_ref.shape[0]
    rows = width // HD // KVH * steps
    mover.wait(first)
    for h in range(width // HD):
        query_rows[h * steps : (h + 1) * steps, :] = query_ref[:, h * HD : (h + 1) * HD].astype(F32)
    usable = lax.broadcasted_iota(jnp.int32, (rows, cache_len), 1) + tp_index * cache_len < length
    left = lax.broadcasted_iota(jnp.int32, (rows, HD), 1) < HD // 2
    for g in range(KVH):
        mover.wait(*arrive[g])
        query = query_rows[g * rows : (g + 1) * rows, :].astype(BF16)
        scores = over_features(query, keys_ref[:, g * HD : (g + 1) * HD]) * (1.0 / HD**0.5)
        maxima = jnp.max(jnp.where(usable, scores, NEG_FILL), axis=1, keepdims=True)
        terms = jnp.where(usable, jnp.exp(scores - maxima), 0.0)
        totals = jnp.sum(terms, axis=1, keepdims=True)
        upper = terms.astype(BF16)
        lower = (terms - upper.astype(F32)).astype(BF16)
        both = dot(jnp.concatenate([upper, lower], axis=0), values_ref[:, g * HD : (g + 1) * HD])
        out_rows[g * rows : (g + 1) * rows, :HD] = both[:rows] + both[rows:]
        out_rows[g * rows : (g + 1) * rows, HD:] = jnp.where(left, maxima, totals)
    count = chunk_refs[0].shape[1]
    for t in range(KVH * rows // count):
        for chunk_ref in chunk_refs:
            for k in range(chunk_ref.shape[0]):

                @pl.when(tp_index ^ (chunk_ref.shape[0] + k) == t)
                def _():
                    chunk_ref[k] = out_rows[t * count : (t + 1) * count, :]

        @pl.when(tp_index == t)
        def _():
            own_ref[:count, :] = out_rows[t * count : (t + 1) * count, :]
            own_ref[count : 2 * count, :HD] = query_rows[t * count : (t + 1) * count, :]

    mover.wait(*news)
    own_ref[count : 2 * count, HD:] = jnp.zeros((count, HD), F32)
    for at, ref in ((0, new_keys_ref), (HD, new_values_ref)):
        chosen = ref[:, :HD].astype(F32)
        for g in range(1, KVH):
            chosen = jnp.where(own_group == g, ref[:, groups[g]].astype(F32), chosen)
        own_ref[2 * count : 2 * count + steps, at : at + HD] = chosen


def combine_kernel(steps, sent, indices, attn_hbm, own_ref, *refs):
    *part_refs, out_hbm, rows_ref, load_ref, sems = refs
    rest = attn_hbm.shape[0] - sent
    arrive = pltpu.make_async_copy(attn_hbm.at[sent:], load_ref.at[:rest], sems.at[0])
    arrive.start()
    count = part_refs[0].shape[1]
    own = own_ref[...]
    rows_ref[...] = jnp.zeros_like(rows_ref)
    step = lax.broadcasted_iota(jnp.int32, (count, 1), 0) % steps
    query = own[count : 2 * count, :HD]
    keys, values = own[2 * count :, :HD], own[2 * count :, HD:]
    parts = [own[:count]] + [part_ref[i] for i, part_ref in zip(indices, part_refs)]
    scores = []
    for j in range(steps):
        score = jnp.sum(query * keys[j : j + 1], axis=-1, keepdims=True) * (1.0 / HD**0.5)
        scores.append(jnp.where(step >= j, score, NEG_FILL))
    maxima = [part[:, HD : HD + 1] for part in parts]
    highest = functools.reduce(jnp.maximum, scores + maxima)
    total = jnp.zeros((count, 1), F32)
    weighted = jnp.zeros((count, HD), F32)
    for part, own in zip(parts, maxima):
        scale = jnp.exp(own - highest)
        total = total + part[:, HD + HD // 2 : HD + HD // 2 + 1] * scale
        weighted = weighted + part[:, :HD] * scale
    for j in range(steps):
        term = jnp.where(step >= j, jnp.exp(scores[j] - highest), 0.0)
        total = total + term
        weighted = weighted + term * values[j : j + 1]
    attended = weighted / total
    for row in range(count):
        h, s = row // steps, row % steps
        rows_ref[s : s + 1, h * HD : (h + 1) * HD] = attended[row : row + 1]
    load_ref[rest:, :] = rows_ref[...].astype(BF16)
    arrive.wait()
    leave = pltpu.make_async_copy(load_ref, out_hbm, sems.at[1])
    leave.start()
    leave.wait()


def cut_kernel(outer, half, early, mover, ins, outs, scratch):
    grad_hbm, attn_hbm = ins
    plane = outs[0].shape[1]
    _, core, z, _, _ = places()
    rows = pl.ds(pl.multiple_of(core * half, half), half)
    for k in range(1, outer):
        columns = pl.ds(pl.multiple_of((z + k) % outer * plane, plane), plane)
        mover.start(grad_hbm.at[rows, columns], scratch[0].at[k - 1, :half])
        mover.start(attn_hbm.at[:early], scratch[0].at[k - 1, half:])
    arrive = list(mover.open)
    for k in range(1, outer):
        mover.wait(*arrive[2 * k - 2 : 2 * k])
        mover.start(scratch[0].at[k - 1], outs[k - 1])


def middle_kernel(outer, mover, ins, outs, scratch):
    grad_hbm, weight_hbm, other_hbm, *cot_hbms = ins
    sent_outs, (total_out, cot_own_out, *cot_far_outs) = outs[: outer - 1], outs[outer - 1 :]
    cots_ref, weight_ref, other_ref, sent_ref, total_ref, cot_own_ref, cot_far_ref = scratch
    _, core, z, x, _ = places()
    tokens = grad_hbm.shape[0]
    plane = cots_ref.shape[1]
    feats = weight_ref.shape[0]
    half = tokens // 2
    weights = [mover.start(weight_hbm, weight_ref), mover.start(other_hbm, other_ref)]
    blocks = [[mover.start(grad_hbm.at[:, pl.ds(pl.multiple_of(z * plane, plane), plane)], cots_ref.at[:tokens])]]
    for k in range(1, outer):
        blocks.append([])
        for hbm, side in ((cot_hbms[k - 1], core), (cot_hbms[outer + k - 2], 1 - core)):
            first = pl.multiple_of(k * tokens + side * half, half)
            blocks[k].append(mover.start(hbm.at[:half], cots_ref.at[pl.ds(first, half)]))
    mover.wait(*weights)
    span = outer * half
    for k in reversed(range(outer)):
        mover.wait(*blocks[k])
        here = slice(k * tokens, (k + 1) * tokens)
        block = cots_ref[here, :]
        low, high = block[:, :feats], block[:, feats:]
        own = jnp.where(x == 0, low, high)
        other = jnp.where(x == 0, high, low)
        total = dot(own, weight_ref[...]) + dot(other, other_ref[...])
        if k == 0:
            total_ref[...] = total
            mover.start(total_ref, total_out)
        else:
            sent_ref[k - 1] = total.astype(BF16)
            mover.start(sent_ref.at[k - 1], sent_outs[k - 1])
        cot_own_ref[here, :] = own
        cot_far_ref[here, :] = other

    size = cot_far_outs[0].shape[0]
    for i, out in enumerate(cot_far_outs):
        first = pl.multiple_of(core * span + i * size, size)
        mover.start(cot_far_ref.at[pl.ds(first, size)], out)
    mover.start(cot_own_ref, cot_own_out)


def decode_kernel(steps, mover, ins, outs, scratch):
    weight_hbm, other_hbm, *load_hbms = ins
    weight_ref, other_ref, dec_ref, rows_ref, by_row_ref, parts_ref = scratch
    _, _, z, x, _ = places()
    tokens = load_hbms[0].shape[0] - PAD
    outer, share = len(load_hbms), outs[0].shape[1]
    arrive = [mover.start(hbm, dec_ref.at[k]) for k, hbm in enumerate(load_hbms)]
    mover.wait(*arrive, mover.start(weight_hbm, weight_ref), mover.start(other_hbm, other_ref))
    for k in range(outer):
        rows_ref[k * steps : (k + 1) * steps, :] = dec_ref[k, tokens:, :].astype(F32)[:steps]
    every = rows_ref[...].astype(BF16)
    own, other = over_features(every, weight_ref[...]), over_features(every, other_ref[...])
    wide = jnp.concatenate([jnp.where(x == 0, own, other), jnp.where(x == 0, other, own)], axis=1)
    for k in range(outer):
        by_row_ref[k] = wide[k * steps : (k + 1) * steps]
    for q in range(parts_ref.shape[0]):
        for i in range(share):
            parts_ref[q, i] = by_row_ref[(z - (q * share + i)) % outer]
    mover.start(parts_ref, outs[0])


def own_kernel(mover, ins, outs, scratch):
    cot_hbm, attn_hbm, half_hbm, twin_hbm = ins
    cots_ref, attn_ref, others_ref = scratch
    _, core, _, _, _ = places()
    size = half_hbm.shape[0]
    arrive = [mover.start(cot_hbm, cots_ref), mover.start(attn_hbm, attn_ref)]
    halves = [
        mover.start(hbm, others_ref.at[pl.ds(pl.multiple_of((core ^ i) * size, size), size)])
        for i, hbm in enumerate((half_hbm, twin_hbm))
    ]
    mover.wait(*arrive)
    outs[0][...] = over_tokens(cots_ref[...], attn_ref[...])
    mover.wait(*halves)
    outs[1][...] = others_ref[...].T


def product_kernel(mover, ins, outs, scratch):
    own_ref, attn_ref, turned_ref = ins
    (out_ref,) = scratch
    pieces = 4
    step = out_ref.shape[0] // pieces
    for i in range(pieces):
        here = slice(i * step, (i + 1) * step)
        out_ref[here, :] = own_ref[here, :] + dot(turned_ref[here, :], attn_ref[...])
        mover.start(out_ref.at[here], outs[0].at[here])
    outs[1][...] = jnp.zeros(outs[1].shape, F32)


def sum_kernel(outer, share, mover, ins, outs, scratch):
    total_ref, *rest = ins
    part_hbms, piece_refs = rest[: outer - 1], rest[outer - 1 :]
    parts_ref, sum_ref = scratch
    _, _, z, _, _ = places()
    plane = piece_refs[0].shape[1]
    arrive = [mover.start(hbm, parts_ref.at[i]) for i, hbm in enumerate(part_hbms)]
    for j in range(share):
        mover.start(piece_refs[j], outs[0].at[0, :, pl.ds(pl.multiple_of((z % share ^ j) * plane, plane), plane)])
    mover.wait(*arrive)
    total = total_ref[...]
    for i in range(outer - 1):
        total = total + parts_ref[i].astype(F32)
    sum_ref[...] = total.astype(BF16)
    mover.start(sum_ref, outs[1])


def pack_kernel(early, skip, mover, ins, outs, scratch):
    low_hbm, high_hbm, own_hbm, *first_hbms = ins
    cots_ref, attn_out = outs
    (attn_ref,) = scratch
    tokens, size = own_hbm.shape[0], low_hbm.shape[0]
    mover.start(low_hbm, cots_ref.at[:size])
    mover.start(high_hbm, cots_ref.at[size:])
    parts = [(own_hbm, 0, tokens)] + [(hbm.at[skip:], (k + 1) * tokens, early) for k, hbm in enumerate(first_hbms)]
    arrive = [mover.start(source, attn_ref.at[at : at + rows]) for source, at, rows in parts]
    for copy, (_, at, rows) in zip(arrive, parts):
        mover.wait(copy)
        mover.start(attn_ref.at[at : at + rows], attn_out.at[at : at + rows])


def gate_kernel(count, early, *refs):
    refs, pack_out, (last_ref, in_sems, out_sems) = refs[count + 2 : -4 - count], refs[-4], refs[-3:]
    rest = refs[0].shape[0] - PAD
    tokens = rest + early
    arrive, leave = [], []
    for k, ref in enumerate(refs[::-1]):
        arrive.append(pltpu.make_async_copy(ref.at[:rest], last_ref.at[k], in_sems.at[k]))
        target = pack_out.at[(k + 1) * tokens + early : (k + 2) * tokens]
        leave.append(pltpu.make_async_copy(last_ref.at[k], target, out_sems.at[k]))
    for copy in arrive:
        copy.start()
    for copy, follow in zip(arrive, leave):
        copy.wait()
        follow.start()
    for copy in leave:
        copy.wait()


def shards(dec_query, new_keys, new_values, cache_keys, cache_values, lengths, out_weight, train_attn, grad_out):
    rows, steps, width = dec_query.shape
    assert rows == 1
    fsdp_size = lax.axis_size("fsdp")
    tp_size = lax.axis_size("tp")
    outer = fsdp_size // INNER
    share = outer // tp_size
    fsdp_index = lax.axis_index("fsdp")
    tp_index = lax.axis_index("tp")
    z, x = fsdp_index // INNER, fsdp_index % INNER
    tokens = grad_out.shape[0]
    feats, cols = out_weight.shape
    plane = feats * INNER
    slot = tp_index % 4
    heads = width // HD
    count = heads // tp_size * steps
    far = range(1, outer)
    others = range(1, tp_size)

    other_weight = flip(out_weight, "fsdp", 1, "weight_x")

    half = tokens // 2

    early = tokens // 4
    cot_rows = half * plane // cols
    if plane == cols:
        cuts = call(
            functools.partial(cut_kernel, outer, half, early),
            "cut",
            [grad_out, train_attn],
            [((half + early, cols), BF16)] * len(far),
            [((len(far), half + early, cols), BF16)],
            room=63,
        )
    else:
        first = tp_index % 2 * half
        cuts = [
            jnp.concatenate(
                [
                    lax.dynamic_slice(grad_out, (first, (z + k) % outer * plane), (half, plane)).reshape(cot_rows, cols),
                    train_attn[:early],
                ]
            )
            for k in far
        ]
    firsts = [turn(cuts[k - 1], k, f"first_z{k}") for k in far]
    got = firsts if plane == cols else [a[:cot_rows].reshape(half, plane) for a in firsts]

    sizes = [1 << b for b in range(tp_size.bit_length() - 1)]
    own, *chunks = call(
        functools.partial(attend_kernel, steps),
        "attend",
        [dec_query, cache_keys, cache_values, new_keys, new_values],
        [((2 * count + 8, 2 * HD), F32)]
        + [((size, count, 2 * HD), F32) for size in sizes],
        shaped(dec_query[0], cache_keys[0], cache_values[0], new_keys[0], new_values[0])
        + [((heads * steps, HD), F32), ((heads * steps, 2 * HD), F32)],
        scalars=lengths,
        room=63,
        fast=range(1 + len(sizes)),
    )
    own = pl.pallas_call(
        lambda in_ref, out_ref: out_ref.__setitem__(..., in_ref[...]),
        out_shape=jax.ShapeDtypeStruct(own.shape, own.dtype),
        in_specs=[pl.BlockSpec(memory_space=pltpu.VMEM)],
        out_specs=pl.BlockSpec(memory_space=pltpu.VMEM),
        compiler_params=pltpu.CompilerParams(vmem_limit_bytes=12 << 20),
        cost_estimate=pl.CostEstimate(flops=0, bytes_accessed=0, transcendentals=0),
        name="hold",
    )(own)
    parts, indices, held = [], [], []
    for size, chunk in reversed(list(zip(sizes, chunks))):
        if size > 1:
            came = [flip(a, "tp", size, f"softmax_tp{size}") for a in [chunk] + [a[size:] for a in held]]
            held = [a[:size] for a in held] + came
        else:
            parts += held + [flip(a, "tp", size, f"softmax_tp{size}") for a in [chunk] + held]
            indices += [0] * len(held) + [0] + [1] * len(held)
    last = pl.pallas_call(
        functools.partial(combine_kernel, steps, early, indices),
        out_shape=jax.ShapeDtypeStruct((tokens - early + PAD, cols), BF16),
        in_specs=[pl.BlockSpec(memory_space=pltpu.HBM)] + [pl.BlockSpec(memory_space=pltpu.VMEM)] * (len(parts) + 1),
        out_specs=pl.BlockSpec(memory_space=pltpu.HBM),
        scratch_shapes=[
            pltpu.VMEM((PAD, cols), F32),
            pltpu.VMEM((tokens - early + PAD, cols), BF16),
            pltpu.SemaphoreType.DMA((2,)),
        ],
        compiler_params=pltpu.CompilerParams(vmem_limit_bytes=12 << 20),
        cost_estimate=pl.CostEstimate(flops=0, bytes_accessed=0, transcendentals=0),
        name="combine",
    )(train_attn, own, *parts)

    lasts = [last] + [turn(last, k, f"last_z{k}") for k in far]

    got = kept(got, [last], "kept")
    twins = [flip(a, "tp", 1, "cot_core") for a in got]

    *sent, total, cot_own, cot_low, cot_high = call(
        functools.partial(middle_kernel, outer),
        "middle",
        [grad_out, out_weight, other_weight, *got, *twins],
        [((tokens, cols), BF16)] * len(far)
        + [((tokens, cols), F32), ((outer * tokens, feats), BF16)] + [((outer * half // 2, feats), BF16)] * 2,
        [
            ((outer * tokens, plane), BF16),
            ((feats, cols), BF16),
            ((feats, cols), BF16),
            ((len(far), tokens, cols), BF16),
            ((tokens, cols), F32),
            ((outer * tokens, feats), BF16),
            ((outer * tokens, feats), BF16),
        ],
        room=12,
    )
    cots_x = [flip(a, "fsdp", 1, "cot_x") for a in (cot_low, cot_high)]

    cots_x, pack = call(
        functools.partial(pack_kernel, early, cot_rows),
        "pack",
        [*cots_x, train_attn, *(got if plane == cols else firsts)],
        [((outer * half, feats), BF16), ((outer * tokens, cols), BF16)],
        [((outer * tokens, cols), BF16)],
        fast=[0],
    )

    results = pl.pallas_call(
        functools.partial(gate_kernel, len(sent), early),
        out_shape=[jax.ShapeDtypeStruct(a.shape, a.dtype) for a in [*sent, pack]],
        in_specs=[pl.BlockSpec(memory_space=pltpu.HBM)] * (len(sent) + 2 + len(far)),
        out_specs=[pl.BlockSpec(memory_space=pltpu.HBM)] * (len(sent) + 1),
        scratch_shapes=[
            pltpu.VMEM((len(far), tokens - early, cols), BF16),
            pltpu.SemaphoreType.DMA((len(far),)),
            pltpu.SemaphoreType.DMA((len(far),)),
        ],
        input_output_aliases={i: i for i in range(len(sent) + 1)},
        compiler_params=pltpu.CompilerParams(vmem_limit_bytes=12 << 20),
        cost_estimate=pl.CostEstimate(flops=0, bytes_accessed=0, transcendentals=0),
        name="gate",
    )(*sent, pack, cots_x, *lasts[:0:-1])
    sent, pack = results[:-1], results[-1]
    sums = [turn(sent[k - 1], outer - k, f"sum_z{k}") for k in far]
    pack_x = flip(pack, "fsdp", 1, "attn_x")
    twin_x = flip(cots_x, "tp", 1, "cot_x_core")

    (dec,) = call(
        functools.partial(decode_kernel, steps),
        "decode",
        [out_weight, other_weight, *lasts],
        [((tp_size, share, steps, plane), F32)],
        [
            ((feats, cols), BF16),
            ((feats, cols), BF16),
            ((outer, tokens - early + PAD, cols), BF16),
            ((outer * steps, cols), F32),
            ((outer, steps, plane), F32),
            ((tp_size, share, steps, plane), F32),
        ],
        waits=[pack],
        room=12,
    )
    with jax.named_scope("dec_tp"):
        dec = lax.all_to_all(dec, "tp", 0, 0, tiled=True).sum(axis=0).astype(BF16)
    pieces = []
    for j in range(share):
        perm = [
            ((a * INNER + b) * tp_size + q, ((q * share + (a % share ^ j)) * INNER + b) * tp_size + a // share)
            for a in range(outer)
            for b in range(INNER)
            for q in range(tp_size)
        ]
        with jax.named_scope("dec_place"):
            pieces.append(lax.ppermute(lax.dynamic_index_in_dim(dec, z % share ^ j, 0, False), ("fsdp", "tp"), perm))
    own_total, turned = call(
        own_kernel,
        "own",
        [cot_own, pack, cots_x, twin_x],
        [((feats, cols), F32), ((feats, outer * tokens), BF16)],
        [((outer * tokens, feats), BF16), ((outer * tokens, cols), BF16), ((outer * tokens, feats), BF16)],
        fast=[0, 1],
    )
    grad_weight, mark = call(
        product_kernel,
        "product",
        [own_total, pack_x, turned],
        [((feats, cols), F32), ((8, HD), F32)],
        [((feats, cols), F32)],
        near=range(3),
        fast=[1],
    )
    operands = [total, *sums[::-1], *pieces]
    dec_out, grad_attn = call(
        functools.partial(sum_kernel, outer, share),
        "sum",
        operands,
        [((rows, steps, share * plane), BF16), ((tokens, cols), BF16)],
        [((len(far), tokens, cols), BF16), ((tokens, cols), BF16)],
        waits=[mark],
        near=[0, *range(outer, len(operands))],
    )
    return dec_out, grad_attn, grad_weight


def solution(mesh):
    return jax.shard_map(
        shards,
        mesh=mesh,
        in_specs=(
            P("fsdp", None, None),
            P("fsdp", None, None),
            P("fsdp", None, None),
            P("fsdp", "tp", None),
            P("fsdp", "tp", None),
            P("fsdp"),
            P("fsdp", "tp"),
            P("fsdp", "tp"),
            P("fsdp", None),
        ),
        out_specs=(P("fsdp", None, "tp"), P("fsdp", "tp"), P("fsdp", "tp")),
        check_vma=False,
    )
```

```python
import functools

import jax
import jax.numpy as jnp
from jax import lax
from jax.experimental import pallas as pl
from jax.experimental.pallas import tpu as pltpu
from jax.sharding import PartitionSpec as P

KVH = 4
HD = 128
NEG_FILL = -1e30
INNER = 2
PAD = 8
BF16 = jnp.bfloat16
F32 = jnp.float32


def flip(a, axis, bits, name):
    size = lax.axis_size(axis)
    with jax.named_scope(name):
        return lax.ppermute(a, axis, [(i, i ^ bits) for i in range(size)])


def turn(a, steps, name):
    outer = lax.axis_size("fsdp") // INNER
    with jax.named_scope(name):
        return lax.ppermute(
            a, "fsdp", [(z * INNER + x, (z + steps) % outer * INNER + x) for z in range(outer) for x in range(INNER)]
        )


def dot(a, b):
    return jnp.dot(a, b, preferred_element_type=F32)


def over_features(a, b):
    return lax.dot_general(a, b, (((1,), (1,)), ((), ())), preferred_element_type=F32)


def over_tokens(a, b):
    return lax.dot_general(a, b, (((0,), (0,)), ((), ())), preferred_element_type=F32)


class Mover:
    def __init__(self, sems):
        self.sems, self.count, self.open = sems, 0, []

    def start(self, source, target):
        copy = pltpu.make_async_copy(source, target, self.sems.at[self.count])
        self.count += 1
        self.open.append(copy)
        copy.start()
        return copy

    def wait(self, *copies):
        for copy in copies:
            copy.wait()
            self.open = [other for other in self.open if other is not copy]

    def finish(self):
        self.wait(*list(self.open))


def places():
    fsdp_index, tp_index = lax.axis_index("fsdp"), lax.axis_index("tp")
    return tp_index, tp_index % 2, fsdp_index // INNER, fsdp_index % INNER, tp_index * KVH // lax.axis_size("tp")


def call(kernel, name, operands, out_shapes, scratch, waits=(), scalars=None, room=12, fast=(), near=()):
    copies = 4 * (len(operands) + len(out_shapes))
    scalars = [] if scalars is None else [scalars]

    def body(*refs):
        front, refs = refs[: len(scalars)], refs[len(scalars) :]
        ins, refs = refs[: len(operands)], refs[len(operands) + len(waits) :]
        outs, refs = refs[: len(out_shapes)], refs[len(out_shapes) :]
        mover = Mover(refs[-1])
        kernel(mover, *front, ins, outs, refs[:-1])
        mover.finish()

    results = pl.pallas_call(
        body,
        out_shape=[jax.ShapeDtypeStruct(shape, dtype) for shape, dtype in out_shapes],
        in_specs=[pl.BlockSpec(memory_space=pltpu.SMEM)] * len(scalars)
        + [pl.BlockSpec(memory_space=pltpu.VMEM if i in near else pltpu.HBM) for i in range(len(operands))]
        + [pl.BlockSpec(memory_space=pltpu.HBM)] * len(waits),
        out_specs=[
            pl.BlockSpec(memory_space=pltpu.VMEM if i in fast else pltpu.HBM) for i in range(len(out_shapes))
        ],
        scratch_shapes=[pltpu.VMEM(shape, dtype) for shape, dtype in scratch] + [pltpu.SemaphoreType.DMA((copies,))],
        compiler_params=pltpu.CompilerParams(vmem_limit_bytes=room << 20),
        cost_estimate=pl.CostEstimate(flops=0, bytes_accessed=0, transcendentals=0),
        name=name,
    )(*scalars, *operands, *waits)
    return list(results)


def kept(arrays, waits, name):
    count = len(arrays)
    results = pl.pallas_call(
        lambda *refs: None,
        out_shape=[jax.ShapeDtypeStruct(a.shape, a.dtype) for a in arrays],
        in_specs=[pl.BlockSpec(memory_space=pltpu.HBM)] * (count + len(waits)),
        out_specs=[pl.BlockSpec(memory_space=pltpu.HBM)] * count,
        input_output_aliases={i: i for i in range(count)},
        compiler_params=pltpu.CompilerParams(vmem_limit_bytes=12 << 20),
        cost_estimate=pl.CostEstimate(flops=0, bytes_accessed=0, transcendentals=0),
        name=name,
    )(*arrays, *waits)
    return list(results)


def shaped(*arrays):
    return [(a.shape, a.dtype) for a in arrays]


def attend_kernel(steps, mover, lengths_ref, ins, outs, scratch):
    query_hbm, keys_hbm, values_hbm, new_keys_hbm, new_values_hbm = ins
    query_ref, keys_ref, values_ref, new_keys_ref, new_values_ref, query_rows, out_rows = scratch
    tp_index, _, _, _, own_group = places()
    length = lengths_ref[0]
    own_ref, *chunk_refs = outs
    first = mover.start(query_hbm.at[0], query_ref)
    news = [mover.start(new_keys_hbm.at[0], new_keys_ref), mover.start(new_values_hbm.at[0], new_values_ref)]
    groups = [slice(g * HD, (g + 1) * HD) for g in range(KVH)]
    arrive = [
        (mover.start(keys_hbm.at[0, :, group], keys_ref.at[:, group]), mover.start(values_hbm.at[0, :, group], values_ref.at[:, group]))
        for group in groups
    ]
    width = query_ref.shape[1]
    cache_len = keys_ref.shape[0]
    rows = width // HD // KVH * steps
    mover.wait(first)
    for h in range(width // HD):
        query_rows[h * steps : (h + 1) * steps, :] = query_ref[:, h * HD : (h + 1) * HD].astype(F32)
    usable = lax.broadcasted_iota(jnp.int32, (rows, cache_len), 1) + tp_index * cache_len < length
    left = lax.broadcasted_iota(jnp.int32, (rows, HD), 1) < HD // 2
    for g in range(KVH):
        mover.wait(*arrive[g])
        query = query_rows[g * rows : (g + 1) * rows, :].astype(BF16)
        scores = over_features(query, keys_ref[:, g * HD : (g + 1) * HD]) * (1.0 / HD**0.5)
        maxima = jnp.max(jnp.where(usable, scores, NEG_FILL), axis=1, keepdims=True)
        terms = jnp.where(usable, jnp.exp(scores - maxima), 0.0)
        totals = jnp.sum(terms, axis=1, keepdims=True)
        upper = terms.astype(BF16)
        lower = (terms - upper.astype(F32)).astype(BF16)
        both = dot(jnp.concatenate([upper, lower], axis=0), values_ref[:, g * HD : (g + 1) * HD])
        out_rows[g * rows : (g + 1) * rows, :HD] = both[:rows] + both[rows:]
        out_rows[g * rows : (g + 1) * rows, HD:] = jnp.where(left, maxima, totals)
    count = chunk_refs[0].shape[1]
    for t in range(KVH * rows // count):
        for chunk_ref in chunk_refs:
            for k in range(chunk_ref.shape[0]):

                @pl.when(tp_index ^ (chunk_ref.shape[0] + k) == t)
                def _():
                    chunk_ref[k] = out_rows[t * count : (t + 1) * count, :]

        @pl.when(tp_index == t)
        def _():
            own_ref[:count, :] = out_rows[t * count : (t + 1) * count, :]
            own_ref[count : 2 * count, :HD] = query_rows[t * count : (t + 1) * count, :]

    mover.wait(*news)
    own_ref[count : 2 * count, HD:] = jnp.zeros((count, HD), F32)
    for at, ref in ((0, new_keys_ref), (HD, new_values_ref)):
        chosen = ref[:, :HD].astype(F32)
        for g in range(1, KVH):
            chosen = jnp.where(own_group == g, ref[:, groups[g]].astype(F32), chosen)
        own_ref[2 * count : 2 * count + steps, at : at + HD] = chosen


def combine_kernel(steps, sent, indices, attn_hbm, own_ref, *refs):
    *part_refs, out_hbm, rows_ref, load_ref, sems = refs
    rest = attn_hbm.shape[0] - sent
    arrive = pltpu.make_async_copy(attn_hbm.at[sent:], load_ref.at[:rest], sems.at[0])
    arrive.start()
    count = part_refs[0].shape[1]
    own = own_ref[...]
    rows_ref[...] = jnp.zeros_like(rows_ref)
    step = lax.broadcasted_iota(jnp.int32, (count, 1), 0) % steps
    query = own[count : 2 * count, :HD]
    keys, values = own[2 * count :, :HD], own[2 * count :, HD:]
    parts = [own[:count]] + [part_ref[i] for i, part_ref in zip(indices, part_refs)]
    scores = []
    for j in range(steps):
        score = jnp.sum(query * keys[j : j + 1], axis=-1, keepdims=True) * (1.0 / HD**0.5)
        scores.append(jnp.where(step >= j, score, NEG_FILL))
    maxima = [part[:, HD : HD + 1] for part in parts]
    highest = functools.reduce(jnp.maximum, scores + maxima)
    total = jnp.zeros((count, 1), F32)
    weighted = jnp.zeros((count, HD), F32)
    for part, own in zip(parts, maxima):
        scale = jnp.exp(own - highest)
        total = total + part[:, HD + HD // 2 : HD + HD // 2 + 1] * scale
        weighted = weighted + part[:, :HD] * scale
    for j in range(steps):
        term = jnp.where(step >= j, jnp.exp(scores[j] - highest), 0.0)
        total = total + term
        weighted = weighted + term * values[j : j + 1]
    attended = weighted / total
    for row in range(count):
        h, s = row // steps, row % steps
        rows_ref[s : s + 1, h * HD : (h + 1) * HD] = attended[row : row + 1]
    load_ref[rest:, :] = rows_ref[...].astype(BF16)
    arrive.wait()
    leave = pltpu.make_async_copy(load_ref, out_hbm, sems.at[1])
    leave.start()
    leave.wait()


def cut_kernel(outer, half, early, mover, ins, outs, scratch):
    grad_hbm, attn_hbm = ins
    plane = outs[0].shape[1]
    _, core, z, _, _ = places()
    rows = pl.ds(pl.multiple_of(core * half, half), half)
    for k in range(1, outer):
        columns = pl.ds(pl.multiple_of((z + k) % outer * plane, plane), plane)
        mover.start(grad_hbm.at[rows, columns], scratch[0].at[k - 1, :half])
        mover.start(attn_hbm.at[:early], scratch[0].at[k - 1, half:])
    arrive = list(mover.open)
    for k in range(1, outer):
        mover.wait(*arrive[2 * k - 2 : 2 * k])
        mover.start(scratch[0].at[k - 1], outs[k - 1])


def middle_kernel(outer, mover, ins, outs, scratch):
    grad_hbm, weight_hbm, other_hbm, *cot_hbms = ins
    sent_outs, (total_out, cot_own_out, *cot_far_outs) = outs[: outer - 1], outs[outer - 1 :]
    cots_ref, weight_ref, other_ref, sent_ref, total_ref, cot_own_ref, cot_far_ref = scratch
    _, core, z, x, _ = places()
    tokens = grad_hbm.shape[0]
    plane = cots_ref.shape[1]
    feats = weight_ref.shape[0]
    half = tokens // 2
    weights = [mover.start(weight_hbm, weight_ref), mover.start(other_hbm, other_ref)]
    blocks = [[mover.start(grad_hbm.at[:, pl.ds(pl.multiple_of(z * plane, plane), plane)], cots_ref.at[:tokens])]]
    for k in range(1, outer):
        blocks.append([])
        for hbm, side in ((cot_hbms[k - 1], core), (cot_hbms[outer + k - 2], 1 - core)):
            first = pl.multiple_of(k * tokens + side * half, half)
            blocks[k].append(mover.start(hbm.at[:half], cots_ref.at[pl.ds(first, half)]))
    mover.wait(*weights)
    span = outer * half
    for k in reversed(range(outer)):
        mover.wait(*blocks[k])
        here = slice(k * tokens, (k + 1) * tokens)
        block = cots_ref[here, :]
        low, high = block[:, :feats], block[:, feats:]
        own = jnp.where(x == 0, low, high)
        other = jnp.where(x == 0, high, low)
        total = dot(own, weight_ref[...]) + dot(other, other_ref[...])
        if k == 0:
            total_ref[...] = total
            mover.start(total_ref, total_out)
        else:
            sent_ref[k - 1] = total.astype(BF16)
            mover.start(sent_ref.at[k - 1], sent_outs[k - 1])
        cot_own_ref[here, :] = own
        cot_far_ref[here, :] = other

    size = cot_far_outs[0].shape[0]
    for i, out in enumerate(cot_far_outs):
        first = pl.multiple_of(core * span + i * size, size)
        mover.start(cot_far_ref.at[pl.ds(first, size)], out)
    mover.start(cot_own_ref, cot_own_out)


def decode_kernel(steps, mover, ins, outs, scratch):
    weight_hbm, other_hbm, *load_hbms = ins
    weight_ref, other_ref, dec_ref, rows_ref, by_row_ref, parts_ref = scratch
    _, _, z, x, _ = places()
    tokens = load_hbms[0].shape[0] - PAD
    outer, share = len(load_hbms), outs[0].shape[1]
    arrive = [mover.start(hbm, dec_ref.at[k]) for k, hbm in enumerate(load_hbms)]
    mover.wait(*arrive, mover.start(weight_hbm, weight_ref), mover.start(other_hbm, other_ref))
    for k in range(outer):
        rows_ref[k * steps : (k + 1) * steps, :] = dec_ref[k, tokens:, :].astype(F32)[:steps]
    every = rows_ref[...].astype(BF16)
    own, other = over_features(every, weight_ref[...]), over_features(every, other_ref[...])
    wide = jnp.concatenate([jnp.where(x == 0, own, other), jnp.where(x == 0, other, own)], axis=1)
    for k in range(outer):
        by_row_ref[k] = wide[k * steps : (k + 1) * steps]
    for q in range(parts_ref.shape[0]):
        for i in range(share):
            parts_ref[q, i] = by_row_ref[(z - (q * share + i)) % outer]
    mover.start(parts_ref, outs[0])


def own_kernel(mover, ins, outs, scratch):
    cot_hbm, attn_hbm, half_hbm, twin_hbm = ins
    cots_ref, attn_ref, others_ref = scratch
    _, core, _, _, _ = places()
    size = half_hbm.shape[0]
    arrive = [mover.start(cot_hbm, cots_ref), mover.start(attn_hbm, attn_ref)]
    halves = [
        mover.start(hbm, others_ref.at[pl.ds(pl.multiple_of((core ^ i) * size, size), size)])
        for i, hbm in enumerate((half_hbm, twin_hbm))
    ]
    mover.wait(*arrive)
    outs[0][...] = over_tokens(cots_ref[...], attn_ref[...])
    mover.wait(*halves)
    outs[1][...] = others_ref[...].T


def product_kernel(mover, ins, outs, scratch):
    own_ref, attn_ref, turned_ref = ins
    (out_ref,) = scratch
    pieces = 4
    step = out_ref.shape[0] // pieces
    for i in range(pieces):
        here = slice(i * step, (i + 1) * step)
        out_ref[here, :] = own_ref[here, :] + dot(turned_ref[here, :], attn_ref[...])
        mover.start(out_ref.at[here], outs[0].at[here])
    outs[1][...] = jnp.zeros(outs[1].shape, F32)


def sum_kernel(outer, share, mover, ins, outs, scratch):
    total_ref, *rest = ins
    part_hbms, piece_refs = rest[: outer - 1], rest[outer - 1 :]
    parts_ref, sum_ref = scratch
    _, _, z, _, _ = places()
    plane = piece_refs[0].shape[1]
    arrive = [mover.start(hbm, parts_ref.at[i]) for i, hbm in enumerate(part_hbms)]
    for j in range(share):
        mover.start(piece_refs[j], outs[0].at[0, :, pl.ds(pl.multiple_of((z % share ^ j) * plane, plane), plane)])
    mover.wait(*arrive)
    total = total_ref[...]
    for i in range(outer - 1):
        total = total + parts_ref[i].astype(F32)
    sum_ref[...] = total.astype(BF16)
    mover.start(sum_ref, outs[1])


def pack_kernel(early, skip, mover, ins, outs, scratch):
    low_hbm, high_hbm, own_hbm, *first_hbms = ins
    cots_ref, attn_out = outs
    (attn_ref,) = scratch
    tokens, size = own_hbm.shape[0], low_hbm.shape[0]
    mover.start(low_hbm, cots_ref.at[:size])
    mover.start(high_hbm, cots_ref.at[size:])
    parts = [(own_hbm, 0, tokens)] + [(hbm.at[skip:], (k + 1) * tokens, early) for k, hbm in enumerate(first_hbms)]
    arrive = [mover.start(source, attn_ref.at[at : at + rows]) for source, at, rows in parts]
    for copy, (_, at, rows) in zip(arrive, parts):
        mover.wait(copy)
        mover.start(attn_ref.at[at : at + rows], attn_out.at[at : at + rows])


def gate_kernel(count, early, *refs):
    refs, pack_out, sems = refs[count + 2 : -2 - count], refs[-2], refs[-1]
    rest = refs[0].shape[0] - PAD
    tokens = rest + early
    copies = []
    for k, ref in enumerate(refs[::-1]):
        target = pack_out.at[(k + 1) * tokens + early : (k + 2) * tokens]
        copies.append(pltpu.make_async_copy(ref.at[:rest], target, sems.at[k]))
    for copy in copies:
        copy.start()
    for copy in copies:
        copy.wait()


def shards(dec_query, new_keys, new_values, cache_keys, cache_values, lengths, out_weight, train_attn, grad_out):
    rows, steps, width = dec_query.shape
    assert rows == 1
    fsdp_size = lax.axis_size("fsdp")
    tp_size = lax.axis_size("tp")
    outer = fsdp_size // INNER
    share = outer // tp_size
    fsdp_index = lax.axis_index("fsdp")
    tp_index = lax.axis_index("tp")
    z, x = fsdp_index // INNER, fsdp_index % INNER
    tokens = grad_out.shape[0]
    feats, cols = out_weight.shape
    plane = feats * INNER
    slot = tp_index % 4
    heads = width // HD
    count = heads // tp_size * steps
    far = range(1, outer)
    others = range(1, tp_size)

    other_weight = flip(out_weight, "fsdp", 1, "weight_x")

    half = tokens // 2

    early = tokens // 4
    cot_rows = half * plane // cols
    if plane == cols:
        cuts = call(
            functools.partial(cut_kernel, outer, half, early),
            "cut",
            [grad_out, train_attn],
            [((half + early, cols), BF16)] * len(far),
            [((len(far), half + early, cols), BF16)],
            room=63,
        )
    else:
        first = tp_index % 2 * half
        cuts = [
            jnp.concatenate(
                [
                    lax.dynamic_slice(grad_out, (first, (z + k) % outer * plane), (half, plane)).reshape(cot_rows, cols),
                    train_attn[:early],
                ]
            )
            for k in far
        ]
    firsts = [turn(cuts[k - 1], k, f"first_z{k}") for k in far]
    got = firsts if plane == cols else [a[:cot_rows].reshape(half, plane) for a in firsts]

    sizes = [1 << b for b in range(tp_size.bit_length() - 1)]
    own, *chunks = call(
        functools.partial(attend_kernel, steps),
        "attend",
        [dec_query, cache_keys, cache_values, new_keys, new_values],
        [((2 * count + 8, 2 * HD), F32)]
        + [((size, count, 2 * HD), F32) for size in sizes],
        shaped(dec_query[0], cache_keys[0], cache_values[0], new_keys[0], new_values[0])
        + [((heads * steps, HD), F32), ((heads * steps, 2 * HD), F32)],
        scalars=lengths,
        room=63,
        fast=range(1 + len(sizes)),
    )
    own = pl.pallas_call(
        lambda in_ref, out_ref: out_ref.__setitem__(..., in_ref[...]),
        out_shape=jax.ShapeDtypeStruct(own.shape, own.dtype),
        in_specs=[pl.BlockSpec(memory_space=pltpu.VMEM)],
        out_specs=pl.BlockSpec(memory_space=pltpu.VMEM),
        compiler_params=pltpu.CompilerParams(vmem_limit_bytes=12 << 20),
        cost_estimate=pl.CostEstimate(flops=0, bytes_accessed=0, transcendentals=0),
        name="hold",
    )(own)
    parts, indices, held = [], [], []
    for size, chunk in reversed(list(zip(sizes, chunks))):
        if size > 1:
            came = [flip(a, "tp", size, f"softmax_tp{size}") for a in [chunk] + [a[size:] for a in held]]
            held = [a[:size] for a in held] + came
        else:
            parts += held + [flip(a, "tp", size, f"softmax_tp{size}") for a in [chunk] + held]
            indices += [0] * len(held) + [0] + [1] * len(held)
    last = pl.pallas_call(
        functools.partial(combine_kernel, steps, early, indices),
        out_shape=jax.ShapeDtypeStruct((tokens - early + PAD, cols), BF16),
        in_specs=[pl.BlockSpec(memory_space=pltpu.HBM)] + [pl.BlockSpec(memory_space=pltpu.VMEM)] * (len(parts) + 1),
        out_specs=pl.BlockSpec(memory_space=pltpu.HBM),
        scratch_shapes=[
            pltpu.VMEM((PAD, cols), F32),
            pltpu.VMEM((tokens - early + PAD, cols), BF16),
            pltpu.SemaphoreType.DMA((2,)),
        ],
        compiler_params=pltpu.CompilerParams(vmem_limit_bytes=12 << 20),
        cost_estimate=pl.CostEstimate(flops=0, bytes_accessed=0, transcendentals=0),
        name="combine",
    )(train_attn, own, *parts)

    lasts = [last] + [turn(last, k, f"last_z{k}") for k in far]

    got = kept(got, [last], "kept")
    twins = [flip(a, "tp", 1, "cot_core") for a in got]

    *sent, total, cot_own, cot_low, cot_high = call(
        functools.partial(middle_kernel, outer),
        "middle",
        [grad_out, out_weight, other_weight, *got, *twins],
        [((tokens, cols), BF16)] * len(far)
        + [((tokens, cols), F32), ((outer * tokens, feats), BF16)] + [((outer * half // 2, feats), BF16)] * 2,
        [
            ((outer * tokens, plane), BF16),
            ((feats, cols), BF16),
            ((feats, cols), BF16),
            ((len(far), tokens, cols), BF16),
            ((tokens, cols), F32),
            ((outer * tokens, feats), BF16),
            ((outer * tokens, feats), BF16),
        ],
        room=12,
    )
    cots_x = [flip(a, "fsdp", 1, "cot_x") for a in (cot_low, cot_high)]

    cots_x, pack = call(
        functools.partial(pack_kernel, early, cot_rows),
        "pack",
        [*cots_x, train_attn, *(got if plane == cols else firsts)],
        [((outer * half, feats), BF16), ((outer * tokens, cols), BF16)],
        [((outer * tokens, cols), BF16)],
        fast=[0],
    )

    results = pl.pallas_call(
        functools.partial(gate_kernel, len(sent), early),
        out_shape=[jax.ShapeDtypeStruct(a.shape, a.dtype) for a in [*sent, pack]],
        in_specs=[pl.BlockSpec(memory_space=pltpu.HBM)] * (len(sent) + 2 + len(far)),
        out_specs=[pl.BlockSpec(memory_space=pltpu.HBM)] * (len(sent) + 1),
        scratch_shapes=[
            pltpu.SemaphoreType.DMA((len(far),)),
        ],
        input_output_aliases={i: i for i in range(len(sent) + 1)},
        compiler_params=pltpu.CompilerParams(vmem_limit_bytes=12 << 20),
        cost_estimate=pl.CostEstimate(flops=0, bytes_accessed=0, transcendentals=0),
        name="gate",
    )(*sent, pack, cots_x, *lasts[:0:-1])
    sent, pack = results[:-1], results[-1]
    sums = [turn(sent[k - 1], outer - k, f"sum_z{k}") for k in far]
    pack_x = flip(pack, "fsdp", 1, "attn_x")
    twin_x = flip(cots_x, "tp", 1, "cot_x_core")

    (dec,) = call(
        functools.partial(decode_kernel, steps),
        "decode",
        [out_weight, other_weight, *lasts],
        [((tp_size, share, steps, plane), F32)],
        [
            ((feats, cols), BF16),
            ((feats, cols), BF16),
            ((outer, tokens - early + PAD, cols), BF16),
            ((outer * steps, cols), F32),
            ((outer, steps, plane), F32),
            ((tp_size, share, steps, plane), F32),
        ],
        waits=[pack],
        room=12,
    )
    with jax.named_scope("dec_tp"):
        dec = lax.all_to_all(dec, "tp", 0, 0, tiled=True).sum(axis=0).astype(BF16)
    pieces = []
    for j in range(share):
        perm = [
            ((a * INNER + b) * tp_size + q, ((q * share + (a % share ^ j)) * INNER + b) * tp_size + a // share)
            for a in range(outer)
            for b in range(INNER)
            for q in range(tp_size)
        ]
        with jax.named_scope("dec_place"):
            pieces.append(lax.ppermute(lax.dynamic_index_in_dim(dec, z % share ^ j, 0, False), ("fsdp", "tp"), perm))
    own_total, turned = call(
        own_kernel,
        "own",
        [cot_own, pack, cots_x, twin_x],
        [((feats, cols), F32), ((feats, outer * tokens), BF16)],
        [((outer * tokens, feats), BF16), ((outer * tokens, cols), BF16), ((outer * tokens, feats), BF16)],
        fast=[0, 1],
    )
    grad_weight, mark = call(
        product_kernel,
        "product",
        [own_total, pack_x, turned],
        [((feats, cols), F32), ((8, HD), F32)],
        [((feats, cols), F32)],
        near=range(3),
        fast=[1],
    )
    operands = [total, *sums[::-1], *pieces]
    dec_out, grad_attn = call(
        functools.partial(sum_kernel, outer, share),
        "sum",
        operands,
        [((rows, steps, share * plane), BF16), ((tokens, cols), BF16)],
        [((len(far), tokens, cols), BF16), ((tokens, cols), BF16)],
        waits=[mark],
        near=[0, *range(outer, len(operands))],
    )
    return dec_out, grad_attn, grad_weight


def solution(mesh):
    return jax.shard_map(
        shards,
        mesh=mesh,
        in_specs=(
            P("fsdp", None, None),
            P("fsdp", None, None),
            P("fsdp", None, None),
            P("fsdp", "tp", None),
            P("fsdp", "tp", None),
            P("fsdp"),
            P("fsdp", "tp"),
            P("fsdp", "tp"),
            P("fsdp", None),
        ),
        out_specs=(P("fsdp", None, "tp"), P("fsdp", "tp"), P("fsdp", "tp")),
        check_vma=False,
    )
```

```python
import functools

import jax
import jax.numpy as jnp
from jax import lax
from jax.experimental import pallas as pl
from jax.experimental.pallas import tpu as pltpu
from jax.sharding import PartitionSpec as P

KVH = 4
HD = 128
NEG_FILL = -1e30
INNER = 2
PAD = 8
BF16 = jnp.bfloat16
F32 = jnp.float32


def flip(a, axis, bits, name):
    size = lax.axis_size(axis)
    with jax.named_scope(name):
        return lax.ppermute(a, axis, [(i, i ^ bits) for i in range(size)])


def turn(a, steps, name):
    outer = lax.axis_size("fsdp") // INNER
    with jax.named_scope(name):
        return lax.ppermute(
            a, "fsdp", [(z * INNER + x, (z + steps) % outer * INNER + x) for z in range(outer) for x in range(INNER)]
        )


def dot(a, b):
    return jnp.dot(a, b, preferred_element_type=F32)


def over_features(a, b):
    return lax.dot_general(a, b, (((1,), (1,)), ((), ())), preferred_element_type=F32)


def over_tokens(a, b):
    return lax.dot_general(a, b, (((0,), (0,)), ((), ())), preferred_element_type=F32)


class Mover:
    def __init__(self, sems):
        self.sems, self.count, self.open = sems, 0, []

    def start(self, source, target):
        copy = pltpu.make_async_copy(source, target, self.sems.at[self.count])
        self.count += 1
        self.open.append(copy)
        copy.start()
        return copy

    def wait(self, *copies):
        for copy in copies:
            copy.wait()
            self.open = [other for other in self.open if other is not copy]

    def finish(self):
        self.wait(*list(self.open))


def places():
    fsdp_index, tp_index = lax.axis_index("fsdp"), lax.axis_index("tp")
    return tp_index, tp_index % 2, fsdp_index // INNER, fsdp_index % INNER, tp_index * KVH // lax.axis_size("tp")


def call(kernel, name, operands, out_shapes, scratch, waits=(), scalars=None, room=12, fast=(), near=()):
    copies = 4 * (len(operands) + len(out_shapes))
    scalars = [] if scalars is None else [scalars]

    def body(*refs):
        front, refs = refs[: len(scalars)], refs[len(scalars) :]
        ins, refs = refs[: len(operands)], refs[len(operands) + len(waits) :]
        outs, refs = refs[: len(out_shapes)], refs[len(out_shapes) :]
        mover = Mover(refs[-1])
        kernel(mover, *front, ins, outs, refs[:-1])
        mover.finish()

    results = pl.pallas_call(
        body,
        out_shape=[jax.ShapeDtypeStruct(shape, dtype) for shape, dtype in out_shapes],
        in_specs=[pl.BlockSpec(memory_space=pltpu.SMEM)] * len(scalars)
        + [pl.BlockSpec(memory_space=pltpu.VMEM if i in near else pltpu.HBM) for i in range(len(operands))]
        + [pl.BlockSpec(memory_space=pltpu.HBM)] * len(waits),
        out_specs=[
            pl.BlockSpec(memory_space=pltpu.VMEM if i in fast else pltpu.HBM) for i in range(len(out_shapes))
        ],
        scratch_shapes=[pltpu.VMEM(shape, dtype) for shape, dtype in scratch] + [pltpu.SemaphoreType.DMA((copies,))],
        compiler_params=pltpu.CompilerParams(vmem_limit_bytes=room << 20),
        cost_estimate=pl.CostEstimate(flops=0, bytes_accessed=0, transcendentals=0),
        name=name,
    )(*scalars, *operands, *waits)
    return list(results)


def kept(arrays, waits, name):
    count = len(arrays)
    results = pl.pallas_call(
        lambda *refs: None,
        out_shape=[jax.ShapeDtypeStruct(a.shape, a.dtype) for a in arrays],
        in_specs=[pl.BlockSpec(memory_space=pltpu.HBM)] * (count + len(waits)),
        out_specs=[pl.BlockSpec(memory_space=pltpu.HBM)] * count,
        input_output_aliases={i: i for i in range(count)},
        compiler_params=pltpu.CompilerParams(vmem_limit_bytes=12 << 20),
        cost_estimate=pl.CostEstimate(flops=0, bytes_accessed=0, transcendentals=0),
        name=name,
    )(*arrays, *waits)
    return list(results)


def shaped(*arrays):
    return [(a.shape, a.dtype) for a in arrays]


def attend_kernel(steps, mover, lengths_ref, ins, outs, scratch):
    query_hbm, keys_hbm, values_hbm, new_keys_hbm, new_values_hbm = ins
    query_ref, keys_ref, values_ref, new_keys_ref, new_values_ref, query_rows, out_rows = scratch
    tp_index, _, _, _, own_group = places()
    length = lengths_ref[0]
    own_ref, *chunk_refs = outs
    first = mover.start(query_hbm.at[0], query_ref)
    news = [mover.start(new_keys_hbm.at[0], new_keys_ref), mover.start(new_values_hbm.at[0], new_values_ref)]
    groups = [slice(g * HD, (g + 1) * HD) for g in range(KVH)]
    arrive = [
        (mover.start(keys_hbm.at[0, :, group], keys_ref.at[:, group]), mover.start(values_hbm.at[0, :, group], values_ref.at[:, group]))
        for group in groups
    ]
    width = query_ref.shape[1]
    cache_len = keys_ref.shape[0]
    rows = width // HD // KVH * steps
    mover.wait(first)
    for h in range(width // HD):
        query_rows[h * steps : (h + 1) * steps, :] = query_ref[:, h * HD : (h + 1) * HD].astype(F32)
    usable = lax.broadcasted_iota(jnp.int32, (rows, cache_len), 1) + tp_index * cache_len < length
    left = lax.broadcasted_iota(jnp.int32, (rows, HD), 1) < HD // 2
    for g in range(KVH):
        mover.wait(*arrive[g])
        query = query_rows[g * rows : (g + 1) * rows, :].astype(BF16)
        scores = over_features(query, keys_ref[:, g * HD : (g + 1) * HD]) * (1.0 / HD**0.5)
        maxima = jnp.max(jnp.where(usable, scores, NEG_FILL), axis=1, keepdims=True)
        terms = jnp.where(usable, jnp.exp(scores - maxima), 0.0)
        totals = jnp.sum(terms, axis=1, keepdims=True)
        upper = terms.astype(BF16)
        lower = (terms - upper.astype(F32)).astype(BF16)
        both = dot(jnp.concatenate([upper, lower], axis=0), values_ref[:, g * HD : (g + 1) * HD])
        out_rows[g * rows : (g + 1) * rows, :HD] = both[:rows] + both[rows:]
        out_rows[g * rows : (g + 1) * rows, HD:] = jnp.where(left, maxima, totals)
    count = chunk_refs[0].shape[1]
    for t in range(KVH * rows // count):
        for chunk_ref in chunk_refs:
            for k in range(chunk_ref.shape[0]):

                @pl.when(tp_index ^ (chunk_ref.shape[0] + k) == t)
                def _():
                    chunk_ref[k] = out_rows[t * count : (t + 1) * count, :]

        @pl.when(tp_index == t)
        def _():
            own_ref[:count, :] = out_rows[t * count : (t + 1) * count, :]
            own_ref[count : 2 * count, :HD] = query_rows[t * count : (t + 1) * count, :]

    mover.wait(*news)
    own_ref[count : 2 * count, HD:] = jnp.zeros((count, HD), F32)
    for at, ref in ((0, new_keys_ref), (HD, new_values_ref)):
        chosen = ref[:, :HD].astype(F32)
        for g in range(1, KVH):
            chosen = jnp.where(own_group == g, ref[:, groups[g]].astype(F32), chosen)
        own_ref[2 * count : 2 * count + steps, at : at + HD] = chosen


def combine_kernel(steps, sent, indices, attn_hbm, own_ref, *refs):
    *part_refs, out_hbm, rows_ref, load_ref, sems = refs
    rest = attn_hbm.shape[0] - sent
    arrive = pltpu.make_async_copy(attn_hbm.at[sent:], load_ref.at[:rest], sems.at[0])
    arrive.start()
    count = part_refs[0].shape[1]
    own = own_ref[...]
    rows_ref[...] = jnp.zeros_like(rows_ref)
    step = lax.broadcasted_iota(jnp.int32, (count, 1), 0) % steps
    query = own[count : 2 * count, :HD]
    keys, values = own[2 * count :, :HD], own[2 * count :, HD:]
    parts = [own[:count]] + [part_ref[i] for i, part_ref in zip(indices, part_refs)]
    scores = []
    for j in range(steps):
        score = jnp.sum(query * keys[j : j + 1], axis=-1, keepdims=True) * (1.0 / HD**0.5)
        scores.append(jnp.where(step >= j, score, NEG_FILL))
    maxima = [part[:, HD : HD + 1] for part in parts]
    highest = functools.reduce(jnp.maximum, scores + maxima)
    total = jnp.zeros((count, 1), F32)
    weighted = jnp.zeros((count, HD), F32)
    for part, own in zip(parts, maxima):
        scale = jnp.exp(own - highest)
        total = total + part[:, HD + HD // 2 : HD + HD // 2 + 1] * scale
        weighted = weighted + part[:, :HD] * scale
    for j in range(steps):
        term = jnp.where(step >= j, jnp.exp(scores[j] - highest), 0.0)
        total = total + term
        weighted = weighted + term * values[j : j + 1]
    attended = weighted / total
    for row in range(count):
        h, s = row // steps, row % steps
        rows_ref[s : s + 1, h * HD : (h + 1) * HD] = attended[row : row + 1]
    load_ref[rest:, :] = rows_ref[...].astype(BF16)
    arrive.wait()
    leave = pltpu.make_async_copy(load_ref, out_hbm, sems.at[1])
    leave.start()
    leave.wait()


def cut_kernel(outer, half, early, mover, ins, outs, scratch):
    grad_hbm, attn_hbm = ins
    plane = outs[0].shape[1]
    _, core, z, _, _ = places()
    rows = pl.ds(pl.multiple_of(core * half, half), half)
    for k in range(1, outer):
        columns = pl.ds(pl.multiple_of((z + k) % outer * plane, plane), plane)
        mover.start(grad_hbm.at[rows, columns], scratch[0].at[k - 1, :half])
        mover.start(attn_hbm.at[:early], scratch[0].at[k - 1, half:])
    arrive = list(mover.open)
    for k in range(1, outer):
        mover.wait(*arrive[2 * k - 2 : 2 * k])
        mover.start(scratch[0].at[k - 1], outs[k - 1])


def middle_kernel(outer, mover, ins, outs, scratch):
    grad_hbm, weight_hbm, other_hbm, *cot_hbms = ins
    sent_outs, (total_out, cot_own_out, *cot_far_outs) = outs[: outer - 1], outs[outer - 1 :]
    cots_ref, weight_ref, other_ref, sent_ref, total_ref, cot_own_ref, cot_far_ref = scratch
    _, core, z, x, _ = places()
    tokens = grad_hbm.shape[0]
    plane = cots_ref.shape[1]
    feats = weight_ref.shape[0]
    half = tokens // 2
    weights = [mover.start(weight_hbm, weight_ref), mover.start(other_hbm, other_ref)]
    blocks = [[mover.start(grad_hbm.at[:, pl.ds(pl.multiple_of(z * plane, plane), plane)], cots_ref.at[:tokens])]]
    for k in range(1, outer):
        blocks.append([])
        for hbm, side in ((cot_hbms[k - 1], core), (cot_hbms[outer + k - 2], 1 - core)):
            first = pl.multiple_of(k * tokens + side * half, half)
            blocks[k].append(mover.start(hbm.at[:half], cots_ref.at[pl.ds(first, half)]))
    mover.wait(*weights)
    span = outer * half
    for k in reversed(range(outer)):
        mover.wait(*blocks[k])
        here = slice(k * tokens, (k + 1) * tokens)
        block = cots_ref[here, :]
        low, high = block[:, :feats], block[:, feats:]
        own = jnp.where(x == 0, low, high)
        other = jnp.where(x == 0, high, low)
        total = dot(own, weight_ref[...]) + dot(other, other_ref[...])
        if k == 0:
            total_ref[...] = total
            mover.start(total_ref, total_out)
        else:
            sent_ref[k - 1] = total.astype(BF16)
            mover.start(sent_ref.at[k - 1], sent_outs[k - 1])
        cot_own_ref[here, :] = own
        cot_far_ref[here, :] = other

    size = cot_far_outs[0].shape[0]
    for i, out in enumerate(cot_far_outs):
        first = pl.multiple_of(core * span + i * size, size)
        mover.start(cot_far_ref.at[pl.ds(first, size)], out)
    mover.start(cot_own_ref, cot_own_out)


def decode_kernel(steps, mover, ins, outs, scratch):
    weight_hbm, other_hbm, *load_hbms = ins
    weight_ref, other_ref, dec_ref, rows_ref, by_row_ref, parts_ref = scratch
    _, _, z, x, _ = places()
    tokens = load_hbms[0].shape[0] - PAD
    outer, share = len(load_hbms), outs[0].shape[1]
    arrive = [mover.start(hbm, dec_ref.at[k]) for k, hbm in enumerate(load_hbms)]
    mover.wait(*arrive, mover.start(weight_hbm, weight_ref), mover.start(other_hbm, other_ref))
    for k in range(outer):
        rows_ref[k * steps : (k + 1) * steps, :] = dec_ref[k, tokens:, :].astype(F32)[:steps]
    every = rows_ref[...].astype(BF16)
    own, other = over_features(every, weight_ref[...]), over_features(every, other_ref[...])
    wide = jnp.concatenate([jnp.where(x == 0, own, other), jnp.where(x == 0, other, own)], axis=1)
    for k in range(outer):
        by_row_ref[k] = wide[k * steps : (k + 1) * steps]
    for q in range(parts_ref.shape[0]):
        for i in range(share):
            parts_ref[q, i] = by_row_ref[(z - (q * share + i)) % outer]
    mover.start(parts_ref, outs[0])


def own_kernel(mover, ins, outs, scratch):
    cot_hbm, attn_hbm, half_hbm, twin_hbm = ins
    cots_ref, attn_ref, others_ref = scratch
    _, core, _, _, _ = places()
    size = half_hbm.shape[0]
    arrive = [mover.start(cot_hbm, cots_ref), mover.start(attn_hbm, attn_ref)]
    halves = [
        mover.start(hbm, others_ref.at[pl.ds(pl.multiple_of((core ^ i) * size, size), size)])
        for i, hbm in enumerate((half_hbm, twin_hbm))
    ]
    mover.wait(*arrive)
    outs[0][...] = over_tokens(cots_ref[...], attn_ref[...])
    mover.wait(*halves)
    outs[1][...] = others_ref[...].T


def product_kernel(mover, ins, outs, scratch):
    own_ref, attn_ref, turned_ref = ins
    (out_ref,) = scratch
    pieces = 4
    step = out_ref.shape[0] // pieces
    for i in range(pieces):
        here = slice(i * step, (i + 1) * step)
        out_ref[here, :] = own_ref[here, :] + dot(turned_ref[here, :], attn_ref[...])
        mover.start(out_ref.at[here], outs[0].at[here])
    outs[1][...] = jnp.zeros(outs[1].shape, F32)


def sum_kernel(outer, share, mover, ins, outs, scratch):
    total_ref, *rest = ins
    part_refs, piece_refs = rest[: outer - 1], rest[outer - 1 :]
    (sum_ref,) = scratch
    _, _, z, _, _ = places()
    plane = piece_refs[0].shape[1]
    for j in range(share):
        mover.start(piece_refs[j], outs[0].at[0, :, pl.ds(pl.multiple_of((z % share ^ j) * plane, plane), plane)])
    pieces = 2
    step = sum_ref.shape[0] // pieces
    for p in range(pieces):
        here = slice(p * step, (p + 1) * step)
        total = total_ref[here, :]
        for part_ref in part_refs:
            total = total + part_ref[here, :].astype(F32)
        sum_ref[here, :] = total.astype(BF16)
        mover.start(sum_ref.at[here], outs[1].at[here])


def pack_kernel(early, skip, mover, ins, outs, scratch):
    low_hbm, high_hbm, own_hbm, *first_hbms = ins
    cots_ref, attn_out = outs
    tokens, size = own_hbm.shape[0], low_hbm.shape[0]
    mover.start(low_hbm, cots_ref.at[:size])
    mover.start(high_hbm, cots_ref.at[size:])
    mover.start(own_hbm, attn_out.at[:tokens])
    for k, hbm in enumerate(first_hbms):
        mover.start(hbm.at[skip:], attn_out.at[(k + 1) * tokens : (k + 1) * tokens + early])


def gate_kernel(count, early, *refs):
    refs, pack_out, sems = refs[count + 2 : -2 - count], refs[-2], refs[-1]
    rest = refs[0].shape[0] - PAD
    tokens = rest + early
    copies = []
    order = [*range(1, len(refs)), 0]
    for k, ref in zip(order[::-1], refs):
        target = pack_out.at[(k + 1) * tokens + early : (k + 2) * tokens]
        copies.append(pltpu.make_async_copy(ref.at[:rest], target, sems.at[k]))
    for copy in copies:
        copy.start()
    for copy in copies:
        copy.wait()


def shards(dec_query, new_keys, new_values, cache_keys, cache_values, lengths, out_weight, train_attn, grad_out):
    rows, steps, width = dec_query.shape
    assert rows == 1
    fsdp_size = lax.axis_size("fsdp")
    tp_size = lax.axis_size("tp")
    outer = fsdp_size // INNER
    share = outer // tp_size
    fsdp_index = lax.axis_index("fsdp")
    tp_index = lax.axis_index("tp")
    z, x = fsdp_index // INNER, fsdp_index % INNER
    tokens = grad_out.shape[0]
    feats, cols = out_weight.shape
    plane = feats * INNER
    slot = tp_index % 4
    heads = width // HD
    count = heads // tp_size * steps
    far = range(1, outer)
    others = range(1, tp_size)

    other_weight = flip(out_weight, "fsdp", 1, "weight_x")

    half = tokens // 2

    early = tokens // 4
    cot_rows = half * plane // cols
    if plane == cols:
        cuts = call(
            functools.partial(cut_kernel, outer, half, early),
            "cut",
            [grad_out, train_attn],
            [((half + early, cols), BF16)] * len(far),
            [((len(far), half + early, cols), BF16)],
            room=63,
        )
    else:
        first = tp_index % 2 * half
        cuts = [
            jnp.concatenate(
                [
                    lax.dynamic_slice(grad_out, (first, (z + k) % outer * plane), (half, plane)).reshape(cot_rows, cols),
                    train_attn[:early],
                ]
            )
            for k in far
        ]
    firsts = [turn(cuts[k - 1], k, f"first_z{k}") for k in far]
    got = firsts if plane == cols else [a[:cot_rows].reshape(half, plane) for a in firsts]

    sizes = [1 << b for b in range(tp_size.bit_length() - 1)]
    own, *chunks = call(
        functools.partial(attend_kernel, steps),
        "attend",
        [dec_query, cache_keys, cache_values, new_keys, new_values],
        [((2 * count + 8, 2 * HD), F32)]
        + [((size, count, 2 * HD), F32) for size in sizes],
        shaped(dec_query[0], cache_keys[0], cache_values[0], new_keys[0], new_values[0])
        + [((heads * steps, HD), F32), ((heads * steps, 2 * HD), F32)],
        scalars=lengths,
        room=63,
        fast=range(1 + len(sizes)),
    )
    own = pl.pallas_call(
        lambda in_ref, out_ref: out_ref.__setitem__(..., in_ref[...]),
        out_shape=jax.ShapeDtypeStruct(own.shape, own.dtype),
        in_specs=[pl.BlockSpec(memory_space=pltpu.VMEM)],
        out_specs=pl.BlockSpec(memory_space=pltpu.VMEM),
        compiler_params=pltpu.CompilerParams(vmem_limit_bytes=12 << 20),
        cost_estimate=pl.CostEstimate(flops=0, bytes_accessed=0, transcendentals=0),
        name="hold",
    )(own)
    parts, indices, held = [], [], []
    for size, chunk in reversed(list(zip(sizes, chunks))):
        if size > 1:
            came = [flip(a, "tp", size, f"softmax_tp{size}") for a in [chunk] + [a[size:] for a in held]]
            held = [a[:size] for a in held] + came
        else:
            parts += held + [flip(a, "tp", size, f"softmax_tp{size}") for a in [chunk] + held]
            indices += [0] * len(held) + [0] + [1] * len(held)
    last = pl.pallas_call(
        functools.partial(combine_kernel, steps, early, indices),
        out_shape=jax.ShapeDtypeStruct((tokens - early + PAD, cols), BF16),
        in_specs=[pl.BlockSpec(memory_space=pltpu.HBM)] + [pl.BlockSpec(memory_space=pltpu.VMEM)] * (len(parts) + 1),
        out_specs=pl.BlockSpec(memory_space=pltpu.HBM),
        scratch_shapes=[
            pltpu.VMEM((PAD, cols), F32),
            pltpu.VMEM((tokens - early + PAD, cols), BF16),
            pltpu.SemaphoreType.DMA((2,)),
        ],
        compiler_params=pltpu.CompilerParams(vmem_limit_bytes=12 << 20),
        cost_estimate=pl.CostEstimate(flops=0, bytes_accessed=0, transcendentals=0),
        name="combine",
    )(train_attn, own, *parts)

    lasts = [last] + [turn(last, k, f"last_z{k}") for k in far]

    got = kept(got, [last], "kept")
    twins = [flip(a, "tp", 1, "cot_core") for a in got]

    *sent, total, cot_own, cot_low, cot_high = call(
        functools.partial(middle_kernel, outer),
        "middle",
        [grad_out, out_weight, other_weight, *got, *twins],
        [((tokens, cols), BF16)] * len(far)
        + [((tokens, cols), F32), ((outer * tokens, feats), BF16)] + [((outer * half // 2, feats), BF16)] * 2,
        [
            ((outer * tokens, plane), BF16),
            ((feats, cols), BF16),
            ((feats, cols), BF16),
            ((len(far), tokens, cols), BF16),
            ((tokens, cols), F32),
            ((outer * tokens, feats), BF16),
            ((outer * tokens, feats), BF16),
        ],
        room=12,
    )
    cots_x = [flip(a, "fsdp", 1, "cot_x") for a in (cot_low, cot_high)]

    cots_x, pack = call(
        functools.partial(pack_kernel, early, cot_rows),
        "pack",
        [*cots_x, train_attn, *(got if plane == cols else firsts)],
        [((outer * half, feats), BF16), ((outer * tokens, cols), BF16)],
        [],
        fast=[0],
    )

    results = pl.pallas_call(
        functools.partial(gate_kernel, len(sent), early),
        out_shape=[jax.ShapeDtypeStruct(a.shape, a.dtype) for a in [*sent, pack]],
        in_specs=[pl.BlockSpec(memory_space=pltpu.HBM)] * (len(sent) + 2 + len(far)),
        out_specs=[pl.BlockSpec(memory_space=pltpu.HBM)] * (len(sent) + 1),
        scratch_shapes=[
            pltpu.SemaphoreType.DMA((len(far),)),
        ],
        input_output_aliases={i: i for i in range(len(sent) + 1)},
        compiler_params=pltpu.CompilerParams(vmem_limit_bytes=12 << 20),
        cost_estimate=pl.CostEstimate(flops=0, bytes_accessed=0, transcendentals=0),
        name="gate",
    )(*sent, pack, cots_x, *[lasts[k + 1] for k in [*range(1, len(far)), 0][::-1]])
    sent, pack = results[:-1], results[-1]
    sums = [turn(sent[k - 1], outer - k, f"sum_z{k}") for k in far]
    pack_x = flip(pack, "fsdp", 1, "attn_x")
    twin_x = flip(cots_x, "tp", 1, "cot_x_core")

    (dec,) = call(
        functools.partial(decode_kernel, steps),
        "decode",
        [out_weight, other_weight, *lasts],
        [((tp_size, share, steps, plane), F32)],
        [
            ((feats, cols), BF16),
            ((feats, cols), BF16),
            ((outer, tokens - early + PAD, cols), BF16),
            ((outer * steps, cols), F32),
            ((outer, steps, plane), F32),
            ((tp_size, share, steps, plane), F32),
        ],
        waits=[pack],
        room=12,
    )
    with jax.named_scope("dec_tp"):
        dec = lax.all_to_all(dec, "tp", 0, 0, tiled=True).sum(axis=0).astype(BF16)
    pieces = []
    for j in range(share):
        perm = [
            ((a * INNER + b) * tp_size + q, ((q * share + (a % share ^ j)) * INNER + b) * tp_size + a // share)
            for a in range(outer)
            for b in range(INNER)
            for q in range(tp_size)
        ]
        with jax.named_scope("dec_place"):
            pieces.append(lax.ppermute(lax.dynamic_index_in_dim(dec, z % share ^ j, 0, False), ("fsdp", "tp"), perm))
    own_total, turned = call(
        own_kernel,
        "own",
        [cot_own, pack, cots_x, twin_x],
        [((feats, cols), F32), ((feats, outer * tokens), BF16)],
        [((outer * tokens, feats), BF16), ((outer * tokens, cols), BF16), ((outer * tokens, feats), BF16)],
        fast=[0, 1],
    )
    grad_weight, mark = call(
        product_kernel,
        "product",
        [own_total, pack_x, turned],
        [((feats, cols), F32), ((8, HD), F32)],
        [((feats, cols), F32)],
        near=range(3),
        fast=[1],
    )
    operands = [total, *sums[::-1], *pieces]
    dec_out, grad_attn = call(
        functools.partial(sum_kernel, outer, share),
        "sum",
        operands,
        [((rows, steps, share * plane), BF16), ((tokens, cols), BF16)],
        [((tokens, cols), BF16)],
        waits=[mark],
        near=range(len(operands)),
    )
    return dec_out, grad_attn, grad_weight


def solution(mesh):
    return jax.shard_map(
        shards,
        mesh=mesh,
        in_specs=(
            P("fsdp", None, None),
            P("fsdp", None, None),
            P("fsdp", None, None),
            P("fsdp", "tp", None),
            P("fsdp", "tp", None),
            P("fsdp"),
            P("fsdp", "tp"),
            P("fsdp", "tp"),
            P("fsdp", None),
        ),
        out_specs=(P("fsdp", None, "tp"), P("fsdp", "tp"), P("fsdp", "tp")),
        check_vma=False,
    )
```
